128 devices in a mesh: seq: 4 (over z), tensor: 2 (over y_lo), fsdp: 16 (over x, y_hi, core).
Axes of the slice: x: 4, y: 4 (y_hi: 2, y_lo: 2; y = y_hi * 2 + y_lo), z: 4, core: 2. Of those that a mesh axis runs over, the one named last changes fastest.
Arguments:
- tokens: bfloat16 [16, 2048, 1536], P('fsdp', 'seq'), may hold values from -6 to 6
- output_gradient: bfloat16 [16, 2048, 1536], P('fsdp', 'seq'), may hold values from -6 to 6
- document_length_table: int32 [16, 4], P('fsdp'), may hold values from 1 to 1792, 2048 in all within a row
- sequence_adapter_index: int32 [16], P('fsdp'), may hold values from 0 to 7
- sequence_window_length: int32 [16], P('fsdp'), may hold values from 512 to 1024, as said below
- attention_norm_gain: float32 [1536], replicated, may hold values from 0.25 to 1.75
- feedforward_norm_gain: float32 [1536], replicated, may hold values from 0.25 to 1.75
- query_projection_weight: bfloat16 [1536, 1536], P('fsdp', 'tensor'), may hold values from -0.15625 to 0.15625
- key_projection_weight: bfloat16 [1536, 512], P('fsdp', 'tensor'), may hold values from -0.15625 to 0.15625
- value_projection_weight: bfloat16 [1536, 512], P('fsdp', 'tensor'), may hold values from -0.15625 to 0.15625
- output_projection_weight: bfloat16 [1536, 1536], P('fsdp', 'tensor'), may hold values from -2.5 to 2.5
- gate_projection_weight: bfloat16 [1536, 3840], P('fsdp', 'tensor'), may hold values from -0.15625 to 0.15625
- up_projection_weight: bfloat16 [1536, 3840], P('fsdp', 'tensor'), may hold values from -0.15625 to 0.15625
- down_projection_weight: bfloat16 [1536, 3840], P('fsdp', 'tensor'), may hold values from -0.75 to 0.75
- query_adapter_first: bfloat16 [8, 1536, 16], replicated, may hold values from -0.15625 to 0.15625
- query_adapter_second: bfloat16 [8, 16, 1536], P(None, None, 'tensor'), may hold values from -0.75 to 0.75
- key_adapter_first: bfloat16 [8, 1536, 16], replicated, may hold values from -0.15625 to 0.15625
- key_adapter_second: bfloat16 [8, 16, 512], P(None, None, 'tensor'), may hold values from -0.75 to 0.75
- value_adapter_first: bfloat16 [8, 1536, 16], replicated, may hold values from -0.15625 to 0.15625
- value_adapter_second: bfloat16 [8, 16, 512], P(None, None, 'tensor'), may hold values from -0.75 to 0.75
- output_adapter_first: bfloat16 [8, 16, 1536], P(None, None, 'tensor'), may hold values from -0.15625 to 0.15625
- output_adapter_second: bfloat16 [8, 16, 1536], replicated, may hold values from -3 to 3
- gate_adapter_first: bfloat16 [8, 1536, 16], replicated, may hold values from -0.15625 to 0.15625
- gate_adapter_second: bfloat16 [8, 16, 3840], P(None, None, 'tensor'), may hold values from -0.75 to 0.75
- up_adapter_first: bfloat16 [8, 1536, 16], replicated, may hold values from -0.15625 to 0.15625
- up_adapter_second: bfloat16 [8, 16, 3840], P(None, None, 'tensor'), may hold values from -0.75 to 0.75
- down_adapter_first: bfloat16 [8, 16, 3840], P(None, None, 'tensor'), may hold values from -0.09375 to 0.09375
- down_adapter_second: bfloat16 [8, 16, 1536], replicated, may hold values from -3 to 3
Outputs:
- output: bfloat16 [16, 2048, 1536], P('fsdp', 'seq')
- token_grad: bfloat16 [16, 2048, 1536], P('fsdp', 'seq')
- query_lora_in_grad: float32 [8, 1536, 16], replicated
- query_lora_out_grad: float32 [8, 16, 1536], replicated
- key_lora_in_grad: float32 [8, 1536, 16], replicated
- key_lora_out_grad: float32 [8, 16, 512], replicated
- value_lora_in_grad: float32 [8, 1536, 16], replicated
- value_lora_out_grad: float32 [8, 16, 512], replicated
- output_lora_in_grad: float32 [8, 16, 1536], replicated
- output_lora_out_grad: float32 [8, 16, 1536], replicated
- gate_lora_in_grad: float32 [8, 1536, 16], replicated
- gate_lora_out_grad: float32 [8, 16, 3840], replicated
- up_lora_in_grad: float32 [8, 1536, 16], replicated
- up_lora_out_grad: float32 [8, 16, 3840], replicated
- down_lora_in_grad: float32 [8, 16, 3840], replicated
- down_lora_out_grad: float32 [8, 16, 1536], replicated
The draws below stay inside these ranges and needn't reach their ends.
Inputs may be any that keep to these rules, and one draw needn't show every extreme that they name: `document_length_table`: each row lists the lengths of the 4 documents of one sequence in order, each 1 or more, summing to 2048; the longest is exactly 1792. `sequence_window_length`: one sequence has a window of exactly 1024.
All inputs are finite; a program needn't handle non-finite values.
Results may differ from the reference program's by a relative error of at most 0.023.
Values may be sent and summed in bfloat16 or wider, within the bound.
No kernel may reach another device: no remote copies, remote signals or barrier semaphores. Data moves between devices by JAX's collectives and lax.ppermute only.
A program may use at most 192 MiB of HBM per device.

```python
import math
import jax
import jax.numpy as jnp
import numpy as np
from jax import lax

MODEL_WIDTH = 1536
HEADS = 24
KV_HEADS = 8
HDIM = 64
HIDDEN_UNITS = 3840
ADAPTER_RANK = 16
ADAPTER_COUNT = 8
WINDOW = 1024
DOCS = 4
GROUP = 3
QUERY_FEATURES = 1536
KEY_FEATURES = 512
SEQS = 16
LENGTH = 2048
MOST = 1792


def draw_sequence_window_length(key, part):
    key = jax.random.fold_in(key, 7)
    first_key, second_key = jax.random.split(key)
    widths = jax.random.randint(first_key, (SEQS,), WINDOW // 2, WINDOW + 1, dtype=jnp.int32)
    chosen = jax.random.randint(second_key, (), 0, SEQS, dtype=jnp.int32)
    return jnp.where(jnp.arange(SEQS, dtype=jnp.int32) == chosen, WINDOW, widths).astype(jnp.int32)


def set_ends(array, key, smallest, largest):
    place = [jax.random.randint(jax.random.fold_in(key, axis), (), 0, length) for axis, length in enumerate(array.shape)]
    longest = array.shape.index(max(array.shape))
    neighbour = place[:longest] + [(place[longest] + 1) % array.shape[longest]] + place[longest + 1:]
    return array.at[tuple(place)].set(smallest).at[tuple(neighbour)].set(largest)


def steps_of(stream_key, dims, shards, least, top_value):
    def one(axis_at, blocks):
        heights = jax.random.uniform(jax.random.fold_in(jax.random.fold_in(stream_key, 6), axis_at), (blocks,), jnp.float32, least / len(shards), top_value / len(shards))
        return jnp.repeat(jnp.exp(heights), dims[axis_at] // blocks).reshape((-1,) + (1,) * (len(dims) - axis_at - 1))

    loudness = one(*shards[0])
    for cut in shards[1:]:
        loudness = loudness * one(*cut)
    return loudness


def length_profile(number_of, total, most, slope):
    loads = [(1 << 20) // math.isqrt(grade ** slope) + 1 for grade in range(2, number_of + 1)]
    surplus, counts = total - most - (number_of - 1), [1] * (number_of - 1)
    while surplus > 0:
        movable = [i for i in range(number_of - 1) if counts[i] < most]
        whole, left = sum([loads[i] for i in movable]), surplus
        for i in movable:
            extra = min(most - counts[i], max(1, left * loads[i] // whole), surplus)
            counts[i] = counts[i] + extra
            surplus = surplus - extra
    return np.array([most] + counts)


def uneven(own_key, number_of, total, bound, lean):
    if number_of == 2:
        one = jax.random.randint(own_key, (), max(1, total - bound), min(bound, total - 1) + 1)
        return jnp.stack([one, total - one])
    tallies = jnp.asarray(length_profile(number_of, total, bound, lean), jnp.int32)
    couples = (number_of - 1) // 2
    source_of, taker = tallies[1:1 + 2 * couples:2], tallies[2:2 + 2 * couples:2]
    room = jnp.minimum(source_of - 1, bound - taker)
    passed = jax.random.randint(jax.random.fold_in(own_key, 1), (couples,), 0, 1 << 20) % (room + 1)
    tallies = tallies.at[1:1 + 2 * couples:2].set(source_of - passed).at[2:2 + 2 * couples:2].set(taker + passed)
    return tallies[jax.random.permutation(jax.random.fold_in(own_key, 2), number_of)]


def normal_values(stream_key, dims, deviation, bound, cuts=(), kind=jnp.bfloat16):
    values = deviation * jax.random.normal(stream_key, dims, jnp.float32)
    if cuts:
        values = values * steps_of(stream_key, dims, cuts, -0.22, 0.18)
    return jnp.clip(values, -bound, bound).astype(kind)


def setup_inputs(seed: int = 0) -> dict:
    arg_keys = jax.random.split(jax.random.key(seed), 29)
    return {
        "tokens": normal_values(arg_keys[0], (SEQS, LENGTH, MODEL_WIDTH), 1.0, 6.0, ((0, 16), (1, 4))),
        "output_gradient": normal_values(arg_keys[1], (SEQS, LENGTH, MODEL_WIDTH), 1.0, 6.0, ((0, 16), (1, 4))),
        "document_length_table": jax.vmap(lambda own: uneven(own, DOCS, LENGTH, MOST, 1))(jax.random.split(arg_keys[2], SEQS)).reshape((SEQS, DOCS)).astype(jnp.int32),
        "sequence_adapter_index": set_ends(jax.random.randint(arg_keys[3], (SEQS,), 0, ADAPTER_COUNT), jax.random.fold_in(arg_keys[3], 1), 0, ADAPTER_COUNT - 1).astype(jnp.int32),
        "sequence_window_length": draw_sequence_window_length(jax.random.fold_in(arg_keys[28], 71), 0),
        "attention_norm_gain": jnp.clip(1.0 + 0.15 * jax.random.normal(arg_keys[5], (MODEL_WIDTH,), jnp.float32), 0.25, 1.75),
        "feedforward_norm_gain": jnp.clip(1.0 + 0.15 * jax.random.normal(arg_keys[6], (MODEL_WIDTH,), jnp.float32), 0.25, 1.75),
        "query_projection_weight": normal_values(arg_keys[7], (MODEL_WIDTH, QUERY_FEATURES), MODEL_WIDTH ** -0.5, 0.15625, ((0, 16), (1, 2))),
        "key_projection_weight": normal_values(arg_keys[8], (MODEL_WIDTH, KEY_FEATURES), MODEL_WIDTH ** -0.5, 0.15625, ((0, 16), (1, 2))),
        "value_projection_weight": normal_values(arg_keys[9], (MODEL_WIDTH, KEY_FEATURES), MODEL_WIDTH ** -0.5, 0.15625, ((0, 16), (1, 2))),
        "output_projection_weight": normal_values(arg_keys[10], (MODEL_WIDTH, QUERY_FEATURES), (max(1, QUERY_FEATURES // 256)) ** -0.5, 2.5, ((0, 16), (1, 2))),
        "gate_projection_weight": normal_values(arg_keys[11], (MODEL_WIDTH, HIDDEN_UNITS), MODEL_WIDTH ** -0.5, 0.15625, ((0, 16), (1, 2))),
        "up_projection_weight": normal_values(arg_keys[12], (MODEL_WIDTH, HIDDEN_UNITS), MODEL_WIDTH ** -0.5, 0.15625, ((0, 16), (1, 2))),
        "down_projection_weight": normal_values(arg_keys[13], (MODEL_WIDTH, HIDDEN_UNITS), (max(1, HIDDEN_UNITS // 64)) ** -0.5, 0.75, ((0, 16), (1, 2))),
        "query_adapter_first": normal_values(arg_keys[14], (ADAPTER_COUNT, MODEL_WIDTH, ADAPTER_RANK), MODEL_WIDTH ** -0.5, 0.15625),
        "query_adapter_second": normal_values(arg_keys[15], (ADAPTER_COUNT, ADAPTER_RANK, QUERY_FEATURES), (4 * ADAPTER_RANK) ** -0.5, 0.75, ((2, 2),)),
        "key_adapter_first": normal_values(arg_keys[16], (ADAPTER_COUNT, MODEL_WIDTH, ADAPTER_RANK), MODEL_WIDTH ** -0.5, 0.15625),
        "key_adapter_second": normal_values(arg_keys[17], (ADAPTER_COUNT, ADAPTER_RANK, KEY_FEATURES), (4 * ADAPTER_RANK) ** -0.5, 0.75, ((2, 2),)),
        "value_adapter_first": normal_values(arg_keys[18], (ADAPTER_COUNT, MODEL_WIDTH, ADAPTER_RANK), MODEL_WIDTH ** -0.5, 0.15625),
        "value_adapter_second": normal_values(arg_keys[19], (ADAPTER_COUNT, ADAPTER_RANK, KEY_FEATURES), (4 * ADAPTER_RANK) ** -0.5, 0.75, ((2, 2),)),
        "output_adapter_first": normal_values(arg_keys[20], (ADAPTER_COUNT, ADAPTER_RANK, QUERY_FEATURES), QUERY_FEATURES ** -0.5, 0.15625, ((2, 2),)),
        "output_adapter_second": normal_values(arg_keys[21], (ADAPTER_COUNT, ADAPTER_RANK, MODEL_WIDTH), (max(1, ADAPTER_RANK // 4)) ** -0.5, 3.0),
        "gate_adapter_first": normal_values(arg_keys[22], (ADAPTER_COUNT, MODEL_WIDTH, ADAPTER_RANK), MODEL_WIDTH ** -0.5, 0.15625),
        "gate_adapter_second": normal_values(arg_keys[23], (ADAPTER_COUNT, ADAPTER_RANK, HIDDEN_UNITS), (4 * ADAPTER_RANK) ** -0.5, 0.75, ((2, 2),)),
        "up_adapter_first": normal_values(arg_keys[24], (ADAPTER_COUNT, MODEL_WIDTH, ADAPTER_RANK), MODEL_WIDTH ** -0.5, 0.15625),
        "up_adapter_second": normal_values(arg_keys[25], (ADAPTER_COUNT, ADAPTER_RANK, HIDDEN_UNITS), (4 * ADAPTER_RANK) ** -0.5, 0.75, ((2, 2),)),
        "down_adapter_first": normal_values(arg_keys[26], (ADAPTER_COUNT, ADAPTER_RANK, HIDDEN_UNITS), HIDDEN_UNITS ** -0.5, 0.09375, ((2, 2),)),
        "down_adapter_second": normal_values(arg_keys[27], (ADAPTER_COUNT, ADAPTER_RANK, MODEL_WIDTH), (max(1, ADAPTER_RANK // 4)) ** -0.5, 3.0),
    }


@jax.custom_vjp
def low(v):
    return lax.optimization_barrier(v.astype(jnp.bfloat16)).astype(jnp.float32)

@jax.custom_vjp
def low_back(v):
    return v

def low_keep(v):
    return (low(v), None)

def low_pass(kept, grad):
    return (grad,)

def back_keep(v):
    return (v, None)

def back_low(kept, grad):
    return (low(grad),)
low.defvjp(low_keep, low_pass)
low_back.defvjp(back_keep, back_low)
highest = lax.Precision.HIGHEST
eps_norm = 1e-05
adapter_scale = 2.0
rope_base = 10000.0
residual_scale = 1.4 / 52.0 ** 0.5
masked_score = -1e+30

def precise_product(left_side, right_side):
    return jnp.dot(left_side, right_side, precision=highest, preferred_element_type=jnp.float32)

def rms_norm(values, gain_vector):
    return values * lax.rsqrt(lax.optimization_barrier(jnp.mean(values * values, axis=-1, keepdims=True)) + eps_norm) * gain_vector

def doc_tables(lengths_row, length_total):
    doc_ends = jnp.cumsum(lengths_row, dtype=jnp.int32)
    places = jnp.arange(length_total, dtype=jnp.int32)
    doc_ids = lax.optimization_barrier(jnp.sum((places[:, None] >= doc_ends[None, :]).astype(jnp.int32), axis=1, dtype=jnp.int32))
    starts = doc_ends - lengths_row
    member = doc_ids[:, None] == jnp.arange(lengths_row.shape[0], dtype=jnp.int32)[None, :]
    begins = lax.optimization_barrier(jnp.sum(jnp.where(member, starts[None, :], 0), axis=1, dtype=jnp.int32))
    return (doc_ids, places - begins)

def rotary_tables(positions):
    frequency = rope_base ** (-(jnp.arange(HDIM // 2, dtype=jnp.float32) * (2.0 / HDIM)))
    angles = positions.astype(jnp.float32)[:, None] * frequency[None, :]
    return (jnp.cos(angles), jnp.sin(angles))

def rotary(values, cosine_table, sine_table):
    half_dim = values.shape[-1] // 2
    first_half = values[..., :half_dim]
    second_half = values[..., half_dim:]
    return jnp.concatenate([first_half * cosine_table - second_half * sine_table, second_half * cosine_table + first_half * sine_table], axis=-1)

def adapter_pick(adapter_selector, factor_stack):
    return jnp.einsum('a,aij->ij', adapter_selector, factor_stack, precision=highest)

def apply_projection(input_tokens, base_weight, adapter_first, adapter_second):
    inner_product = precise_product(input_tokens, adapter_first)
    return precise_product(input_tokens, base_weight) + adapter_scale * precise_product(inner_product, adapter_second)

def apply_row_projection(input_tokens, base_weight, adapter_first, adapter_second):
    inner_product = precise_product(input_tokens, adapter_first.T)
    return precise_product(input_tokens, base_weight.T) + adapter_scale * precise_product(inner_product, adapter_second)

def attention(queries, keys_all, values_all, doc_ids, window):
    query_block = min(512, LENGTH)
    places = jnp.arange(LENGTH, dtype=jnp.int32)

    def attend_block(start):
        query_rows = lax.dynamic_slice_in_dim(queries, start, query_block, 0)
        row_places = start + jnp.arange(query_block, dtype=jnp.int32)
        row_docs = lax.dynamic_slice_in_dim(doc_ids, start, query_block, 0)
        scores = jnp.einsum('ikgd,jkd->kgij', query_rows, keys_all, precision=highest) * HDIM ** (-0.5)
        scores = low_back(scores)
        allowed = (row_docs[:, None] == doc_ids[None, :]) & (places[None, :] <= row_places[:, None]) & (row_places[:, None] - places[None, :] < window)
        scores = jnp.where(allowed, scores, masked_score)
        probabilities = low(jax.nn.softmax(scores, axis=-1))
        return jnp.einsum('kgij,jkd->ikgd', probabilities, values_all, precision=highest)
    block_starts = jnp.arange(LENGTH // query_block, dtype=jnp.int32) * query_block
    attended = lax.map(jax.checkpoint(attend_block), block_starts)
    return attended.reshape(LENGTH, HEADS * HDIM)

def layer_forward(tokens_f, adapter_factor_list, frozen, adapter_selector, doc_ids, cosine_table, sine_table, window):
    attention_norm_gain, feedforward_norm_gain, query_projection_weight, key_projection_weight, value_projection_weight, output_projection_weight, gate_projection_weight, up_projection_weight, down_projection_weight = frozen
    picked = [adapter_pick(adapter_selector, adapter_factor) for adapter_factor in adapter_factor_list]
    normed_attn = low(rms_norm(tokens_f, attention_norm_gain))
    query_raw = apply_projection(normed_attn, query_projection_weight, picked[0], picked[1])
    key_raw = apply_projection(normed_attn, key_projection_weight, picked[2], picked[3])
    value_raw = apply_projection(normed_attn, value_projection_weight, picked[4], picked[5])
    queries = low(rotary(low_back(query_raw).reshape(LENGTH, KV_HEADS, GROUP, HDIM), cosine_table[:, None, None, :], sine_table[:, None, None, :]))
    keys_all = low(rotary(low_back(key_raw).reshape(LENGTH, KV_HEADS, HDIM), cosine_table[:, None, :], sine_table[:, None, :]))
    values_all = low(low_back(value_raw)).reshape(LENGTH, KV_HEADS, HDIM)
    attended = low(low_back(attention(queries, keys_all, values_all, doc_ids, window)))
    attn_branch = low_back(apply_row_projection(attended, output_projection_weight, picked[6], picked[7]))
    residual = tokens_f + residual_scale * attn_branch
    normed_ffn = low(rms_norm(residual, feedforward_norm_gain))
    gate_value = low_back(apply_projection(normed_ffn, gate_projection_weight, picked[8], picked[9]))
    up_value = low_back(apply_projection(normed_ffn, up_projection_weight, picked[10], picked[11]))
    hidden = low(jax.nn.silu(gate_value) * up_value)
    ffn_branch = low_back(apply_row_projection(hidden, down_projection_weight, picked[12], picked[13]))
    return residual + residual_scale * ffn_branch

def reference(tokens, output_gradient, document_length_table, sequence_adapter_index, sequence_window_length, attention_norm_gain, feedforward_norm_gain, query_projection_weight, key_projection_weight, value_projection_weight, output_projection_weight, gate_projection_weight, up_projection_weight, down_projection_weight, query_adapter_first, query_adapter_second, key_adapter_first, key_adapter_second, value_adapter_first, value_adapter_second, output_adapter_first, output_adapter_second, gate_adapter_first, gate_adapter_second, up_adapter_first, up_adapter_second, down_adapter_first, down_adapter_second):
    frozen = (attention_norm_gain, feedforward_norm_gain) + tuple((weight_arg.astype(jnp.float32) for weight_arg in (query_projection_weight, key_projection_weight, value_projection_weight, output_projection_weight, gate_projection_weight, up_projection_weight, down_projection_weight)))
    adapter_factor_list = tuple((adapter_factor.astype(jnp.float32) for adapter_factor in (query_adapter_first, query_adapter_second, key_adapter_first, key_adapter_second, value_adapter_first, value_adapter_second, output_adapter_first, output_adapter_second, gate_adapter_first, gate_adapter_second, up_adapter_first, up_adapter_second, down_adapter_first, down_adapter_second)))
    initial = tuple((jnp.zeros(adapter_factor.shape, jnp.float32) for adapter_factor in adapter_factor_list))

    def per_sequence(totals, input_tokens):
        seq_tokens, seq_grad, lengths_row, index_value, window = input_tokens
        adapter_selector = (jnp.arange(ADAPTER_COUNT, dtype=jnp.int32) == index_value).astype(jnp.float32)
        doc_ids, doc_pos = doc_tables(lengths_row, LENGTH)
        cosine_table, sine_table = rotary_tables(doc_pos)

        def forward(tokens_f, factor_set):
            return layer_forward(tokens_f, factor_set, frozen, adapter_selector, doc_ids, cosine_table, sine_table, window)
        result, pullback = jax.vjp(forward, seq_tokens.astype(jnp.float32), adapter_factor_list)
        input_gradient, factor_grads = pullback(seq_grad.astype(jnp.float32))
        totals = tuple((total_part + new_part for total_part, new_part in zip(totals, factor_grads)))
        return (totals, (result.astype(jnp.bfloat16), input_gradient.astype(jnp.bfloat16)))
    totals, (output, token_grad) = lax.scan(per_sequence, initial, (tokens, output_gradient, document_length_table, sequence_adapter_index, sequence_window_length))
    return (output, token_grad, totals[0], totals[1], totals[2], totals[3], totals[4], totals[5], totals[6], totals[7], totals[8], totals[9], totals[10], totals[11], totals[12], totals[13])
```

```python
import jax
import jax.numpy as jnp
from jax import lax
from jax.experimental import pallas as pl
from jax.experimental.pallas import tpu as pltpu
from jax.sharding import Mesh
from jax.sharding import PartitionSpec as P

F32 = jnp.float32
BF16 = jnp.bfloat16
EPS = 1e-05
ROPE_BASE = 10000.0
RS = 1.4 / 52.0**0.5
MASKED = -1e30
TOK = 512
D = 1536
HQ = 768
HK = 256
HDIM = 64
SPAN = 1280
RT = 256
HALO = 1024
CHUNKS = (512, 512, 512, 384)
CHUNK_PATH = ("yx", "xy", "yx", "xy")
VMEM_LIMIT = 56 * 1024 * 1024


def nn(a, b):
    return lax.dot_general(a, b, (((1,), (0,)), ((), ())), preferred_element_type=F32)


def nt(a, b):
    return lax.dot_general(a, b, (((1,), (1,)), ((), ())), preferred_element_type=F32)


def tn(a, b):
    return lax.dot_general(a, b, (((0,), (0,)), ((), ())), preferred_element_type=F32)


VM = pl.BlockSpec(memory_space=pltpu.VMEM)
SM = pl.BlockSpec(memory_space=pltpu.SMEM)
HB = pl.BlockSpec(memory_space=pl.ANY)


def params():
    return pltpu.CompilerParams(vmem_limit_bytes=VMEM_LIMIT)


def sds(shape, dtype):
    return jax.ShapeDtypeStruct(shape, dtype)


def piece_copies(offs, refs, dst, sems):
    copies = []
    for ref in refs:
        for k in range(ref.shape[0]):
            row = pl.multiple_of(offs[len(copies)] * 96, 96)
            copies.append(
                pltpu.make_async_copy(ref.at[k], dst.at[pl.ds(row, 96)], sems.at[len(copies)])
            )
    return copies


def half_swap(v, sign=1):
    lane = lax.broadcasted_iota(jnp.int32, v.shape, 1)
    width = v.shape[1]
    from_low = pltpu.roll(v, 32, 1)
    from_high = pltpu.roll(v, width - 32, 1)
    return jnp.where((lane % 64) < 32, from_high, from_low)


def qkv_kernel(
    offs_a, offs_b, tok, gain, a1, b2, cos, sin, q0, q1, q2, q3, q4, k0, k1, k2, k3, k4,
    normed_o, q_o, kv_o, mid_o, wq, wkv, sem_a, sem_b,
):
    cq = piece_copies(offs_a, (q0, q1, q2, q3, q4), wq, sem_a)
    ck = piece_copies(offs_b, (k0, k1, k2, k3, k4), wkv, sem_b)
    for c in cq + ck:
        c.start()
    for r in range(4):
        rows = pl.ds(r * 128, 128)
        x = tok[rows, :].astype(F32)
        inv = lax.rsqrt(jnp.mean(x * x, axis=-1, keepdims=True) + EPS)
        normed_o[rows, :] = (x * inv * gain[...]).astype(BF16)
    normed = normed_o[...]
    mid = nt(normed, a1[...]).astype(BF16)
    mid_o[...] = mid
    for c in cq + ck:
        c.wait()
    cw = jnp.concatenate([cos[...], cos[...]], axis=1)
    sw = jnp.concatenate([sin[...], sin[...]], axis=1)
    for n in range(5):
        if n < 3:
            w = wq[:, n * 256 : (n + 1) * 256]
        else:
            w = wkv[:, (n - 3) * 256 : (n - 2) * 256]
        acc = nn(normed, w) + nn(mid, b2[:, n * 256 : (n + 1) * 256])
        if n < 4:
            acc = acc * cw + half_swap(acc) * sw
        if n < 3:
            q_o[:, n * 256 : (n + 1) * 256] = (acc.astype(BF16).astype(F32) * 0.125).astype(BF16)
        else:
            kv_o[n - 3] = acc.astype(BF16)


def qkv_call(offs_a, offs_b, tok, gain, a1, b2, cos, sin, wq, wkv):
    return pl.pallas_call(
        qkv_kernel,
        out_shape=(
            sds((TOK, D), BF16),
            sds((TOK, HQ), BF16),
            sds((2, TOK, HK), BF16),
            sds((TOK, 128), BF16),
        ),
        in_specs=[SM, SM] + [VM] * 6 + [HB] * 10,
        out_specs=(VM,) * 4,
        scratch_shapes=[
            pltpu.VMEM((D, HQ), BF16),
            pltpu.VMEM((D, 2 * HK), BF16),
            pltpu.SemaphoreType.DMA((16,)),
            pltpu.SemaphoreType.DMA((16,)),
        ],
        compiler_params=params(),
        cost_estimate=pl.CostEstimate(
            flops=2 * TOK * D * 1280, bytes_accessed=9_000_000, transcendentals=0
        ),
        name="norm_qkv",
    )(offs_a, offs_b, tok, gain, a1, b2, cos, sin, *wq, *wkv)


HEADS_OF_PAIR = ((0, 0, 0), (0, 1, 0), (1, 0, 0), (1, 1, 1), (2, 0, 1), (2, 1, 1))


def bias_of(lo, r):
    key = lax.broadcasted_iota(jnp.int32, (SPAN, RT), 0) + r * RT
    row = lax.broadcasted_iota(jnp.int32, (SPAN, RT), 1) + r * RT + HALO
    return jnp.where((key >= lo) & (key <= row), 0.0, MASKED)


def variants(dst, src):
    lane = lax.broadcasted_iota(jnp.int32, src.shape, 1)
    srcf = src.astype(F32)
    rolled = pltpu.roll(srcf, 64, 1)
    low = lane < 64
    dst[0] = jnp.where(low, srcf, 0.0).astype(BF16)
    dst[1] = jnp.where(low, 0.0, rolled).astype(BF16)
    dst[2] = jnp.where(low, rolled, 0.0).astype(BF16)
    dst[3] = jnp.where(low, 0.0, srcf).astype(BF16)


def attend_kernel(q, lo, kv2, kv1, kv0, out, lse, kvar, vt, bias, ot):
    r = pl.program_id(1)

    @pl.when(r == 0)
    def _():
        kcat = jnp.concatenate([kv2[0], kv1[0], kv0[0]], axis=0)
        variants(kvar, kcat)
        vcat = jnp.concatenate([kv2[1], kv1[1], kv0[1]], axis=0)
        vt[...] = vcat.astype(F32).T.astype(BF16)

    bias[...] = bias_of(lo[...], r)
    keys = pl.ds(pl.multiple_of(r * RT, RT), SPAN)
    for i, (tile, half, kv) in enumerate(HEADS_OF_PAIR):
        qt = q[:, tile * 128 : (tile + 1) * 128]
        s = nt(kvar[2 * kv + half, keys, :], qt) + bias[...]
        m = jnp.max(s, axis=0, keepdims=True)
        e = jnp.exp(s - m)
        total = jnp.sum(e, axis=0, keepdims=True)
        o = nn(vt[kv * 64 : (kv + 1) * 64, keys], e.astype(BF16))
        ot[i * 64 : (i + 1) * 64, :] = o * (1.0 / total)
        lse[i : i + 1, :] = m + jnp.log(total)
    out[...] = ot[...].T.astype(BF16)


def attend_call(q, lo, kv2, kv1, kv0):
    kvspec = pl.BlockSpec((2, TOK, 128), lambda p, r: (0, 0, p))
    return pl.pallas_call(
        attend_kernel,
        grid=(2, 2),
        out_shape=(sds((TOK, HQ), BF16), sds((16, TOK), F32)),
        in_specs=[
            pl.BlockSpec((RT, 384), lambda p, r: (r, p)),
            pl.BlockSpec((1, RT), lambda p, r: (0, r)),
            kvspec,
            kvspec,
            kvspec,
        ],
        out_specs=(
            pl.BlockSpec((RT, 384), lambda p, r: (r, p)),
            pl.BlockSpec((8, RT), lambda p, r: (p, r)),
        ),
        scratch_shapes=[
            pltpu.VMEM((4, HALO + TOK, 128), BF16),
            pltpu.VMEM((128, HALO + TOK), BF16),
            pltpu.VMEM((SPAN, RT), F32),
            pltpu.VMEM((384, RT), F32),
        ],
        compiler_params=params(),
        cost_estimate=pl.CostEstimate(
            flops=4 * 12 * 2 * RT * SPAN * 128, bytes_accessed=4_000_000, transcendentals=0
        ),
        name="attend",
    )(q, lo, kv2, kv1, kv0)


def attend_back_kernel(
    q, do, lse, delta, lo, kv2, kv1, kv0, dq, d2, d1, d0,
    kvar, vvar, kt, bias, dqt, dk_same, dk_cross, dv_same, dv_cross,
):
    r = pl.program_id(1)

    @pl.when(r == 0)
    def _():
        kcat = jnp.concatenate([kv2[0], kv1[0], kv0[0]], axis=0)
        variants(kvar, kcat)
        kt[...] = kcat.astype(F32).T.astype(BF16)
        vcat = jnp.concatenate([kv2[1], kv1[1], kv0[1]], axis=0)
        variants(vvar, vcat)
        for ref in (dk_same, dk_cross, dv_same, dv_cross):
            ref[...] = jnp.zeros_like(ref)

    bias[...] = bias_of(lo[...], r)
    keys = pl.ds(pl.multiple_of(r * RT, RT), SPAN)
    lane = lax.broadcasted_iota(jnp.int32, (RT, 128), 1)
    for i, (tile, half, kv) in enumerate(HEADS_OF_PAIR):
        cols = slice(tile * 128, (tile + 1) * 128)
        qt = q[:, cols]
        dt = do[:, cols]
        keep = (lane < 64) if half == 0 else (lane >= 64)
        qm = jnp.where(keep, qt, jnp.zeros_like(qt))
        dm = jnp.where(keep, dt, jnp.zeros_like(dt))
        s = nt(kvar[2 * kv + half, keys, :], qt) + bias[...]
        p = jnp.exp(s - lse[i : i + 1, :])
        dp = nt(vvar[2 * kv + half, keys, :], dt)
        ds = (p * (dp - delta[i : i + 1, :])).astype(BF16)
        dk_acc, dv_acc = (dk_same, dv_same) if half == kv else (dk_cross, dv_cross)
        dv_acc[keys, :] += nn(p.astype(BF16), dm)
        dk_acc[keys, :] += nn(ds, qm)
        dqt[i * 64 : (i + 1) * 64, :] = nn(kt[kv * 64 : (kv + 1) * 64, keys], ds)
    dq[...] = dqt[...].T * 0.125

    @pl.when(r == 1)
    def _():
        dk = dk_same[...] + pltpu.roll(dk_cross[...], 64, 1)
        dv = dv_same[...] + pltpu.roll(dv_cross[...], 64, 1)
        d2[0] = dk[0:512].astype(BF16)
        d2[1] = dv[0:512].astype(BF16)
        d1[0] = dk[512:1024].astype(BF16)
        d1[1] = dv[512:1024].astype(BF16)
        d0[0] = dk[1024:1536]
        d0[1] = dv[1024:1536]


def attend_back_call(q, do, lse, delta, lo, kv2, kv1, kv0):
    kvspec = pl.BlockSpec((2, TOK, 128), lambda p, r: (0, 0, p))
    rowspec = pl.BlockSpec((RT, 384), lambda p, r: (r, p))
    statspec = pl.BlockSpec((8, RT), lambda p, r: (p, r))
    acc = pltpu.VMEM((HALO + TOK, 128), F32)
    return pl.pallas_call(
        attend_back_kernel,
        grid=(2, 2),
        out_shape=(
            sds((TOK, HQ), F32),
            sds((2, TOK, HK), BF16),
            sds((2, TOK, HK), BF16),
            sds((2, TOK, HK), F32),
        ),
        in_specs=[
            rowspec,
            rowspec,
            statspec,
            statspec,
            pl.BlockSpec((1, RT), lambda p, r: (0, r)),
            kvspec,
            kvspec,
            kvspec,
        ],
        out_specs=(rowspec, kvspec, kvspec, kvspec),
        scratch_shapes=[
            pltpu.VMEM((4, HALO + TOK, 128), BF16),
            pltpu.VMEM((4, HALO + TOK, 128), BF16),
            pltpu.VMEM((128, HALO + TOK), BF16),
            pltpu.VMEM((SPAN, RT), F32),
            pltpu.VMEM((384, RT), F32),
            acc,
            acc,
            acc,
            acc,
        ],
        compiler_params=params(),
        cost_estimate=pl.CostEstimate(
            flops=10 * 12 * 2 * RT * SPAN * 128, bytes_accessed=6_000_000, transcendentals=0
        ),
        name="attend_back",
    )(q, do, lse, delta, lo, kv2, kv1, kv0)


def out_proj_kernel(offs, att, oi, oo2, w0, w1, w2, w3, w4, part, mid_o, w, sem):
    cs = piece_copies(offs, (w0, w1, w2, w3, w4), w, sem)
    for c in cs:
        c.start()
    a = att[...]
    mid = nt(a, oi[...]).astype(BF16)
    mid_o[...] = mid
    for c in cs:
        c.wait()
    for n in range(6):
        cols = slice(n * 256, (n + 1) * 256)
        part[:, cols] = (nt(a, w[cols, :]) + nn(mid, oo2[:, cols])).astype(BF16)


def out_proj_call(offs, att, oi, oo2, wo):
    return pl.pallas_call(
        out_proj_kernel,
        out_shape=(sds((TOK, D), BF16), sds((TOK, 128), BF16)),
        in_specs=[SM] + [VM] * 3 + [HB] * 5,
        out_specs=(VM, VM),
        scratch_shapes=[pltpu.VMEM((D, HQ), BF16), pltpu.SemaphoreType.DMA((16,))],
        compiler_params=params(),
        cost_estimate=pl.CostEstimate(
            flops=2 * TOK * D * HQ, bytes_accessed=5_000_000, transcendentals=0
        ),
        name="out_proj",
    )(offs, att, oi, oo2, *wo)


def ffn_in_kernel(tok, own, other, gain, a_gu, resid_o, nf_o, mid_o):
    for r in range(4):
        rows = pl.ds(r * 128, 128)
        branch = own[rows, :].astype(F32) + other[rows, :].astype(F32)
        x = tok[rows, :].astype(F32) + RS * branch
        resid_o[rows, :] = x
        inv = lax.rsqrt(jnp.mean(x * x, axis=-1, keepdims=True) + EPS)
        nf_o[rows, :] = (x * inv * gain[...]).astype(BF16)
    mid_o[...] = nt(nf_o[...], a_gu[...]).astype(BF16)


def ffn_in_call(tok, own, other, gain, a_gu):
    return pl.pallas_call(
        ffn_in_kernel,
        out_shape=(sds((TOK, D), F32), sds((TOK, D), BF16), sds((TOK, 128), BF16)),
        in_specs=[VM] * 5,
        out_specs=(VM,) * 3,
        compiler_params=params(),
        cost_estimate=pl.CostEstimate(
            flops=2 * TOK * D * 256, bytes_accessed=10_000_000, transcendentals=0
        ),
        name="ffn_norm",
    )(tok, own, other, gain, a_gu)


def cot_kernel(og, do2, fg_o, mid_o):
    fg_o[...] = (RS * og[...].astype(F32)).astype(BF16)
    mid_o[...] = nt(fg_o[...], do2[...]).astype(BF16)


def cot_call(og, do2):
    return pl.pallas_call(
        cot_kernel,
        out_shape=(sds((TOK, D), BF16), sds((TOK, 128), BF16)),
        in_specs=[VM] * 2,
        out_specs=(VM,) * 2,
        compiler_params=params(),
        cost_estimate=pl.CostEstimate(
            flops=2 * TOK * D * 256, bytes_accessed=4_000_000, transcendentals=0
        ),
        name="branch_cotangent",
    )(og, do2)


def ffn_kernel(width, first, last, *refs):
    offs, nf, fg, mid_gu, mid_dg, bg, bu, di = refs[:8]
    refs = refs[8:]
    w0, w1, w2, w3, w4 = refs[:5]
    refs = refs[5:]
    if last:
        a_gu, do2 = refs[:2]
        refs = refs[2:]
    if not first:
        accf_i, accn_i, midd_i, midg_i = refs[:4]
        refs = refs[4:]
    if last:
        part_f, part_n, gu_in, d_out, gout, uout, din = refs[:7]
        refs = refs[7:]
    else:
        accf_o, accn_o, midd_o, midg_o, gout, uout, din = refs[:7]
        refs = refs[7:]
    w, accf, accn, midd, midg, sem, sem_acc = refs
    cs = piece_copies(offs, (w0, w1, w2, w3, w4), w, sem)
    for c in cs:
        c.start()
    if not first:
        ca = [
            pltpu.make_async_copy(accf_i, accf, sem_acc.at[0]),
            pltpu.make_async_copy(accn_i, accn, sem_acc.at[1]),
        ]
        for c in ca:
            c.start()
        midd[...] = midd_i[...]
        midg[...] = midg_i[...]
    else:
        midd[...] = jnp.zeros_like(midd)
        midg[...] = jnp.zeros_like(midg)
    mid_t = mid_gu[...].astype(F32).T.astype(BF16)
    dg_t = mid_dg[...].astype(F32).T.astype(BF16)
    for c in cs:
        c.wait()
    if not first:
        for c in ca:
            c.wait()
    start = 0
    while start < width:
        n = min(256, width - start)
        blk = slice(start, start + n)
        wg = w[:, start : start + n]
        wu = w[:, width + start : width + start + n]
        wd = w[:, 2 * width + start : 2 * width + start + n]
        g = nn(nf[...], wg) + nn(mid_gu[...], bg[:, blk])
        u = nn(nf[...], wu) + nn(mid_gu[...], bu[:, blk])
        hg = nn(fg[...], wd) + nn(mid_dg[...], di[:, blk])
        sig = 1.0 / (1.0 + jnp.exp(-g))
        si = g * sig
        hid = (si * u).astype(BF16)
        gg = (hg * u * (sig * (1.0 + g * (1.0 - sig)))).astype(BF16)
        ug = (hg * si).astype(BF16)
        gout[:, blk] = 2.0 * nn(mid_t[0:16], gg)
        uout[:, blk] = 2.0 * nn(mid_t[16:32], ug)
        din[:, blk] = nn(dg_t[0:16], hid)
        midd[...] += nt(hid, di[:, blk])
        midg[...] += nt(gg, bg[:, blk]) + nt(ug, bu[:, blk])
        for c0 in range(0, D, 512):
            cols = slice(c0, c0 + 512)
            f = nt(hid, wd[cols, :])
            d = nt(gg, wg[cols, :]) + nt(ug, wu[cols, :])
            if first and start == 0:
                accf[:, cols] = f
                accn[:, cols] = d
            else:
                accf[:, cols] += f
                accn[:, cols] += d
        start += n
    if last:
        midd_b = midd[...].astype(BF16)
        midg_b = midg[...].astype(BF16)
        for c0 in range(0, D, 512):
            cols = slice(c0, c0 + 512)
            part_f[:, cols] = (accf[:, cols] + nn(midd_b, do2[:, cols])).astype(BF16)
            part_n[:, cols] = (accn[:, cols] + nn(midg_b, a_gu[:, cols])).astype(BF16)
        d_out[...] = 2.0 * nn(midd[...].T.astype(BF16)[0:16], fg[...])
        gu_in[...] = nn(midg[...].T.astype(BF16)[0:32], nf[...])
    else:
        co = [
            pltpu.make_async_copy(accf, accf_o, sem_acc.at[0]),
            pltpu.make_async_copy(accn, accn_o, sem_acc.at[1]),
        ]
        for c in co:
            c.start()
        midd_o[...] = midd[...]
        midg_o[...] = midg[...]
        for c in co:
            c.wait()


def ffn_call(width, first, last, offs, nf, fg, mid_gu, mid_dg, bg, bu, di, wp, tail, prev):
    args = [offs, nf, fg, mid_gu, mid_dg, bg, bu, di, *wp]
    specs = [SM] + [VM] * 7 + [HB] * 5
    if last:
        args += list(tail)
        specs += [VM] * 2
    if not first:
        args += list(prev)
        specs += [HB, HB, VM, VM]
    small = [sds((16, width), F32)] * 3
    if last:
        shapes = [sds((TOK, D), BF16)] * 2 + [sds((32, D), F32), sds((16, D), F32)] + small
        ospecs = [VM] * 7
    else:
        shapes = [sds((TOK, D), F32)] * 2 + [sds((TOK, 128), F32)] * 2 + small
        ospecs = [HB, HB] + [VM] * 5

    def body(*refs):
        ffn_kernel(width, first, last, *refs)

    return pl.pallas_call(
        body,
        out_shape=tuple(shapes),
        in_specs=specs,
        out_specs=tuple(ospecs),
        scratch_shapes=[
            pltpu.VMEM((D, 3 * width), BF16),
            pltpu.VMEM((TOK, D), F32),
            pltpu.VMEM((TOK, D), F32),
            pltpu.VMEM((TOK, 128), F32),
            pltpu.VMEM((TOK, 128), F32),
            pltpu.SemaphoreType.DMA((16,)),
            pltpu.SemaphoreType.DMA((2,)),
        ],
        compiler_params=params(),
        cost_estimate=pl.CostEstimate(
            flops=12 * TOK * D * width, bytes_accessed=20_000_000, transcendentals=0
        ),
        name="ffn_chunk",
    )(*args)


def out_back_kernel(
    offs, og, resid, own, other, gain, oi, oo2, mid_att, att, hsel, w0, w1, w2, w3, w4,
    rg_o, do_o, delta_o, oout_o, oin_o, w, abg, sem,
):
    cs = piece_copies(offs, (w0, w1, w2, w3, w4), w, sem)
    for c in cs:
        c.start()
    for r in range(4):
        rows = pl.ds(r * 128, 128)
        x = resid[rows, :]
        inv = lax.rsqrt(jnp.mean(x * x, axis=-1, keepdims=True) + EPS)
        wv = (own[rows, :].astype(F32) + other[rows, :].astype(F32)) * gain[...]
        dot = jnp.mean(wv * x, axis=-1, keepdims=True)
        rg = og[rows, :].astype(F32) + inv * wv - x * (inv * inv * inv * dot)
        rg_o[rows, :] = rg
        abg[rows, :] = (RS * rg).astype(BF16)
    g = abg[...]
    mid_g = nt(g, oo2[...]).astype(BF16)
    oout_o[...] = 2.0 * nn(mid_att[...].astype(F32).T.astype(BF16)[0:16], g)
    oin_o[...] = nn(mid_g.astype(F32).T.astype(BF16)[0:16], att[...])
    for c in cs:
        c.wait()
    delta = jnp.zeros((16, TOK), F32)
    for n in range(3):
        cols = slice(n * 256, (n + 1) * 256)
        dd = (nn(g, w[:, cols]) + nn(mid_g, oi[:, cols])).astype(BF16)
        do_o[:, cols] = dd
        prod = dd.astype(F32) * att[:, cols].astype(F32)
        high = prod.astype(BF16)
        low = (prod - high.astype(F32)).astype(BF16)
        delta = delta + nt(hsel[:, cols], high) + nt(hsel[:, cols], low)
    delta_o[...] = delta


def out_back_call(offs, og, resid, own, other, gain, oi, oo2, mid_att, att, hsel, wo):
    return pl.pallas_call(
        out_back_kernel,
        out_shape=(
            sds((TOK, D), F32),
            sds((TOK, HQ), BF16),
            sds((16, TOK), F32),
            sds((16, D), F32),
            sds((16, HQ), F32),
        ),
        in_specs=[SM] + [VM] * 10 + [HB] * 5,
        out_specs=(VM,) * 5,
        scratch_shapes=[
            pltpu.VMEM((D, HQ), BF16),
            pltpu.VMEM((TOK, D), BF16),
            pltpu.SemaphoreType.DMA((16,)),
        ],
        compiler_params=params(),
        cost_estimate=pl.CostEstimate(
            flops=2 * TOK * D * HQ, bytes_accessed=14_000_000, transcendentals=0
        ),
        name="out_proj_back",
    )(offs, og, resid, own, other, gain, oi, oo2, mid_att, att, hsel, *wo)


def qkv_back_kernel(
    offs_a, offs_b, dq, d0, d1, d2, cos, sin, b2, a1, mid, normed,
    q0, q1, q2, q3, q4, k0, k1, k2, k3, k4,
    part, in_o, out_o, wq, wkv, dall, sem_a, sem_b,
):
    cq = piece_copies(offs_a, (q0, q1, q2, q3, q4), wq, sem_a)
    ck = piece_copies(offs_b, (k0, k1, k2, k3, k4), wkv, sem_b)
    for c in cq + ck:
        c.start()
    cw = jnp.concatenate([cos[...], cos[...]], axis=1)
    sw = jnp.concatenate([sin[...], sin[...]], axis=1)
    for n in range(3):
        g = dq[:, n * 256 : (n + 1) * 256]
        dall[:, n * 256 : (n + 1) * 256] = (g * cw - half_swap(g) * sw).astype(BF16)
    g = d0[0] + d1[0].astype(F32) + d2[0].astype(F32)
    dall[:, 768:1024] = (g * cw - half_swap(g) * sw).astype(BF16)
    dall[:, 1024:1280] = (d0[1] + d1[1].astype(F32) + d2[1].astype(F32)).astype(BF16)
    d = dall[...]
    mid_g = nt(d, b2[...]).astype(BF16)
    mid_t = mid[...].astype(F32).T.astype(BF16)
    out_o[:, 0:768] = 2.0 * nn(mid_t[0:16], dall[:, 0:768])
    out_o[:, 768:1024] = 2.0 * nn(mid_t[16:32], dall[:, 768:1024])
    out_o[:, 1024:1280] = 2.0 * nn(mid_t[32:48], dall[:, 1024:1280])
    in_o[...] = nn(mid_g.astype(F32).T.astype(BF16)[0:48], normed[...])
    for c in cq + ck:
        c.wait()
    for n in range(6):
        cols = slice(n * 256, (n + 1) * 256)
        acc = nt(dall[:, 0:768], wq[cols, :]) + nt(dall[:, 768:1280], wkv[cols, :])
        part[:, cols] = (acc + nn(mid_g, a1[:, cols])).astype(BF16)


def qkv_back_call(offs_a, offs_b, dq, d0, d1, d2, cos, sin, b2, a1, mid, normed, wq, wkv):
    return pl.pallas_call(
        qkv_back_kernel,
        out_shape=(sds((TOK, D), BF16), sds((48, D), F32), sds((16, 1280), F32)),
        in_specs=[SM, SM] + [VM] * 10 + [HB] * 10,
        out_specs=(VM,) * 3,
        scratch_shapes=[
            pltpu.VMEM((D, HQ), BF16),
            pltpu.VMEM((D, 2 * HK), BF16),
            pltpu.VMEM((TOK, 1280), BF16),
            pltpu.SemaphoreType.DMA((16,)),
            pltpu.SemaphoreType.DMA((16,)),
        ],
        compiler_params=params(),
        cost_estimate=pl.CostEstimate(
            flops=2 * TOK * D * 1280, bytes_accessed=12_000_000, transcendentals=0
        ),
        name="qkv_back",
    )(offs_a, offs_b, dq, d0, d1, d2, cos, sin, b2, a1, mid, normed, *wq, *wkv)


def token_grad_kernel(tok, rg, own, other, gain, out):
    for r in range(4):
        rows = pl.ds(r * 128, 128)
        x = tok[rows, :].astype(F32)
        inv = lax.rsqrt(jnp.mean(x * x, axis=-1, keepdims=True) + EPS)
        wv = (own[rows, :].astype(F32) + other[rows, :].astype(F32)) * gain[...]
        dot = jnp.mean(wv * x, axis=-1, keepdims=True)
        out[rows, :] = (rg[rows, :] + inv * wv - x * (inv * inv * inv * dot)).astype(BF16)


def token_grad_call(tok, rg, own, other, gain):
    return pl.pallas_call(
        token_grad_kernel,
        out_shape=sds((TOK, D), BF16),
        in_specs=[VM] * 5,
        out_specs=VM,
        compiler_params=params(),
        cost_estimate=pl.CostEstimate(
            flops=TOK * D * 10, bytes_accessed=9_000_000, transcendentals=0
        ),
        name="token_grad",
    )(tok, rg, own, other, gain)


YLIN = (0, 2, 1, 3)


def go_x(v, step):
    return lax.ppermute(v, "x", [(i, (i + step) % 4) for i in range(4)])


def go_y(v, step):
    return lax.ppermute(
        v, ("tensor", "yh"), [(YLIN[i], YLIN[(i + step) % 4]) for i in range(4)]
    )


def go_z(v, step):
    return lax.ppermute(v, "seq", [(i, (i + step) % 4) for i in range(4)])


def go_core(v):
    return lax.ppermute(v, "core", [(0, 1), (1, 0)])


def to_role(v):
    return lax.ppermute(v, ("tensor", "core"), [(0, 0), (1, 2), (2, 1), (3, 3)])


REL = (0, -1, 1, 2)


def ring_gather(shard, near, far):
    line = jnp.stack([shard, near(shard, 1), near(shard, -1), near(shard, 2)])
    below, above = far(line, 1), far(line, -1)
    return (line, below, above, far(below[:2], 1), far(above[2:], -1))


def offsets(x, y, path):
    out = []
    for far_rel, near_rel in ((0, REL), (-1, REL), (1, REL), (2, REL[:2]), (2, REL[2:])):
        for nr in near_rel:
            if path == "yx":
                out.append(((x + far_rel) % 4) * 4 + (y + nr) % 4)
            else:
                out.append(((x + nr) % 4) * 4 + (y + far_rel) % 4)
    return jnp.stack(out).astype(jnp.int32)


def finish_grads(packed, z, core, index):
    m = packed.shape[1] // 4
    parts = packed.reshape(16, 4, m)
    pick = lambda k: lax.dynamic_index_in_dim(parts, (z + k) % 4, 1, keepdims=False)
    total = pick(0).astype(F32)
    for k in (1, 2, 3):
        total = total + go_z(pick(k), k).astype(F32)
    mine = jnp.concatenate(
        [total.astype(BF16), jnp.full((16, 128), index.astype(BF16), BF16)], axis=1
    )
    line = jnp.stack([mine, go_y(mine, 1), go_y(mine, -1), go_y(mine, 2)])
    plane = jnp.concatenate([line, go_x(line, 1), go_x(line, -1), go_x(line, 2)], axis=0)
    which = plane[:, 0, m].astype(F32)
    onehot = (which[None, :] == jnp.arange(8, dtype=F32)[:, None]).astype(BF16)
    dense = lax.dot_general(
        onehot, plane[:, :, :m], (((1,), (0,)), ((), ())), preferred_element_type=F32
    ).astype(BF16)
    whole = jnp.zeros((4, 8, 16, m), BF16)
    for rel, piece in (
        (0, dense),
        (-1, go_z(dense, 1)),
        (1, go_z(dense, -1)),
        (2, go_z(dense, 2)),
    ):
        whole = lax.dynamic_update_index_in_dim(whole, piece, (z + rel) % 4, 0)
    other = go_core(whole)
    first = jnp.where(core == 0, whole, other)
    second = jnp.where(core == 0, other, whole)
    flat = lambda v: v.transpose(1, 2, 0, 3).reshape(8, 16, 4 * m).astype(F32)
    return flat(first), flat(second)


def core_sum(rep, core):
    low, high = rep[:, :768].astype(BF16), rep[:, 768:].astype(BF16)
    send = jnp.where(core == 0, high, low)
    keep = jnp.where(core == 0, low, high)
    return (keep.astype(F32) + go_core(send).astype(F32)).astype(BF16)


def pad_rows(v, rows=128, at=0):
    return jnp.pad(v, ((at, rows - at - v.shape[0]), (0, 0)))


def shards(
    tokens,
    output_gradient,
    document_length_table,
    sequence_adapter_index,
    sequence_window_length,
    attention_norm_gain,
    feedforward_norm_gain,
    query_projection_weight,
    key_projection_weight,
    value_projection_weight,
    output_projection_weight,
    gate_projection_weight,
    up_projection_weight,
    down_projection_weight,
    query_adapter_first,
    query_adapter_second,
    key_adapter_first,
    key_adapter_second,
    value_adapter_first,
    value_adapter_second,
    output_adapter_first,
    output_adapter_second,
    gate_adapter_first,
    gate_adapter_second,
    up_adapter_first,
    up_adapter_second,
    down_adapter_first,
    down_adapter_second,
):
    z = lax.axis_index("seq")
    yl = lax.axis_index("tensor")
    x = lax.axis_index("x")
    y = lax.axis_index("yh") * 2 + yl
    core = lax.axis_index("core")
    same = core == yl

    w_q = to_role(query_projection_weight)
    w_kv = to_role(jnp.concatenate([key_projection_weight, value_projection_weight], axis=1))
    starts = [sum(CHUNKS[:i]) for i in range(len(CHUNKS))]
    three = (gate_projection_weight, up_projection_weight, down_projection_weight)
    chunk_cols = [
        jnp.concatenate([w[:, s : s + n] for w in three], axis=1)
        for s, n in zip(starts, CHUNKS, strict=True)
    ]
    yx_cols = to_role(
        jnp.concatenate([c for c, p in zip(chunk_cols, CHUNK_PATH) if p == "yx"], axis=1)
    )
    xy_cols = to_role(
        jnp.concatenate(
            [output_projection_weight]
            + [c for c, p in zip(chunk_cols, CHUNK_PATH) if p == "xy"],
            axis=1,
        )
    )
    offs = {"yx": offsets(x, y, "yx"), "xy": offsets(x, y, "xy")}
    full_q = ring_gather(w_q, go_y, go_x)
    full_kv = ring_gather(w_kv, go_x, go_y)
    full_o = ring_gather(xy_cols[:, :HQ], go_x, go_y)
    full_ffn = []
    at = {"yx": 0, "xy": HQ}
    for n, path in zip(CHUNKS, CHUNK_PATH, strict=True):
        src = yx_cols if path == "yx" else xy_cols
        cols = src[:, at[path] : at[path] + 3 * n]
        at[path] += 3 * n
        full_ffn.append(ring_gather(cols, *((go_y, go_x) if path == "yx" else (go_x, go_y))))

    tok_other = go_core(tokens[0])
    tok = jnp.where(same, tokens[0], tok_other)
    og_other = go_core(output_gradient[0])
    og = jnp.where(same, output_gradient[0], og_other)
    meta = jnp.concatenate(
        [document_length_table[0], sequence_adapter_index, sequence_window_length]
    )
    meta = jnp.where(same, meta, go_core(meta))
    lengths, index, window = meta[:4], meta[4], meta[5]
    own_index = sequence_adapter_index[0]
    pick_own = lambda v: lax.dynamic_index_in_dim(v, own_index, 0, keepdims=False)
    pick = lambda v: lax.dynamic_index_in_dim(v, index, 0, keepdims=False)
    halves = to_role(
        jnp.concatenate(
            [
                pick_own(v)
                for v in (
                    query_adapter_second,
                    key_adapter_second,
                    value_adapter_second,
                    output_adapter_first,
                    gate_adapter_second,
                    up_adapter_second,
                    down_adapter_first,
                )
            ],
            axis=1,
        )
    )
    b_q, b_k, b_v, o_i = halves[:, :768], halves[:, 768:1024], halves[:, 1024:1280], halves[:, 1280:2048]
    b_g, b_u, d_i = halves[:, 2048:3968], halves[:, 3968:5888], halves[:, 5888:7808]
    a_q, a_k, a_v, a_g, a_u = (
        pick(v.swapaxes(1, 2))
        for v in (
            query_adapter_first,
            key_adapter_first,
            value_adapter_first,
            gate_adapter_first,
            up_adapter_first,
        )
    )
    o_o, d_o = pick(output_adapter_second), pick(down_adapter_second)
    a_qkv = pad_rows(jnp.concatenate([a_q, a_k, a_v], axis=0))
    b_qkv = 2 * jnp.concatenate(
        [pad_rows(b_q), pad_rows(b_k, at=16), pad_rows(b_v, at=32)], axis=1
    )
    a_gu = pad_rows(jnp.concatenate([a_g, a_u], axis=0))
    bg2, bu2 = pad_rows(2 * b_g), pad_rows(2 * b_u, at=16)
    di_p, oi_p = pad_rows(d_i), pad_rows(o_i)
    oo2, do2 = pad_rows(2 * o_o), pad_rows(2 * d_o)

    ends = jnp.cumsum(lengths, dtype=jnp.int32)
    begins = ends - lengths
    place = z * TOK + jnp.arange(TOK, dtype=jnp.int32)
    begin = jnp.max(jnp.where(place[:, None] >= begins[None, :], begins[None, :], 0), axis=1)
    lo = (jnp.maximum(begin, place - window + 1) - (z * TOK - HALO))[None, :]
    lane = jnp.arange(128, dtype=jnp.int32) % HDIM
    frequency = ROPE_BASE ** (-((lane % 32).astype(F32) * (2.0 / HDIM)))
    angles = (place - begin).astype(F32)[:, None] * frequency[None, :]
    cos = jnp.cos(angles)
    sin = jnp.sin(angles) * jnp.where(lane < 32, -1.0, 1.0)[None, :]

    gain1 = attention_norm_gain[None, :]
    gain2 = feedforward_norm_gain[None, :]

    normed, q, kv0, mid_qkv = qkv_call(
        offs["yx"], offs["xy"], tok, gain1, a_qkv, b_qkv, cos, sin, full_q, full_kv
    )
    kv1 = lax.ppermute(kv0, "seq", [(0, 1), (1, 2), (2, 3)])
    kv2 = lax.ppermute(kv0, "seq", [(0, 2), (1, 3)])
    att, lse = attend_call(q, lo, kv2, kv1, kv0)
    attn_part, mid_att = out_proj_call(offs["xy"], att, oi_p, oo2, full_o)
    attn_other = go_core(attn_part)
    resid, nf, mid_gu = ffn_in_call(tok, attn_part, attn_other, gain2, a_gu)
    fg, mid_dg = cot_call(og, do2)
    prev = None
    couts = []
    for i, (s, n) in enumerate(zip(starts, CHUNKS, strict=True)):
        first, last = i == 0, i == len(CHUNKS) - 1
        res = ffn_call(
            n, first, last, offs[CHUNK_PATH[i]], nf, fg, mid_gu, mid_dg,
            bg2[:, s : s + n], bu2[:, s : s + n], di_p[:, s : s + n], full_ffn[i], (a_gu, do2), prev,
        )
        prev = res[:4]
        couts.append(res[4:])
    ffn_part, nfg_part, gu_in, d_out = prev
    g_out, u_out, d_in = (jnp.concatenate([c[k] for c in couts], axis=1) for k in range(3))
    nfg_other = go_core(nfg_part)
    ffn_other = go_core(ffn_part)
    out = (resid + RS * (ffn_part.astype(F32) + ffn_other.astype(F32))).astype(BF16)
    output = to_role(out)

    hsel = jnp.stack(
        [
            (jnp.arange(HQ) // HDIM == (6 * (r // 8) + r % 8)) & (r % 8 < 6)
            for r in range(16)
        ]
    ).astype(BF16)
    rg, do, delta, o_out, o_in = out_back_call(
        offs["xy"], og, resid, nfg_part, nfg_other, gain2, oi_p, oo2, mid_att, att, hsel, full_o
    )
    dq, d2, d1, d0 = attend_back_call(q, do, lse, delta, lo, kv2, kv1, kv0)
    r1 = lax.ppermute(d1, "seq", [(1, 0), (2, 1), (3, 2)])
    r2 = lax.ppermute(d2, "seq", [(2, 0), (3, 1)])
    na_part, qkv_in, qkv_out = qkv_back_call(
        offs["yx"], offs["xy"], dq, d0, r1, r2, cos, sin, b_qkv, a_qkv, mid_qkv, normed,
        full_q, full_kv,
    )
    na_other = go_core(na_part)
    token_grad = to_role(token_grad_call(tok, rg, na_part, na_other, gain1))

    rep = core_sum(jnp.concatenate([gu_in, d_out, o_out], axis=0), core)
    early = jnp.concatenate(
        [rep[0:16], rep[16:32], rep[32:48], rep[48:64]]
        + [v.astype(BF16) for v in (g_out, u_out, d_in, o_in)]
        + [jnp.zeros((16, 128), BF16)],
        axis=1,
    )
    e0, e1 = finish_grads(early, z, core, index)
    rep = core_sum(qkv_in, core)
    late = jnp.concatenate([rep[0:16], rep[16:32], rep[32:48], qkv_out.astype(BF16)], axis=1)
    l0, l1 = finish_grads(late, z, core, index)

    def join(pair, start, width):
        return jnp.concatenate([v[:, :, start : start + width] for v in pair], axis=2)

    e, l = (e0, e1), (l0, l1)
    g_in_f, u_in_f, d_out_f, o_out_f = (join(e, k * 768, 768) for k in range(4))
    g_out_f = join(e, 3072, 1920)
    u_out_f = join(e, 4992, 1920)
    d_in_f = join(e, 6912, 1920)
    o_in_f = join(e, 8832, 768)
    q_in_f, k_in_f, v_in_f = (join(l, k * 768, 768) for k in range(3))
    q_out_f = join(l, 2304, 768)
    k_out_f = join(l, 3072, 256)
    v_out_f = join(l, 3328, 256)
    t = lambda v: v.swapaxes(1, 2)
    return (
        output[None],
        token_grad[None],
        t(q_in_f),
        q_out_f,
        t(k_in_f),
        k_out_f,
        t(v_in_f),
        v_out_f,
        o_in_f,
        o_out_f,
        t(g_in_f),
        g_out_f,
        t(u_in_f),
        u_out_f,
        d_in_f,
        d_out_f,
    )


def solution(mesh):
    fine = Mesh(mesh.devices.reshape(4, 2, 4, 2, 2), ("seq", "tensor", "x", "yh", "core"))
    fsdp = ("x", "yh", "core")
    weight = P(fsdp, "tensor")
    half = P(None, None, "tensor")
    return jax.shard_map(
        shards,
        mesh=fine,
        in_specs=(
            P(fsdp, "seq", None),
            P(fsdp, "seq", None),
            P(fsdp, None),
            P(fsdp),
            P(fsdp),
            P(),
            P(),
        )
        + (weight,) * 7
        + (P(), half, P(), half, P(), half, half, P(), P(), half, P(), half, half, P()),
        out_specs=(P(fsdp, "seq", None), P(fsdp, "seq", None)) + (P(),) * 14,
        check_vma=False,
    )
```

```python
import jax
import jax.numpy as jnp
import numpy as np
from jax import lax
from jax.experimental import pallas as pl
from jax.experimental.pallas import tpu as pltpu
from jax.sharding import Mesh
from jax.sharding import PartitionSpec as P

F32 = jnp.float32
BF16 = jnp.bfloat16
EPS = 1e-05
ROPE_BASE = 10000.0
RS = 1.4 / 52.0**0.5
MASKED = -1e30
TOK = 512
D = 1536
DX = D + 128
HQ = 768
HK = 256
HDIM = 64
SPAN = 1280
RT = 256
HALO = 1024
FH = 1920
FA, FB, FC = 640, 640, 640
EARLY = 2048
LATE = 1280


def nn(a, b):
    return lax.dot_general(a, b, (((1,), (0,)), ((), ())), preferred_element_type=F32)


def nt(a, b):
    return lax.dot_general(a, b, (((1,), (1,)), ((), ())), preferred_element_type=F32)


def tn(a, b):
    return lax.dot_general(a, b, (((0,), (0,)), ((), ())), preferred_element_type=F32)


VM = pl.BlockSpec(memory_space=pltpu.VMEM)
SM = pl.BlockSpec(memory_space=pltpu.SMEM)
HB = pl.BlockSpec(memory_space=pl.ANY)


def row_block(width):
    return pl.BlockSpec((128, width), lambda i: (i, 0))


def all_block(rows, width):
    return pl.BlockSpec((rows, width), lambda i: (0, 0))


def params():
    return pltpu.CompilerParams(vmem_limit_bytes=58 * 1024 * 1024)


def cost():
    return pl.CostEstimate(flops=1, bytes_accessed=1, transcendentals=0)


def sds(shape, dtype):
    return jax.ShapeDtypeStruct(shape, dtype)


def piece_copies(offs, refs, dst, sems):
    copies = []
    for ref in refs:
        for k in range(ref.shape[0]):
            row = pl.multiple_of(offs[len(copies)] * 96, 96)
            copies.append(
                pltpu.make_async_copy(ref.at[k], dst.at[pl.ds(row, 96)], sems.at[len(copies)])
            )
    return copies


def half_swap(v, sign=1):
    lane = lax.broadcasted_iota(jnp.int32, v.shape, 1)
    width = v.shape[1]
    from_low = pltpu.roll(v, 32, 1)
    from_high = pltpu.roll(v, width - 32, 1)
    return jnp.where((lane % 64) < 32, from_high, from_low)


def qkv_kernel(offs, tok, gain, a1, b2, cos, sin, *refs):
    pieces, (normed_o, q_o, kv_o, mid_o, w, sem) = refs[:5], refs[5:]
    cs = piece_copies(offs, pieces, w, sem)
    for c in cs:
        c.start()
    for r in range(4):
        rows = pl.ds(r * 128, 128)
        x = tok[rows, :].astype(F32)
        inv = lax.rsqrt(jnp.mean(x * x, axis=-1, keepdims=True) + EPS)
        normed_o[rows, :] = (x * inv * gain[...]).astype(BF16)
    normed = normed_o[...]
    mid = nt(normed, a1[...]).astype(BF16)
    mid_o[...] = mid
    for c in cs:
        c.wait()
    cw = jnp.concatenate([cos[...], cos[...]], axis=1)
    sw = jnp.concatenate([sin[...], sin[...]], axis=1)
    for n in (3, 4, 0, 1, 2):
        cols = slice(n * 256, (n + 1) * 256)
        acc = nn(normed, w[:, cols]) + nn(mid, b2[:, cols])
        if n < 4:
            acc = acc * cw + half_swap(acc) * sw
        if n < 3:
            q_o[:, cols] = (acc.astype(BF16).astype(F32) * 0.125).astype(BF16)
        else:
            kv_o[n - 3] = acc.astype(BF16)


def qkv_call(offs, tok, gain, a1, b2, cos, sin, w):
    return pl.pallas_call(
        qkv_kernel,
        out_shape=(
            sds((TOK, D), BF16),
            sds((TOK, HQ), BF16),
            sds((2, TOK, HK), BF16),
            sds((TOK, 128), BF16),
        ),
        in_specs=[SM] + [VM] * 6 + [HB] * 5,
        out_specs=(VM,) * 4,
        scratch_shapes=[pltpu.VMEM((D, 1280), BF16), pltpu.SemaphoreType.DMA((16,))],
        compiler_params=params(),
        cost_estimate=cost(),
        name="norm_qkv",
    )(offs, tok, gain, a1, b2, cos, sin, *w)


HEADS_OF_PAIR = ((0, 0, 0), (0, 1, 0), (1, 0, 0), (1, 1, 1), (2, 0, 1), (2, 1, 1))


def bias_of(lo, r):
    key = lax.broadcasted_iota(jnp.int32, (SPAN, RT), 0) + r * RT
    row = lax.broadcasted_iota(jnp.int32, (SPAN, RT), 1) + r * RT + HALO
    return jnp.where((key >= lo) & (key <= row), 0.0, MASKED)


def variants(dst, src):
    lane = lax.broadcasted_iota(jnp.int32, src.shape, 1)
    srcf = src.astype(F32)
    rolled = pltpu.roll(srcf, 64, 1)
    low = lane < 64
    dst[0] = jnp.where(low, srcf, 0.0).astype(BF16)
    dst[1] = jnp.where(low, 0.0, rolled).astype(BF16)
    dst[2] = jnp.where(low, rolled, 0.0).astype(BF16)
    dst[3] = jnp.where(low, 0.0, srcf).astype(BF16)


def attend_kernel(q, lo, kv2, kv1, kv0, out, lse, kvar, vt, bias, ot):
    r = pl.program_id(1)

    @pl.when(r == 0)
    def _():
        kcat = jnp.concatenate([kv2[0], kv1[0], kv0[0]], axis=0)
        variants(kvar, kcat)
        vcat = jnp.concatenate([kv2[1], kv1[1], kv0[1]], axis=0)
        vt[...] = vcat.astype(F32).T.astype(BF16)

    bias[...] = bias_of(lo[...], r)
    keys = pl.ds(pl.multiple_of(r * RT, RT), SPAN)
    for i, (tile, half, kv) in enumerate(HEADS_OF_PAIR):
        qt = q[:, tile * 128 : (tile + 1) * 128]
        s = nt(kvar[2 * kv + half, keys, :], qt) + bias[...]
        m = jnp.max(s, axis=0, keepdims=True)
        e = jnp.exp(s - m)
        total = jnp.sum(e, axis=0, keepdims=True)
        o = nn(vt[kv * 64 : (kv + 1) * 64, keys], e.astype(BF16))
        ot[i * 64 : (i + 1) * 64, :] = o * (1.0 / total)
        lse[i : i + 1, :] = m + jnp.log(total)
    out[...] = ot[...].T.astype(BF16)


def attend_call(q, lo, kv2, kv1, kv0):
    kvspec = pl.BlockSpec((2, TOK, 128), lambda p, r: (0, 0, p))
    return pl.pallas_call(
        attend_kernel,
        grid=(2, 2),
        out_shape=(sds((TOK, HQ), BF16), sds((16, TOK), F32)),
        in_specs=[
            pl.BlockSpec((RT, 384), lambda p, r: (r, p)),
            pl.BlockSpec((1, RT), lambda p, r: (0, r)),
            kvspec,
            kvspec,
            kvspec,
        ],
        out_specs=(
            pl.BlockSpec((RT, 384), lambda p, r: (r, p)),
            pl.BlockSpec((8, RT), lambda p, r: (p, r)),
        ),
        scratch_shapes=[
            pltpu.VMEM((4, HALO + TOK, 128), BF16),
            pltpu.VMEM((128, HALO + TOK), BF16),
            pltpu.VMEM((SPAN, RT), F32),
            pltpu.VMEM((384, RT), F32),
        ],
        compiler_params=params(),
        cost_estimate=cost(),
        name="attend",
    )(q, lo, kv2, kv1, kv0)


def attend_back_kernel(
    q, do, lse, delta, lo, kv2, kv1, kv0, dq, d2, d1, d0,
    kvar, vvar, kt, bias, dqt, dk_same, dk_cross, dv_same, dv_cross,
):
    r = pl.program_id(1)

    @pl.when(r == 0)
    def _():
        kcat = jnp.concatenate([kv2[0], kv1[0], kv0[0]], axis=0)
        variants(kvar, kcat)
        kt[...] = kcat.astype(F32).T.astype(BF16)
        vcat = jnp.concatenate([kv2[1], kv1[1], kv0[1]], axis=0)
        variants(vvar, vcat)
        for ref in (dk_same, dk_cross, dv_same, dv_cross):
            ref[...] = jnp.zeros_like(ref)

    bias[...] = bias_of(lo[...], r)
    keys = pl.ds(pl.multiple_of(r * RT, RT), SPAN)
    lane = lax.broadcasted_iota(jnp.int32, (RT, 128), 1)
    for i, (tile, half, kv) in enumerate(HEADS_OF_PAIR):
        cols = slice(tile * 128, (tile + 1) * 128)
        qt = q[:, cols]
        dt = do[:, cols]
        keep = (lane < 64) if half == 0 else (lane >= 64)
        qm = jnp.where(keep, qt, jnp.zeros_like(qt))
        dm = jnp.where(keep, dt, jnp.zeros_like(dt))
        s = nt(kvar[2 * kv + half, keys, :], qt) + bias[...]
        p = jnp.exp(s - lse[i : i + 1, :])
        dp = nt(vvar[2 * kv + half, keys, :], dt)
        ds = (p * (dp - delta[i : i + 1, :])).astype(BF16)
        dk_acc, dv_acc = (dk_same, dv_same) if half == kv else (dk_cross, dv_cross)
        dv_acc[keys, :] += nn(p.astype(BF16), dm)
        dk_acc[keys, :] += nn(ds, qm)
        dqt[i * 64 : (i + 1) * 64, :] = nn(kt[kv * 64 : (kv + 1) * 64, keys], ds)
    dq[...] = dqt[...].T * 0.125

    @pl.when(r == 1)
    def _():
        dk = dk_same[...] + pltpu.roll(dk_cross[...], 64, 1)
        dv = dv_same[...] + pltpu.roll(dv_cross[...], 64, 1)
        d2[0] = dk[0:512].astype(BF16)
        d2[1] = dv[0:512].astype(BF16)
        d1[0] = dk[512:1024].astype(BF16)
        d1[1] = dv[512:1024].astype(BF16)
        d0[0] = dk[1024:1536]
        d0[1] = dv[1024:1536]


def attend_back_call(p, q, do, lse, delta, lo, kv2, kv1, kv0):
    kvspec = pl.BlockSpec((2, TOK, 128), lambda i, r: (0, 0, p))
    rowspec = pl.BlockSpec((RT, 384), lambda i, r: (r, p))
    statspec = pl.BlockSpec((8, RT), lambda i, r: (p, r))
    kvout = pl.BlockSpec((2, TOK, 128), lambda i, r: (0, 0, 0))
    acc = pltpu.VMEM((HALO + TOK, 128), F32)
    return pl.pallas_call(
        attend_back_kernel,
        grid=(1, 2),
        out_shape=(
            sds((TOK, 384), F32),
            sds((2, TOK, 128), BF16),
            sds((2, TOK, 128), BF16),
            sds((2, TOK, 128), F32),
        ),
        in_specs=[
            rowspec,
            rowspec,
            statspec,
            statspec,
            pl.BlockSpec((1, RT), lambda i, r: (0, r)),
            kvspec,
            kvspec,
            kvspec,
        ],
        out_specs=(pl.BlockSpec((RT, 384), lambda i, r: (r, 0)), kvout, kvout, kvout),
        scratch_shapes=[
            pltpu.VMEM((4, HALO + TOK, 128), BF16),
            pltpu.VMEM((4, HALO + TOK, 128), BF16),
            pltpu.VMEM((128, HALO + TOK), BF16),
            pltpu.VMEM((SPAN, RT), F32),
            pltpu.VMEM((384, RT), F32),
            acc,
            acc,
            acc,
            acc,
        ],
        compiler_params=params(),
        cost_estimate=cost(),
        name="attend_back",
    )(q, do, lse, delta, lo, kv2, kv1, kv0)


def out_proj_kernel(offs, att, oi, oo2, wo, part, mid_o, w, sem):
    cs = piece_copies(offs, (wo,), w, sem)
    for c in cs:
        c.start()
    a = att[...]
    mid = nt(a, oi[...]).astype(BF16)
    mid_o[...] = mid
    for c in cs:
        c.wait()
    for n in range(3):
        cols = slice(n * 512, (n + 1) * 512)
        part[:, cols] = (nt(a, w[cols, :]) + nn(mid, oo2[:, cols])).astype(BF16)


def out_proj_call(offs, att, oi, oo2, wo):
    return pl.pallas_call(
        out_proj_kernel,
        out_shape=(sds((TOK, D), BF16), sds((TOK, 128), BF16)),
        in_specs=[SM] + [VM] * 3 + [HB],
        out_specs=(VM, VM),
        scratch_shapes=[pltpu.VMEM((D, HQ), BF16), pltpu.SemaphoreType.DMA((16,))],
        compiler_params=params(),
        cost_estimate=cost(),
        name="out_proj",
    )(offs, att, oi, oo2, wo)


def ffn_in_kernel(tok, own, other, gain, a_gu, resid_o, nf_o, mid_o):
    branch = own[...].astype(F32) + other[...].astype(F32)
    x = tok[...].astype(F32) + RS * branch
    resid_o[...] = x
    inv = lax.rsqrt(jnp.mean(x * x, axis=-1, keepdims=True) + EPS)
    nf_o[...] = (x * inv * gain[...]).astype(BF16)
    mid_o[...] = nt(nf_o[...], a_gu[...]).astype(BF16)


def ffn_in_call(tok, own, other, gain, a_gu):
    return pl.pallas_call(
        ffn_in_kernel,
        grid=(4,),
        out_shape=(sds((TOK, D), F32), sds((TOK, D), BF16), sds((TOK, 128), BF16)),
        in_specs=[row_block(D)] * 3 + [all_block(1, D), all_block(128, D)],
        out_specs=(row_block(D), row_block(D), row_block(128)),
        compiler_params=params(),
        cost_estimate=cost(),
        name="ffn_norm",
    )(tok, own, other, gain, a_gu)


def cot_kernel(og, do2, fg_o, mid_o):
    fg_o[...] = (RS * og[...].astype(F32)).astype(BF16)
    mid_o[...] = nt(fg_o[...], do2[...]).astype(BF16)


def cot_call(og, do2):
    return pl.pallas_call(
        cot_kernel,
        out_shape=(sds((TOK, D), BF16), sds((TOK, 128), BF16)),
        in_specs=[VM] * 2,
        out_specs=(VM,) * 2,
        compiler_params=params(),
        cost_estimate=cost(),
        name="branch_cotangent",
    )(og, do2)


def ffn_kernel(offs_a, offs_b, nf, fg, mid_gu, mid_dg, bg, bu, di, a_gu, do2, *refs):
    pb, pa, pc = refs[:5], refs[5:10], refs[10:15]
    part_f, part_n, rep_o, gout, uout, din = refs[15:21]
    wb, wa, wc, xn, xf, accf, accn, sem_b, sem_a, sem_c = refs[21:]
    cb = piece_copies(offs_b, pb, wb, sem_b)
    ca = piece_copies(offs_a, pa, wa, sem_a)
    cc = piece_copies(offs_b, pc, wc, sem_c)
    for c in cb + ca + cc:
        c.start()
    xn[:, 0:D] = nf[...]
    xn[:, D:DX] = mid_gu[...]
    xf[:, 0:D] = fg[...]
    xf[:, D:DX] = mid_dg[...]
    mid_t = mid_gu[...].astype(F32).T.astype(BF16)[0:32]
    dg_t = mid_dg[...].astype(F32).T.astype(BF16)[0:16]
    for w, copies, start, n in ((wb, cb, FA, FB), (wa, ca, 0, FA), (wc, cc, FA + FB, FC)):
        blk = slice(start, start + n)
        w[D:DX, 0:n] = bg[:, blk]
        w[D:DX, n : 2 * n] = bu[:, blk]
        w[D:DX, 2 * n : 3 * n] = di[:, blk]
        for c in copies:
            c.wait()
        gu = nn(xn[...], w[:, 0 : 2 * n])
        hg = nn(xf[...], w[:, 2 * n : 3 * n])
        g, u = gu[:, 0:n], gu[:, n : 2 * n]
        sig = 1.0 / (1.0 + jnp.exp(-g))
        si = g * sig
        hid = (si * u).astype(BF16)
        gg = (hg * u * (sig * (1.0 + g * (1.0 - sig)))).astype(BF16)
        ug = (hg * si).astype(BF16)
        both = jnp.concatenate([gg, ug], axis=1)
        terms = 2.0 * nn(mid_t, both)
        gout[:, blk] = terms[0:16, 0:n].astype(BF16)
        uout[:, blk] = terms[16:32, n : 2 * n].astype(BF16)
        din[:, blk] = nn(dg_t, hid).astype(BF16)
        for c0, c1 in ((0, 512), (512, 1024), (1024, DX)):
            cols = slice(c0, c1)
            f = nt(hid, w[cols, 2 * n : 3 * n])
            d = nt(both, w[cols, 0 : 2 * n])
            if w is wb:
                accf[:, cols] = f
                accn[:, cols] = d
            else:
                accf[:, cols] += f
                accn[:, cols] += d
    midd, midg = accf[:, D:DX], accn[:, D:DX]
    midd_b = midd.astype(BF16)
    midg_b = midg.astype(BF16)
    for c0 in range(0, D, 512):
        cols = slice(c0, c0 + 512)
        part_n[:, cols] = (accn[:, cols] + nn(midg_b, a_gu[:, cols])).astype(BF16)
        part_f[:, cols] = (accf[:, cols] + nn(midd_b, do2[:, cols])).astype(BF16)
    gu_in = nn(midg.T.astype(BF16)[0:32], nf[...])
    d_out = 2.0 * nn(midd.T.astype(BF16)[0:16], fg[...])
    for c in range(2):
        half = slice(c * 768, (c + 1) * 768)
        rep_o[c, 0:32] = gu_in[:, half].astype(BF16)
        rep_o[c, 32:48] = d_out[:, half].astype(BF16)


def ffn_call(offs_a, offs_b, nf, fg, mid_gu, mid_dg, bg, bu, di, a_gu, do2, wb, wa, wc):
    return pl.pallas_call(
        ffn_kernel,
        out_shape=(sds((TOK, D), BF16), sds((TOK, D), BF16), sds((2, 48, 768), BF16))
        + (sds((16, FH), BF16),) * 3,
        in_specs=[SM, SM] + [VM] * 9 + [HB] * 15,
        out_specs=(VM,) * 6,
        scratch_shapes=[
            pltpu.VMEM((DX, 3 * FB), BF16),
            pltpu.VMEM((DX, 3 * FA), BF16),
            pltpu.VMEM((DX, 3 * FC), BF16),
            pltpu.VMEM((TOK, DX), BF16),
            pltpu.VMEM((TOK, DX), BF16),
            pltpu.VMEM((TOK, DX), F32),
            pltpu.VMEM((TOK, DX), F32),
            pltpu.SemaphoreType.DMA((16,)),
            pltpu.SemaphoreType.DMA((16,)),
            pltpu.SemaphoreType.DMA((16,)),
        ],
        compiler_params=params(),
        cost_estimate=cost(),
        name="ffn_both",
    )(offs_a, offs_b, nf, fg, mid_gu, mid_dg, bg, bu, di, a_gu, do2, *wb, *wa, *wc)


def out_back_kernel(
    offs, og, resid, own, other, gain, oi, oo2, mid_att, att, hsel, wo,
    rg_o, do_o, delta_o, rep_o, oin_o, w, abg, sem,
):
    cs = piece_copies(offs, (wo,), w, sem)
    for c in cs:
        c.start()
    for r in range(4):
        rows = pl.ds(r * 128, 128)
        x = resid[rows, :]
        inv = lax.rsqrt(jnp.mean(x * x, axis=-1, keepdims=True) + EPS)
        wv = (own[rows, :].astype(F32) + other[rows, :].astype(F32)) * gain[...]
        dot = jnp.mean(wv * x, axis=-1, keepdims=True)
        rg = og[rows, :].astype(F32) + inv * wv - x * (inv * inv * inv * dot)
        rg_o[rows, :] = rg
        abg[rows, :] = (RS * rg).astype(BF16)
    g = abg[...]
    mid_g = nt(g, oo2[...]).astype(BF16)
    for c in cs:
        c.wait()
    delta = jnp.zeros((16, TOK), F32)
    for n in range(3):
        cols = slice(n * 256, (n + 1) * 256)
        dd = (nn(g, w[:, cols]) + nn(mid_g, oi[:, cols])).astype(BF16)
        do_o[:, cols] = dd
        prod = dd.astype(F32) * att[:, cols].astype(F32)
        high = prod.astype(BF16)
        low = (prod - high.astype(F32)).astype(BF16)
        delta = delta + nt(hsel[:, cols], high) + nt(hsel[:, cols], low)
    delta_o[...] = delta
    o_out = 2.0 * nn(mid_att[...].astype(F32).T.astype(BF16)[0:16], g)
    for c in range(2):
        rep_o[c] = o_out[:, c * 768 : (c + 1) * 768].astype(BF16)
    oin_o[...] = nn(mid_g.astype(F32).T.astype(BF16)[0:16], att[...]).astype(BF16)


def out_back_call(offs, og, resid, own, other, gain, oi, oo2, mid_att, att, hsel, wo):
    return pl.pallas_call(
        out_back_kernel,
        out_shape=(
            sds((TOK, D), F32),
            sds((TOK, HQ), BF16),
            sds((16, TOK), F32),
            sds((2, 16, 768), BF16),
            sds((16, HQ), BF16),
        ),
        in_specs=[SM] + [VM] * 10 + [HB],
        out_specs=(VM,) * 5,
        scratch_shapes=[
            pltpu.VMEM((D, HQ), BF16),
            pltpu.VMEM((TOK, D), BF16),
            pltpu.SemaphoreType.DMA((16,)),
        ],
        compiler_params=params(),
        cost_estimate=cost(),
        name="out_proj_back",
    )(offs, og, resid, own, other, gain, oi, oo2, mid_att, att, hsel, wo)


def q_back_kernel(offs, dq0, dq1, cos, sin, b2, a1, mid, normed, *refs):
    pieces, (part, in_o, out_o, w, dall, sem) = refs[:5], refs[5:]
    cs = piece_copies(offs, [p.at[:, :, pl.ds(0, HQ)] for p in pieces], w, sem)
    for c in cs:
        c.start()
    cw = jnp.concatenate([cos[...], cos[...]], axis=1)
    sw = jnp.concatenate([sin[...], sin[...]], axis=1)
    dq = jnp.concatenate([dq0[...], dq1[...]], axis=1)
    for n in range(3):
        g = dq[:, n * 256 : (n + 1) * 256]
        dall[:, n * 256 : (n + 1) * 256] = (g * cw - half_swap(g) * sw).astype(BF16)
    d = dall[...]
    mid_g = nt(d, b2[:, 0:HQ]).astype(BF16)
    mid_t = mid[...].astype(F32).T.astype(BF16)
    out_o[...] = (2.0 * nn(mid_t[0:16], d)).astype(BF16)
    in_o[...] = nn(mid_g.astype(F32).T.astype(BF16)[0:16], normed[...]).astype(BF16)
    for c in cs:
        c.wait()
    for n in range(3):
        cols = slice(n * 512, (n + 1) * 512)
        part[:, cols] = nt(d, w[cols, :]) + nn(mid_g, a1[:, cols])


def q_back_call(offs, dq0, dq1, cos, sin, b2, a1, mid, normed, w):
    return pl.pallas_call(
        q_back_kernel,
        out_shape=(sds((TOK, D), F32), sds((16, D), BF16), sds((16, HQ), BF16)),
        in_specs=[SM] + [VM] * 8 + [HB] * 5,
        out_specs=(VM,) * 3,
        scratch_shapes=[
            pltpu.VMEM((D, HQ), BF16),
            pltpu.VMEM((TOK, HQ), BF16),
            pltpu.SemaphoreType.DMA((16,)),
        ],
        compiler_params=params(),
        cost_estimate=cost(),
        name="q_back",
    )(offs, dq0, dq1, cos, sin, b2, a1, mid, normed, *w)


def kv_back_kernel(offs, qpart, q_in, da0, da1, da2, db0, db1, db2, cos, sin, b2, a1, mid, normed, orep, *refs):
    pieces, (part, rep_o, out_o, w, dall, sem) = refs[:5], refs[5:]
    cs = piece_copies(offs, [p.at[:, :, pl.ds(HQ, 512)] for p in pieces], w, sem)
    for c in cs:
        c.start()
    cw = jnp.concatenate([cos[...], cos[...]], axis=1)
    sw = jnp.concatenate([sin[...], sin[...]], axis=1)
    both = []
    for i in range(2):
        own = jnp.concatenate([da0[i], db0[i]], axis=1)
        one = jnp.concatenate([da1[i], db1[i]], axis=1)
        two = jnp.concatenate([da2[i], db2[i]], axis=1)
        both.append(own + one.astype(F32) + two.astype(F32))
    dall[:, 0:256] = (both[0] * cw - half_swap(both[0]) * sw).astype(BF16)
    dall[:, 256:512] = both[1].astype(BF16)
    d = dall[...]
    mid_g = nt(d, b2[:, HQ:1280]).astype(BF16)
    mid_t = mid[...].astype(F32).T.astype(BF16)
    out_o[:, 0:256] = (2.0 * nn(mid_t[16:32], dall[:, 0:256])).astype(BF16)
    out_o[:, 256:512] = (2.0 * nn(mid_t[32:48], dall[:, 256:512])).astype(BF16)
    in_grads = nn(mid_g.astype(F32).T.astype(BF16)[16:48], normed[...]).astype(BF16)
    for c in range(2):
        cols = slice(c * 768, (c + 1) * 768)
        rep_o[c, 0:16] = q_in[:, cols]
        rep_o[c, 16:48] = in_grads[:, cols]
        rep_o[c, 48:64] = orep[c]
    for c in cs:
        c.wait()
    for n in range(3):
        cols = slice(n * 512, (n + 1) * 512)
        part[:, cols] = (qpart[:, cols] + nt(d, w[cols, :]) + nn(mid_g, a1[:, cols])).astype(BF16)


def kv_back_call(offs, qpart, q_in, da, db, cos, sin, b2, a1, mid, normed, orep, w):
    return pl.pallas_call(
        kv_back_kernel,
        out_shape=(sds((TOK, D), BF16), sds((2, 64, 768), BF16), sds((16, 512), BF16)),
        in_specs=[SM] + [VM] * 15 + [HB] * 5,
        out_specs=(VM,) * 3,
        scratch_shapes=[
            pltpu.VMEM((D, 512), BF16),
            pltpu.VMEM((TOK, 512), BF16),
            pltpu.SemaphoreType.DMA((16,)),
        ],
        compiler_params=params(),
        cost_estimate=cost(),
        name="kv_back",
    )(offs, qpart, q_in, *da, *db, cos, sin, b2, a1, mid, normed, orep, *w)


def token_grad_kernel(tok, rg, own, other, gain, out):
    x = tok[...].astype(F32)
    inv = lax.rsqrt(jnp.mean(x * x, axis=-1, keepdims=True) + EPS)
    wv = (own[...].astype(F32) + other[...].astype(F32)) * gain[...]
    dot = jnp.mean(wv * x, axis=-1, keepdims=True)
    out[...] = (rg[...] + inv * wv - x * (inv * inv * inv * dot)).astype(BF16)


def token_grad_call(tok, rg, own, other, gain):
    return pl.pallas_call(
        token_grad_kernel,
        grid=(4,),
        out_shape=sds((TOK, D), BF16),
        in_specs=[row_block(D)] * 4 + [all_block(1, D)],
        out_specs=row_block(D),
        compiler_params=params(),
        cost_estimate=cost(),
        name="token_grad",
    )(tok, rg, own, other, gain)


def pack_first_kernel(q, k, v, out):
    out[:, 0:768] = q[...]
    out[:, 768:1024] = k[...]
    out[:, 1024:1280] = v[...]


def pack_first_call(q, k, v):
    return pl.pallas_call(
        pack_first_kernel,
        out_shape=sds((96, 1280), BF16),
        in_specs=[VM] * 3,
        out_specs=VM,
        compiler_params=params(),
        cost_estimate=cost(),
        name="pack_qkv",
    )(q, k, v)


def pack_rest_kernel(o, g, u, d, yx, xy1, xy2):
    yx[:, 0:HQ] = o[...]
    for i, w in enumerate((g, u, d)):
        yx[:, HQ + i * FA : HQ + (i + 1) * FA] = w[:, 0:FA]
        xy1[:, i * FB : (i + 1) * FB] = w[:, FA : FA + FB]
        xy2[:, i * FC : (i + 1) * FC] = w[:, FA + FB : FH]


def pack_rest_call(o, g, u, d):
    return pl.pallas_call(
        pack_rest_kernel,
        out_shape=(
            sds((96, HQ + 3 * FA), BF16),
            sds((96, 3 * FB), BF16),
            sds((96, 3 * FC), BF16),
        ),
        in_specs=[VM] * 4,
        out_specs=(VM,) * 3,
        compiler_params=params(),
        cost_estimate=cost(),
        name="pack_rest",
    )(o, g, u, d)


def line_call(parts, head):
    n = parts[0].shape[1] - head

    def kernel(*refs):
        ins, outs = refs[:4], refs[4:]
        for i in range(4):
            if head:
                outs[0][i] = ins[i][:, 0:head]
            outs[-1][i] = ins[i][:, head:]

    shapes = (sds((4, 96, head), BF16),) * bool(head) + (sds((4, 96, n), BF16),)
    return pl.pallas_call(
        kernel,
        out_shape=shapes,
        in_specs=[VM] * 4,
        out_specs=(VM,) * len(shapes),
        compiler_params=params(),
        cost_estimate=cost(),
        name="line",
    )(*parts)


def own_half_kernel(idx, q, k, v, o, g, u, d, out):
    at = 0
    for ref in (q, k, v, o, g, u, d):
        n = ref.shape[2]
        out[:, at : at + n] = ref[0]
        at += n


def own_half_call(index, arrays):
    return pl.pallas_call(
        own_half_kernel,
        out_shape=sds((16, 7808), BF16),
        grid_spec=pltpu.PrefetchScalarGridSpec(
            num_scalar_prefetch=1,
            grid=(1,),
            in_specs=[
                pl.BlockSpec((1, 16, a.shape[2]), lambda i, idx: (idx[0], 0, 0)) for a in arrays
            ],
            out_specs=pl.BlockSpec((16, 7808), lambda i, idx: (0, 0)),
        ),
        compiler_params=params(),
        cost_estimate=cost(),
        name="pick_halves",
    )(index, *arrays)


def factors_kernel(
    idx, halves, aq, ak, av, ag, au, oo, do, a_qkv, b_qkv, a_gu, bg, bu, di, oi, oo2, do2
):
    for ref in (a_qkv, b_qkv, a_gu, bg, bu, di, oi, oo2, do2):
        ref[...] = jnp.zeros_like(ref)
    for i, ref in enumerate((aq, ak, av)):
        a_qkv[i * 16 : (i + 1) * 16] = ref[0]
    for i, ref in enumerate((ag, au)):
        a_gu[i * 16 : (i + 1) * 16] = ref[0]
    oo2[0:16] = 2 * oo[0]
    do2[0:16] = 2 * do[0]
    b_qkv[0:16, 0:768] = 2 * halves[:, 0:768]
    b_qkv[16:32, 768:1024] = 2 * halves[:, 768:1024]
    b_qkv[32:48, 1024:1280] = 2 * halves[:, 1024:1280]
    oi[0:16] = halves[:, 1280:2048]
    bg[0:16] = 2 * halves[:, 2048:3968]
    bu[16:32] = 2 * halves[:, 3968:5888]
    di[0:16] = halves[:, 5888:7808]


def factors_call(index, halves, arrays):
    widths = (D, 1280, D, FH, FH, FH, HQ, D, D)
    return pl.pallas_call(
        factors_kernel,
        out_shape=tuple(sds((128, w), BF16) for w in widths),
        grid_spec=pltpu.PrefetchScalarGridSpec(
            num_scalar_prefetch=1,
            grid=(1,),
            in_specs=[pl.BlockSpec((16, 7808), lambda i, idx: (0, 0))]
            + [pl.BlockSpec((1, 16, D), lambda i, idx: (idx[0], 0, 0))] * 7,
            out_specs=tuple(pl.BlockSpec((128, w), lambda i, idx: (0, 0)) for w in widths),
        ),
        compiler_params=params(),
        cost_estimate=cost(),
        name="factors",
    )(index, halves, *arrays)


def quarters_kernel(m, place, rep, got, *refs):
    parts, outs, buf = refs[:-5], refs[-5:-1], refs[-1]
    core, z = place[0], place[1]
    n_rep = rep.shape[1] // 16
    kept = (rep[core].astype(F32) + got[...].astype(F32)).astype(BF16)
    for i in range(n_rep):
        buf[:, i * 768 : (i + 1) * 768] = kept[i * 16 : (i + 1) * 16]
    at = n_rep * 768
    for p in parts:
        buf[:, at : at + p.shape[1]] = p[...]
        at += p.shape[1]
    if at < 4 * m:
        buf[:, at : 4 * m] = jnp.zeros((16, 4 * m - at), BF16)
    for k, out in enumerate(outs):
        quarter = lax.rem(z + k, 4)
        out[...] = buf[:, pl.ds(pl.multiple_of(quarter * m, 128), m)]


def quarters_call(m, place, rep, got, parts):
    def kernel(*refs):
        quarters_kernel(m, *refs)

    return pl.pallas_call(
        kernel,
        out_shape=(sds((16, m), BF16),) * 4,
        in_specs=[SM] + [VM] * (2 + len(parts)),
        out_specs=(VM,) * 4,
        scratch_shapes=[pltpu.VMEM((16, 4 * m), BF16)],
        compiler_params=params(),
        cost_estimate=cost(),
        name="quarters",
    )(place, rep, got, *parts)


def pack_early_kernel(place, rep, got, g, u, d, out):
    kept = (rep[place[0]].astype(F32) + got[...].astype(F32)).astype(BF16)
    for i in range(3):
        out[:, i * 768 : (i + 1) * 768] = kept[i * 16 : (i + 1) * 16]
    for i, ref in enumerate((g, u, d)):
        out[:, 2304 + i * FH : 2304 + (i + 1) * FH] = ref[...]
    out[:, 8064:8192] = jnp.zeros((16, 128), BF16)


def pack_early_call(place, rep, got, g, u, d):
    return pl.pallas_call(
        pack_early_kernel,
        out_shape=sds((16, 4 * EARLY), BF16),
        in_specs=[SM] + [VM] * 5,
        out_specs=VM,
        compiler_params=params(),
        cost_estimate=cost(),
        name="pack_early",
    )(place, rep, got, g, u, d)


def quarter_kernel(place, total, out):
    at = pl.multiple_of(place[1] * EARLY, 128)
    out[:, 0:EARLY] = total[:, pl.ds(at, EARLY)]
    out[:, EARLY : EARLY + 128] = (
        jnp.full((16, 128), place[2], jnp.int32).astype(F32).astype(BF16)
    )


def quarter_call(place, total):
    return pl.pallas_call(
        quarter_kernel,
        out_shape=sds((16, EARLY + 128), BF16),
        in_specs=[SM, VM],
        out_specs=VM,
        compiler_params=params(),
        cost_estimate=cost(),
        name="quarter",
    )(place, total)


def sum_kernel(place, a, b, c, d, out):
    m = a.shape[1]
    total = a[...].astype(F32) + b[...].astype(F32) + c[...].astype(F32) + d[...].astype(F32)
    out[:, 0:m] = total.astype(BF16)
    out[:, m : m + 128] = jnp.full((16, 128), place[2], jnp.int32).astype(F32).astype(BF16)


def sum_call(place, parts):
    m = parts[0].shape[1]
    return pl.pallas_call(
        sum_kernel,
        out_shape=sds((16, m + 128), BF16),
        in_specs=[SM] + [VM] * 4,
        out_specs=VM,
        compiler_params=params(),
        cost_estimate=cost(),
        name="sum_tokens",
    )(place, *parts)


def by_adapter_kernel(*refs):
    ins, out = refs[:-1], refs[-1]
    m = out.shape[2]
    rows = [(r, k) for r in ins for k in range(r.shape[0])]
    for a in range(8):
        total = jnp.zeros((16, m), F32)
        for r, k in rows:
            hit = r[k, :, m : m + 1].astype(F32) == float(a)
            total = total + jnp.where(hit, r[k, :, 0:m].astype(F32), 0.0)
        out[a] = total.astype(BF16)


def by_adapter_call(parts, m):
    return pl.pallas_call(
        by_adapter_kernel,
        out_shape=sds((8, 16, m), BF16),
        in_specs=[VM] * len(parts),
        out_specs=VM,
        compiler_params=params(),
        cost_estimate=cost(),
        name="by_adapter",
    )(*parts)


def spread(buf, outs, jobs, widths):
    at = 0
    for out, n in zip(outs, widths, strict=True):
        for c in range(2):
            out[:, :, c * n : (c + 1) * n] = buf[c, :, :, at : at + n].astype(F32)
        at += n


def unpack_early_kernel(src, *refs):
    outs, buf, sem = refs[:-2], refs[-2], refs[-1]
    copies = []
    for z in range(4):
        for c in range(2):
            copies.append(
                pltpu.make_async_copy(
                    src.at[2 * z + c], buf.at[c, :, :, pl.ds(z * EARLY, EARLY)], sem.at[2 * z + c]
                )
            )
    for c in copies:
        c.start()
    for c in copies:
        c.wait()
    spread(buf, outs, None, (768, 768, 768, FH, FH, FH))


def unpack_early_call(src):
    widths = (D, D, D, 2 * FH, 2 * FH, 2 * FH)
    return pl.pallas_call(
        unpack_early_kernel,
        out_shape=tuple(sds((8, 16, w), F32) for w in widths),
        in_specs=[HB],
        out_specs=(VM,) * 6,
        scratch_shapes=[pltpu.VMEM((2, 8, 16, 4 * EARLY), BF16), pltpu.SemaphoreType.DMA((8,))],
        compiler_params=params(),
        cost_estimate=cost(),
        name="unpack_early",
    )(src)


def unpack_late_kernel(place, *refs):
    srcs, outs, buf, sem = refs[:8], refs[8:-2], refs[-2], refs[-1]
    core, z = place[0], place[1]
    copies = []
    for i, src in enumerate(srcs):
        c = core if i < 4 else 1 - core
        at = lax.rem(z + REL[i % 4] + 4, 4) * LATE
        copies.append(
            pltpu.make_async_copy(
                src, buf.at[c, :, :, pl.ds(pl.multiple_of(at, 128), LATE)], sem.at[i]
            )
        )
    for c in copies:
        c.start()
    for c in copies:
        c.wait()
    spread(buf, outs, None, (768, 768, 768, 768, 768, 256, 256, 768))


def unpack_late_call(place, srcs):
    widths = (D, D, D, D, D, 512, 512, D)
    return pl.pallas_call(
        unpack_late_kernel,
        out_shape=tuple(sds((8, 16, w), F32) for w in widths),
        in_specs=[SM] + [HB] * 8,
        out_specs=(VM,) * 8,
        scratch_shapes=[pltpu.VMEM((2, 8, 16, 4 * LATE), BF16), pltpu.SemaphoreType.DMA((8,))],
        compiler_params=params(),
        cost_estimate=cost(),
        name="unpack_late",
    )(place, *srcs)


YLIN = (0, 2, 1, 3)


def go_x(v, step):
    return lax.ppermute(v, "x", [(i, (i + step) % 4) for i in range(4)])


def go_y(v, step):
    return lax.ppermute(
        v, ("tensor", "yh"), [(YLIN[i], YLIN[(i + step) % 4]) for i in range(4)]
    )


def go_z(v, step):
    return lax.ppermute(v, "seq", [(i, (i + step) % 4) for i in range(4)])


def go_core(v):
    return lax.ppermute(v, "core", [(0, 1), (1, 0)])


def to_role(v):
    return lax.ppermute(v, ("tensor", "core"), [(1, 2), (2, 1)])


REL = (0, -1, 1, 2)


def near_line(shard, near):
    return (shard, near(shard, 1), near(shard, -1), near(shard, 2))


def ring_start(line, far):
    return (line, far(line, 1), far(line, -1))


def ring_halves(below, above):
    return below[:2], above[2:]


class Order:
    def __init__(self):
        self.last = ()

    def gate(self, v):
        return lax.optimization_barrier((v, self.last))[0]

    def done(self, v):
        v = self.gate(v)
        self.last = jax.tree.leaves(v)[-1:]
        return v

    def run(self, step, *args):
        out = step(*self.gate(args))
        self.last = jax.tree.leaves(out)[-1:]
        return out


def offsets(x, y, path):
    near = np.tile(np.array(REL, np.int32), 4)
    far = np.repeat(np.array(REL, np.int32), 4)
    if path == "yx":
        return ((x + far + 4) % 4) * 4 + (y + near + 4) % 4
    if path == "xy":
        return np.tile(np.arange(4, dtype=np.int32), 4) * 4 + (y + far + 4) % 4
    return np.repeat(np.arange(4, dtype=np.int32), 4) * 4 + (y + near + 4) % 4


def halo_back(grads):
    two, one, own = grads
    one = lax.ppermute(one, "seq", [(1, 0), (2, 1), (3, 2)])
    return (own, one, lax.ppermute(two, "seq", [(2, 0), (3, 1)]))


def shards(
    tokens,
    output_gradient,
    document_length_table,
    sequence_adapter_index,
    sequence_window_length,
    attention_norm_gain,
    feedforward_norm_gain,
    query_projection_weight,
    key_projection_weight,
    value_projection_weight,
    output_projection_weight,
    gate_projection_weight,
    up_projection_weight,
    down_projection_weight,
    query_adapter_first,
    query_adapter_second,
    key_adapter_first,
    key_adapter_second,
    value_adapter_first,
    value_adapter_second,
    output_adapter_first,
    output_adapter_second,
    gate_adapter_first,
    gate_adapter_second,
    up_adapter_first,
    up_adapter_second,
    down_adapter_first,
    down_adapter_second,
):
    z = lax.axis_index("seq")
    yl = lax.axis_index("tensor")
    x = lax.axis_index("x")
    y = lax.axis_index("yh") * 2 + yl
    core = lax.axis_index("core")
    same = core == yl

    o = Order()
    t = lambda v: v.swapaxes(1, 2)
    mine = lambda own, got: jnp.where(same, own, got)
    offs_yx, offs_xy, offs_o = (offsets(x, y, p) for p in ("yx", "xy", "o"))
    gain1 = attention_norm_gain[None, :]
    gain2 = feedforward_norm_gain[None, :]

    own_qkv = o.run(
        pack_first_call, query_projection_weight, key_projection_weight, value_projection_weight
    )
    got_qkv = to_role(own_qkv)
    own_yx, own_b, own_c = o.run(
        pack_rest_call,
        output_projection_weight,
        gate_projection_weight,
        up_projection_weight,
        down_projection_weight,
    )
    got_b = to_role(own_b)
    meta = jnp.concatenate(
        [document_length_table[0], sequence_adapter_index, sequence_window_length]
    )
    meta_other = go_core(meta)
    tok_other = go_core(o.gate(tokens[0]))
    own_halves = o.run(
        own_half_call,
        sequence_adapter_index,
        (
            query_adapter_second,
            key_adapter_second,
            value_adapter_second,
            output_adapter_first,
            gate_adapter_second,
            up_adapter_second,
            down_adapter_first,
        ),
    )
    near_qkv = near_line(o.run(mine, own_qkv, o.done(got_qkv)), go_y)
    line_b = lax.all_gather(o.run(mine, own_b, o.done(got_b)), "x", axis=0)

    def tables(own, other):
        meta = mine(own, other)
        lengths, index, window = meta[:4], meta[4:5], meta[5]
        place = jnp.concatenate([jnp.stack([core, z]).astype(jnp.int32), index])
        ends = jnp.cumsum(lengths, dtype=jnp.int32)
        begins = ends - lengths
        row = z * TOK + jnp.arange(TOK, dtype=jnp.int32)
        begin = jnp.max(jnp.where(row[:, None] >= begins[None, :], begins[None, :], 0), axis=1)
        low_key = (jnp.maximum(begin, row - window + 1) - (z * TOK - HALO))[None, :]
        lane = jnp.arange(128, dtype=jnp.int32) % HDIM
        frequency = ROPE_BASE ** (-((lane % 32).astype(F32) * (2.0 / HDIM)))
        angles = (row - begin).astype(F32)[:, None] * frequency[None, :]
        cos = jnp.cos(angles)
        sin = jnp.sin(angles) * jnp.where(lane < 32, -1.0, 1.0)[None, :]
        return index, place, low_key, cos, sin

    index, place, low_key, cos, sin = o.run(tables, meta, o.done(meta_other))
    tok = o.run(mine, tokens[0], o.done(tok_other))
    line_qkv = o.run(lambda *v: line_call(v, 0)[0], *o.done(near_qkv))
    below_qkv, above_qkv = go_x(line_qkv, 1), go_x(line_qkv, -1)
    got_halves, got_yx, got_c = (to_role(o.gate(v)) for v in (own_halves, own_yx, own_c))
    og_other = go_core(o.gate(output_gradient[0]))
    halves = o.run(mine, own_halves, o.done(got_halves))
    a_qkv, b_qkv, a_gu, bg2, bu2, di_p, oi_p, oo2, do2 = o.run(
        factors_call,
        index,
        halves,
        (
            t(query_adapter_first),
            t(key_adapter_first),
            t(value_adapter_first),
            t(gate_adapter_first),
            t(up_adapter_first),
            output_adapter_second,
            down_adapter_second,
        ),
    )
    near_yx = near_line(o.run(mine, own_yx, o.done(got_yx)), go_y)
    line_c = lax.all_gather(o.run(mine, own_c, o.done(got_c)), "x", axis=0)
    og = o.run(mine, output_gradient[0], o.done(og_other))
    fg, mid_dg = o.run(cot_call, og, do2)
    line_b = o.done(line_b)
    below_b, above_b = go_y(line_b, 1), go_y(line_b, -1)
    low, high = o.run(ring_halves, *o.done((below_qkv, above_qkv)))
    far_qkv = (go_x(low, 1), go_x(high, -1))
    line_o, line_a = o.run(lambda *v: line_call(v, HQ), *o.done(near_yx))
    full_o = lax.all_gather(line_o, "x", axis=0, tiled=True)
    full_qkv = (line_qkv, below_qkv, above_qkv) + o.done(far_qkv)

    normed, q, kv0, mid_qkv = o.run(
        qkv_call, offs_yx, tok, gain1, a_qkv, b_qkv, cos, sin, full_qkv
    )
    kv1 = lax.ppermute(kv0, "seq", [(0, 1), (1, 2), (2, 3)])
    kv2 = lax.ppermute(kv0, "seq", [(0, 2), (1, 3)])
    line_a = o.gate(line_a)
    below_a, above_a = go_x(line_a, 1), go_x(line_a, -1)
    low, high = o.run(ring_halves, *o.done((below_b, above_b)))
    far_b = (go_y(low, 1), go_y(high, -1))
    line_c = o.done(line_c)
    below_c, above_c = go_y(line_c, 1), go_y(line_c, -1)
    kv1, kv2 = o.done((kv1, kv2))
    att, lse = o.run(attend_call, q, low_key, kv2, kv1, kv0)
    full_o = o.done(full_o)
    attn_part, mid_att = o.run(out_proj_call, offs_o, att, oi_p, oo2, full_o)
    attn_other = go_core(attn_part)
    low, high = o.run(ring_halves, *o.done((below_a, above_a)))
    far_a = (go_x(low, 1), go_x(high, -1))
    resid, nf, mid_gu = o.run(ffn_in_call, tok, attn_part, o.done(attn_other), gain2, a_gu)
    low, high = o.run(ring_halves, *o.done((below_c, above_c)))
    far_c = (go_y(low, 1), go_y(high, -1))
    full_b = (line_b, below_b, above_b) + o.done(far_b)
    full_a = (line_a, below_a, above_a) + o.done(far_a)
    full_c = (line_c, below_c, above_c) + o.done(far_c)
    ffn_part, nfg_part, rep_e, g_out, u_out, d_in = o.run(
        ffn_call,
        offs_yx, offs_xy, nf, fg, mid_gu, mid_dg, bg2, bu2, di_p, a_gu, do2, full_b, full_a, full_c,
    )

    def exchange(rep):
        return go_core(lax.dynamic_index_in_dim(rep, 1 - core, 0, keepdims=False))

    nfg_other = go_core(nfg_part)
    got_e = exchange(rep_e)
    quarters = o.run(
        lambda *v: quarters_call(EARLY, place, v[0], v[1], v[2:]),
        rep_e, o.done(got_e), g_out, u_out, d_in,
    )
    sent = [go_z(quarters[k], k) for k in (1, 2, 3)]
    head = np.arange(16)
    head = np.where(head % 8 < 6, 6 * (head // 8) + head % 8, -1)
    hsel = jnp.asarray((np.arange(HQ) // HDIM)[None, :] == head[:, None], BF16)
    rg, do, delta, rep_o, o_in = o.run(
        out_back_call,
        offs_o, og, resid, nfg_part, o.done(nfg_other), gain2, oi_p, oo2, mid_att, att, hsel, full_o,
    )
    ffn_other = go_core(o.gate(ffn_part))
    near = near_line(o.run(sum_call, place, [quarters[0]] + o.done(sent)), go_y)
    stats = (lse, delta, low_key, kv2, kv1, kv0)
    dqa, *da = o.run(lambda *v: attend_back_call(0, *v), q, do, *stats)
    ra = halo_back(da)
    plane = lax.all_gather(o.run(lambda *v: jnp.stack(v), *o.done(near)), "x", axis=0, tiled=True)
    dqb, *db = o.run(lambda *v: attend_back_call(1, *v), q, do, *stats)
    rb = halo_back(db)
    qpart, q_in, q_out = o.run(
        q_back_call, offs_yx, dqa, dqb, cos, sin, b_qkv, a_qkv, mid_qkv, normed, full_qkv
    )
    out = o.run(
        lambda r, a, b: (r + RS * (a.astype(F32) + b.astype(F32))).astype(BF16),
        resid, ffn_part, o.done(ffn_other),
    )
    out_other = to_role(out)
    dense = o.run(lambda v: by_adapter_call([v], EARLY), o.done(plane))
    ra, rb = o.done((ra, rb))
    early = lax.all_gather(o.gate(dense), ("seq", "core"), axis=0)
    na_part, rep_l, kv_out = o.run(
        kv_back_call,
        offs_yx, qpart, q_in, ra, rb, cos, sin, b_qkv, a_qkv, mid_qkv, normed, rep_o, full_qkv,
    )
    na_other = go_core(na_part)
    got_l = exchange(rep_l)

    quarters = o.run(
        lambda *v: quarters_call(LATE, place, v[0], v[1], v[2:]),
        rep_l, o.done(got_l), q_out, kv_out, o_in,
    )
    sent = [go_z(quarters[k], k) for k in (1, 2, 3)]
    token_grad = o.run(token_grad_call, tok, rg, na_part, o.done(na_other), gain1)
    tg_other = to_role(token_grad)
    near = near_line(o.run(sum_call, place, [quarters[0]] + o.done(sent)), go_y)
    line = o.run(lambda *v: jnp.stack(v), *o.done(near))
    lines = [go_x(line, 1), go_x(line, -1), go_x(line, 2)]
    output = o.run(mine, out, o.done(out_other))
    dense = o.run(lambda *v: by_adapter_call(v, LATE), line, *o.done(lines))
    zs = [go_z(dense, 1), go_z(dense, -1), go_z(dense, 2)]
    cores = [go_core(dense)]
    g_in, u_in, d_out, g_out, u_out, d_in = o.run(unpack_early_call, o.done(early))
    zs = o.done(zs)
    cores += [go_core(v) for v in zs]
    token_grad = o.run(mine, token_grad, o.done(tg_other))
    q_in, k_in, v_in, o_out, q_out, k_out, v_out, o_in = o.run(
        unpack_late_call, place, [dense] + zs + o.done(cores)
    )
    return (
        output[None],
        token_grad[None],
        t(q_in),
        q_out,
        t(k_in),
        k_out,
        t(v_in),
        v_out,
        o_in,
        o_out,
        t(g_in),
        g_out,
        t(u_in),
        u_out,
        d_in,
        d_out,
    )


def solution(mesh):
    fine = Mesh(mesh.devices.reshape(4, 2, 4, 2, 2), ("seq", "tensor", "x", "yh", "core"))
    fsdp = ("x", "yh", "core")
    weight = P(fsdp, "tensor")
    half = P(None, None, "tensor")
    return jax.shard_map(
        shards,
        mesh=fine,
        in_specs=(
            P(fsdp, "seq", None),
            P(fsdp, "seq", None),
            P(fsdp, None),
            P(fsdp),
            P(fsdp),
            P(),
            P(),
        )
        + (weight,) * 7
        + (P(), half, P(), half, P(), half, half, P(), P(), half, P(), half, half, P()),
        out_specs=(P(fsdp, "seq", None), P(fsdp, "seq", None)) + (P(),) * 14,
        check_vma=False,
    )
```

```python
import jax
import jax.numpy as jnp
import numpy as np
from jax import lax
from jax.experimental import pallas as pl
from jax.experimental.pallas import tpu as pltpu
from jax.sharding import Mesh
from jax.sharding import PartitionSpec as P

F32 = jnp.float32
BF16 = jnp.bfloat16
EPS = 1e-05
ROPE_BASE = 10000.0
RS = 1.4 / 52.0**0.5
MASKED = -1e30
TOK = 512
D = 1536
DX = D + 128
HQ = 768
HK = 256
HDIM = 64
SPAN = 1280
RT = 256
HALO = 1024
FH = 1920
FA, FB = 768, 1152
EARLY = 2048
LATE = 1280


def nn(a, b):
    return lax.dot_general(a, b, (((1,), (0,)), ((), ())), preferred_element_type=F32)


def nt(a, b):
    return lax.dot_general(a, b, (((1,), (1,)), ((), ())), preferred_element_type=F32)


def tn(a, b):
    return lax.dot_general(a, b, (((0,), (0,)), ((), ())), preferred_element_type=F32)


VM = pl.BlockSpec(memory_space=pltpu.VMEM)
SM = pl.BlockSpec(memory_space=pltpu.SMEM)
HB = pl.BlockSpec(memory_space=pl.ANY)


def row_block(width):
    return pl.BlockSpec((128, width), lambda i: (i, 0))


def all_block(rows, width):
    return pl.BlockSpec((rows, width), lambda i: (0, 0))


def params():
    return pltpu.CompilerParams(vmem_limit_bytes=58 * 1024 * 1024)


def cost():
    return pl.CostEstimate(flops=1, bytes_accessed=1, transcendentals=0)


def sds(shape, dtype):
    return jax.ShapeDtypeStruct(shape, dtype)


def piece_copies(offs, refs, dst, sems):
    copies = []
    for ref in refs:
        for k in range(ref.shape[0]):
            row = pl.multiple_of(offs[len(copies)] * 96, 96)
            copies.append(
                pltpu.make_async_copy(ref.at[k], dst.at[pl.ds(row, 96)], sems.at[len(copies)])
            )
    return copies


def half_swap(v):
    lane = lax.broadcasted_iota(jnp.int32, v.shape, 1)
    width = v.shape[1]
    from_low = pltpu.roll(v, 32, 1)
    from_high = pltpu.roll(v, width - 32, 1)
    return jnp.where((lane % 64) < 32, from_high, from_low)


def qkv_kernel(offs, tok, gain, a1, b2, cos, sin, *refs):
    pieces, (normed_o, q_o, kv_o, mid_o, w, sem) = refs[:5], refs[5:]
    cs = piece_copies(offs, pieces, w, sem)
    for c in cs:
        c.start()
    for r in range(4):
        rows = pl.ds(r * 128, 128)
        x = tok[rows, :].astype(F32)
        inv = lax.rsqrt(jnp.mean(x * x, axis=-1, keepdims=True) + EPS)
        normed_o[rows, :] = (x * inv * gain[...]).astype(BF16)
    normed = normed_o[...]
    mid = nt(normed, a1[...]).astype(BF16)
    mid_o[...] = mid
    for c in cs:
        c.wait()
    cw = jnp.concatenate([cos[...], cos[...]], axis=1)
    sw = jnp.concatenate([sin[...], sin[...]], axis=1)
    for n in (3, 4, 0, 1, 2):
        cols = slice(n * 256, (n + 1) * 256)
        acc = nn(normed, w[:, cols]) + nn(mid, b2[:, cols])
        if n < 4:
            acc = acc * cw + half_swap(acc) * sw
        if n < 3:
            q_o[:, cols] = (acc.astype(BF16).astype(F32) * 0.125).astype(BF16)
        else:
            kv_o[n - 3] = acc.astype(BF16)


def qkv_call(offs, tok, gain, a1, b2, cos, sin, w):
    return pl.pallas_call(
        qkv_kernel,
        out_shape=(
            sds((TOK, D), BF16),
            sds((TOK, HQ), BF16),
            sds((2, TOK, HK), BF16),
            sds((TOK, 128), BF16),
        ),
        in_specs=[SM] + [VM] * 6 + [HB] * 5,
        out_specs=(VM,) * 4,
        scratch_shapes=[pltpu.VMEM((D, 1280), BF16), pltpu.SemaphoreType.DMA((16,))],
        compiler_params=params(),
        cost_estimate=cost(),
        name="norm_qkv",
    )(offs, tok, gain, a1, b2, cos, sin, *w)


HEADS_OF_PAIR = ((0, 0, 0), (0, 1, 0), (1, 0, 0), (1, 1, 1), (2, 0, 1), (2, 1, 1))


def bias_of(lo, r):
    key = lax.broadcasted_iota(jnp.int32, (SPAN, RT), 0) + r * RT
    row = lax.broadcasted_iota(jnp.int32, (SPAN, RT), 1) + r * RT + HALO
    return jnp.where((key >= lo) & (key <= row), 0.0, MASKED)


def variants(dst, src, other=0.0):
    lane = lax.broadcasted_iota(jnp.int32, src.shape, 1)
    srcf = src.astype(F32)
    rolled = pltpu.roll(srcf, 64, 1)
    low = lane < 64
    dst[0] = jnp.where(low, srcf, other).astype(BF16)
    dst[1] = jnp.where(low, other, rolled).astype(BF16)
    dst[2] = jnp.where(low, rolled, other).astype(BF16)
    dst[3] = jnp.where(low, other, srcf).astype(BF16)


def in_half(v, half, want):
    return v if half == want else pltpu.roll(v, 64, 1)


def attend_kernel(q, lo, kv2, kv1, kv0, out, lse, kvar, vvar, bias):
    r = pl.program_id(1)
    lane = lax.broadcasted_iota(jnp.int32, (RT, 128), 1)
    low = lane < 64

    @pl.when(r == 0)
    def _():
        variants(kvar, jnp.concatenate([kv2[0], kv1[0], kv0[0]], axis=0))
        variants(vvar, jnp.concatenate([kv2[1], kv1[1], kv0[1]], axis=0), 1.0)

    key = lax.broadcasted_iota(jnp.int32, (RT, SPAN), 1) + r * RT
    row = lax.broadcasted_iota(jnp.int32, (RT, SPAN), 0) + r * RT + HALO
    bias[...] = jnp.where((key >= lo[...]) & (key <= row), 0.0, MASKED)
    keys = pl.ds(pl.multiple_of(r * RT, RT), SPAN)
    stats = jnp.zeros((RT, 128), F32)
    for tile in range(3):
        qt = q[:, tile * 128 : (tile + 1) * 128]
        pair = []
        for i in (2 * tile, 2 * tile + 1):
            _, half, kv = HEADS_OF_PAIR[i]
            s = nt(qt, kvar[2 * kv + half, keys, :]) + bias[...]
            m = jnp.max(s, axis=1, keepdims=True)
            e = jnp.exp(s - m).astype(BF16)
            o = nn(e, vvar[2 * kv + half, keys, :])
            total = o[:, 64:65] if half == 0 else o[:, 0:1]
            stats = jnp.where(lane == i, m + jnp.log(total), stats)
            pair.append(o)
        total = pltpu.roll(jnp.where(low, pair[1], pair[0]), 64, 1)
        out[:, tile * 128 : (tile + 1) * 128] = (jnp.where(low, pair[0], pair[1]) / total).astype(BF16)
    lse[...] = stats.T[0:8]


def attend_call(q, lo, kv2, kv1, kv0):
    kvspec = pl.BlockSpec((2, TOK, 128), lambda p, r: (0, 0, p))
    return pl.pallas_call(
        attend_kernel,
        grid=(2, 2),
        out_shape=(sds((TOK, HQ), BF16), sds((16, TOK), F32)),
        in_specs=[
            pl.BlockSpec((RT, 384), lambda p, r: (r, p)),
            pl.BlockSpec((RT, 1), lambda p, r: (r, 0)),
            kvspec,
            kvspec,
            kvspec,
        ],
        out_specs=(
            pl.BlockSpec((RT, 384), lambda p, r: (r, p)),
            pl.BlockSpec((8, RT), lambda p, r: (p, r)),
        ),
        scratch_shapes=[
            pltpu.VMEM((4, HALO + TOK, 128), BF16),
            pltpu.VMEM((4, HALO + TOK, 128), BF16),
            pltpu.VMEM((RT, SPAN), F32),
        ],
        compiler_params=params(),
        cost_estimate=cost(),
        name="attend",
    )(q, lo.T, kv2, kv1, kv0)


def attend_back_kernel(
    q, do, lse, delta, lo, kv2, kv1, kv0, dq, d2, d1, d0, kvar, vvar, kt, bias, dqt, dk_acc, dv_acc
):
    r = pl.program_id(1)

    @pl.when(r == 0)
    def _():
        kcat = jnp.concatenate([kv2[0], kv1[0], kv0[0]], axis=0)
        variants(kvar, kcat)
        kt[...] = kcat.astype(F32).T.astype(BF16)
        vcat = jnp.concatenate([kv2[1], kv1[1], kv0[1]], axis=0)
        variants(vvar, vcat)
        for ref in (dk_acc, dv_acc):
            ref[...] = jnp.zeros_like(ref)

    bias[...] = bias_of(lo[...], r)
    keys = pl.ds(pl.multiple_of(r * RT, RT), SPAN)
    low = lax.broadcasted_iota(jnp.int32, (RT, 128), 1) < 64
    for u in range(2):
        ps, dss, qs, dos = [], [], [], []
        for i in range(3 * u, 3 * u + 3):
            cols = slice((i // 2) * 128, (i // 2 + 1) * 128)
            half = i % 2
            qt = q[:, cols]
            dt = do[:, cols]
            keep = low if u == 0 else ~low
            qs.append(jnp.where(keep, in_half(qt.astype(F32), half, u), 0.0).astype(BF16))
            dos.append(jnp.where(keep, in_half(dt.astype(F32), half, u), 0.0).astype(BF16))
            s = nt(kvar[2 * u + half, keys, :], qt) + bias[...]
            p = jnp.exp(s - lse[i : i + 1, :])
            dp = nt(vvar[2 * u + half, keys, :], dt)
            dss.append((p * (dp - delta[i : i + 1, :])).astype(BF16))
            ps.append(p.astype(BF16))
        ds = jnp.concatenate(dss, axis=1)
        dv_acc[keys, :] += nn(jnp.concatenate(ps, axis=1), jnp.concatenate(dos, axis=0))
        dk_acc[keys, :] += nn(ds, jnp.concatenate(qs, axis=0))
        dqu = nn(kt[u * 64 : (u + 1) * 64, keys], ds)
        for g in range(3):
            i = 3 * u + g
            dqt[i * 64 : (i + 1) * 64, :] = dqu[:, g * RT : (g + 1) * RT]
    dq[...] = dqt[...].T * 0.125

    @pl.when(r == 1)
    def _():
        dk, dv = dk_acc[...], dv_acc[...]
        d2[0] = dk[0:512].astype(BF16)
        d2[1] = dv[0:512].astype(BF16)
        d1[0] = dk[512:1024].astype(BF16)
        d1[1] = dv[512:1024].astype(BF16)
        d0[0] = dk[1024:1536]
        d0[1] = dv[1024:1536]


def attend_back_call(p, q, do, lse, delta, lo, kv2, kv1, kv0):
    kvspec = pl.BlockSpec((2, TOK, 128), lambda i, r: (0, 0, p))
    rowspec = pl.BlockSpec((RT, 384), lambda i, r: (r, p))
    statspec = pl.BlockSpec((8, RT), lambda i, r: (p, r))
    kvout = pl.BlockSpec((2, TOK, 128), lambda i, r: (0, 0, 0))
    acc = pltpu.VMEM((HALO + TOK, 128), F32)
    return pl.pallas_call(
        attend_back_kernel,
        grid=(1, 2),
        out_shape=(
            sds((TOK, 384), F32),
            sds((2, TOK, 128), BF16),
            sds((2, TOK, 128), BF16),
            sds((2, TOK, 128), F32),
        ),
        in_specs=[
            rowspec,
            rowspec,
            statspec,
            statspec,
            pl.BlockSpec((1, RT), lambda i, r: (0, r)),
            kvspec,
            kvspec,
            kvspec,
        ],
        out_specs=(pl.BlockSpec((RT, 384), lambda i, r: (r, 0)), kvout, kvout, kvout),
        scratch_shapes=[
            pltpu.VMEM((4, HALO + TOK, 128), BF16),
            pltpu.VMEM((4, HALO + TOK, 128), BF16),
            pltpu.VMEM((128, HALO + TOK), BF16),
            pltpu.VMEM((SPAN, RT), F32),
            pltpu.VMEM((384, RT), F32),
            acc,
            acc,
        ],
        compiler_params=params(),
        cost_estimate=cost(),
        name="attend_back",
    )(q, do, lse, delta, lo, kv2, kv1, kv0)


def out_proj_kernel(offs, att, oi, oo2, wo, part, mid_o, w, sem):
    cs = piece_copies(offs, (wo,), w, sem)
    for c in cs:
        c.start()
    a = att[...]
    mid = nt(a, oi[...]).astype(BF16)
    mid_o[...] = mid
    for c in cs:
        c.wait()
    for n in range(3):
        cols = slice(n * 512, (n + 1) * 512)
        part[:, cols] = (nt(a, w[cols, :]) + nn(mid, oo2[:, cols])).astype(BF16)


def out_proj_call(offs, att, oi, oo2, wo):
    return pl.pallas_call(
        out_proj_kernel,
        out_shape=(sds((TOK, D), BF16), sds((TOK, 128), BF16)),
        in_specs=[SM] + [VM] * 3 + [HB],
        out_specs=(VM, VM),
        scratch_shapes=[pltpu.VMEM((D, HQ), BF16), pltpu.SemaphoreType.DMA((16,))],
        compiler_params=params(),
        cost_estimate=cost(),
        name="out_proj",
    )(offs, att, oi, oo2, wo)


def ffn_in_kernel(tok, own, other, gain, a_gu, resid_o, nf_o, mid_o):
    branch = own[...].astype(F32) + other[...].astype(F32)
    x = tok[...].astype(F32) + RS * branch
    resid_o[...] = x
    inv = lax.rsqrt(jnp.mean(x * x, axis=-1, keepdims=True) + EPS)
    nf_o[...] = (x * inv * gain[...]).astype(BF16)
    mid_o[...] = nt(nf_o[...], a_gu[...]).astype(BF16)


def ffn_in_call(tok, own, other, gain, a_gu):
    return pl.pallas_call(
        ffn_in_kernel,
        grid=(4,),
        out_shape=(sds((TOK, D), F32), sds((TOK, D), BF16), sds((TOK, 128), BF16)),
        in_specs=[row_block(D)] * 3 + [all_block(1, D), all_block(128, D)],
        out_specs=(row_block(D), row_block(D), row_block(128)),
        compiler_params=params(),
        cost_estimate=cost(),
        name="ffn_norm",
    )(tok, own, other, gain, a_gu)


def cot_kernel(place, own, other, do2, og_o, fg_o, mid_o):
    @pl.when(place[3] == 1)
    def _():
        og_o[...] = own[...]

    @pl.when(place[3] == 0)
    def _():
        og_o[...] = other[...]

    fg_o[...] = (RS * og_o[...].astype(F32)).astype(BF16)
    mid_o[...] = nt(fg_o[...], do2[...]).astype(BF16)


def cot_call(place, own, other, do2):
    return pl.pallas_call(
        cot_kernel,
        out_shape=(sds((TOK, D), BF16), sds((TOK, D), BF16), sds((TOK, 128), BF16)),
        in_specs=[SM] + [VM] * 3,
        out_specs=(VM,) * 3,
        compiler_params=params(),
        cost_estimate=cost(),
        name="branch_cotangent",
    )(place, own, other, do2)


SPLIT = ((0, FA, 0, 0, FA), (1, FB, FA, 0, FB))
NCUT = ((0, 512), (512, 1024), (1024, DX))


def ffn_kernel(split, offs_a, offs_b, nf, fg, mid_gu, mid_dg, bg, bu, di, a_gu, do2, *refs):
    pa, pb = refs[:5], refs[5:10]
    part_f, part_n, rep_o, gout, uout, din = refs[10:16]
    wa, wb, xn, xf, accf, accn, sem_a, sem_b, sem = refs[16:]

    def adapter_rows(w, start, total, at):
        blk = pl.ds(start, total)
        return [
            pltpu.make_async_copy(src.at[:, blk], w.at[pl.ds(D, 128), pl.ds(k * total, total)], sem.at[at + k])
            for k, src in enumerate((bg, bu, di))
        ]

    first = piece_copies(offs_a, pa, wa, sem_a) + adapter_rows(wa, 0, FA, 0)
    inputs = [
        pltpu.make_async_copy(nf, xn.at[:, pl.ds(0, D)], sem.at[6]),
        pltpu.make_async_copy(mid_gu, xn.at[:, pl.ds(D, 128)], sem.at[7]),
        pltpu.make_async_copy(fg, xf.at[:, pl.ds(0, D)], sem.at[8]),
        pltpu.make_async_copy(mid_dg, xf.at[:, pl.ds(D, 128)], sem.at[9]),
    ]
    for c in inputs + first:
        c.start()
    for c in inputs:
        c.wait()
    mid_t = xn[:, D:DX].astype(F32).T.astype(BF16)[0:32]
    dg_t = xf[:, D:DX].astype(F32).T.astype(BF16)[0:16]
    for c in first:
        c.wait()
    second = piece_copies(offs_b, pb, wb, sem_b) + adapter_rows(wb, FA, FB, 3)
    for c in second:
        c.start()
    for w, total, start, at, n in split:
        if w == 0:
            w = wa
        else:
            w = wb
            if at == 0:
                for c in second:
                    c.wait()
        blk = slice(start, start + n)
        gc, uc, dc = (slice(k * total + at, k * total + at + n) for k in range(3))
        if n == total:
            gu = nn(xn[...], w[:, 0 : 2 * n])
            g, u = gu[:, 0:n], gu[:, n : 2 * n]
        else:
            g = nn(xn[...], w[:, gc])
            u = nn(xn[...], w[:, uc])
        hg = nn(xf[...], w[:, dc])
        sig = 1.0 / (1.0 + jnp.exp(-g))
        si = g * sig
        hid = (si * u).astype(BF16)
        gg = (hg * u * (sig * (1.0 + g * (1.0 - sig)))).astype(BF16)
        ug = (hg * si).astype(BF16)
        both = jnp.concatenate([gg, ug], axis=1)
        terms = 2.0 * nn(mid_t, both)
        gout[:, blk] = terms[0:16, 0:n].astype(BF16)
        uout[:, blk] = terms[16:32, n : 2 * n].astype(BF16)
        din[:, blk] = nn(dg_t, hid).astype(BF16)
        for c0, c1 in NCUT:
            cols = slice(c0, c1)
            f = nt(hid, w[cols, dc])
            if n == total:
                d = nt(both, w[cols, 0 : 2 * n])
            else:
                d = nt(gg, w[cols, gc]) + nt(ug, w[cols, uc])
            if start == 0:
                accf[:, cols] = f
                accn[:, cols] = d
            else:
                accf[:, cols] += f
                accn[:, cols] += d
    midd, midg = accf[:, D:DX], accn[:, D:DX]
    midd_b = midd.astype(BF16)
    midg_b = midg.astype(BF16)
    for c0 in range(0, D, 512):
        cols = slice(c0, c0 + 512)
        part_n[:, cols] = (accn[:, cols] + nn(midg_b, a_gu[:, cols])).astype(BF16)
        part_f[:, cols] = (accf[:, cols] + nn(midd_b, do2[:, cols])).astype(BF16)
    gu_in = nn(midg.T.astype(BF16)[0:32], xn[:, 0:D])
    d_out = 2.0 * nn(midd.T.astype(BF16)[0:16], xf[:, 0:D])
    for c in range(2):
        half = slice(c * 768, (c + 1) * 768)
        rep_o[c, 0:32] = gu_in[:, half].astype(BF16)
        rep_o[c, 32:48] = d_out[:, half].astype(BF16)


def ffn_call(offs_a, offs_b, nf, fg, mid_gu, mid_dg, bg, bu, di, a_gu, do2, wa, wb):
    def kernel(*refs):
        ffn_kernel(SPLIT, *refs)

    return pl.pallas_call(
        kernel,
        out_shape=(sds((TOK, D), BF16), sds((TOK, D), BF16), sds((2, 48, 768), BF16))
        + (sds((16, FH), BF16),) * 3,
        in_specs=[SM, SM] + [HB] * 7 + [VM] * 2 + [HB] * 10,
        out_specs=(VM,) * 6,
        scratch_shapes=[
            pltpu.VMEM((DX, 3 * FA), BF16),
            pltpu.VMEM((DX, 3 * FB), BF16),
            pltpu.VMEM((TOK, DX), BF16),
            pltpu.VMEM((TOK, DX), BF16),
            pltpu.VMEM((TOK, DX), F32),
            pltpu.VMEM((TOK, DX), F32),
            pltpu.SemaphoreType.DMA((16,)),
            pltpu.SemaphoreType.DMA((16,)),
            pltpu.SemaphoreType.DMA((10,)),
        ],
        compiler_params=params(),
        cost_estimate=cost(),
        name="ffn_both",
    )(offs_a, offs_b, nf, fg, mid_gu, mid_dg, bg, bu, di, a_gu, do2, *wa, *wb)


def out_back_kernel(
    offs, og, resid, own, other, gain, oi, oo2, mid_att, att, hsel, wo,
    rg_o, do_o, delta_o, rep_o, oin_o, w, abg, sem,
):
    cs = piece_copies(offs, (wo,), w, sem)
    for c in cs:
        c.start()
    for r in range(4):
        rows = pl.ds(r * 128, 128)
        x = resid[rows, :]
        inv = lax.rsqrt(jnp.mean(x * x, axis=-1, keepdims=True) + EPS)
        wv = (own[rows, :].astype(F32) + other[rows, :].astype(F32)) * gain[...]
        dot = jnp.mean(wv * x, axis=-1, keepdims=True)
        rg = og[rows, :].astype(F32) + inv * wv - x * (inv * inv * inv * dot)
        rg_o[rows, :] = rg
        abg[rows, :] = (RS * rg).astype(BF16)
    g = abg[...]
    mid_g = nt(g, oo2[...]).astype(BF16)
    for c in cs:
        c.wait()
    delta = jnp.zeros((16, TOK), F32)
    for n in range(3):
        cols = slice(n * 256, (n + 1) * 256)
        dd = (nn(g, w[:, cols]) + nn(mid_g, oi[:, cols])).astype(BF16)
        do_o[:, cols] = dd
        prod = dd.astype(F32) * att[:, cols].astype(F32)
        high = prod.astype(BF16)
        low = (prod - high.astype(F32)).astype(BF16)
        delta = delta + nt(hsel[:, cols], high) + nt(hsel[:, cols], low)
    delta_o[...] = delta
    o_out = 2.0 * nn(mid_att[...].astype(F32).T.astype(BF16)[0:16], g)
    for c in range(2):
        rep_o[c] = o_out[:, c * 768 : (c + 1) * 768].astype(BF16)
    oin_o[...] = nn(mid_g.astype(F32).T.astype(BF16)[0:16], att[...]).astype(BF16)


def out_back_call(offs, og, resid, own, other, gain, oi, oo2, mid_att, att, hsel, wo):
    return pl.pallas_call(
        out_back_kernel,
        out_shape=(
            sds((TOK, D), F32),
            sds((TOK, HQ), BF16),
            sds((16, TOK), F32),
            sds((2, 16, 768), BF16),
            sds((16, HQ), BF16),
        ),
        in_specs=[SM] + [VM] * 10 + [HB],
        out_specs=(VM,) * 5,
        scratch_shapes=[
            pltpu.VMEM((D, HQ), BF16),
            pltpu.VMEM((TOK, D), BF16),
            pltpu.SemaphoreType.DMA((16,)),
        ],
        compiler_params=params(),
        cost_estimate=cost(),
        name="out_proj_back",
    )(offs, og, resid, own, other, gain, oi, oo2, mid_att, att, hsel, wo)


def q_back_kernel(offs, dq0, dq1, cos, sin, b2, a1, mid, normed, *refs):
    pieces, (part, in_o, out_o, w, dall, sem) = refs[:5], refs[5:]
    cs = piece_copies(offs, [p.at[:, :, pl.ds(0, HQ)] for p in pieces], w, sem)
    for c in cs:
        c.start()
    cw = jnp.concatenate([cos[...], cos[...]], axis=1)
    sw = jnp.concatenate([sin[...], sin[...]], axis=1)
    dq = jnp.concatenate([dq0[...], dq1[...]], axis=1)
    for n in range(3):
        g = dq[:, n * 256 : (n + 1) * 256]
        dall[:, n * 256 : (n + 1) * 256] = (g * cw - half_swap(g) * sw).astype(BF16)
    d = dall[...]
    mid_g = nt(d, b2[:, 0:HQ]).astype(BF16)
    mid_t = mid[...].astype(F32).T.astype(BF16)
    out_o[...] = (2.0 * nn(mid_t[0:16], d)).astype(BF16)
    in_o[...] = nn(mid_g.astype(F32).T.astype(BF16)[0:16], normed[...]).astype(BF16)
    for c in cs:
        c.wait()
    for n in range(3):
        cols = slice(n * 512, (n + 1) * 512)
        part[:, cols] = nt(d, w[cols, :]) + nn(mid_g, a1[:, cols])


def q_back_call(offs, dq0, dq1, cos, sin, b2, a1, mid, normed, w):
    return pl.pallas_call(
        q_back_kernel,
        out_shape=(sds((TOK, D), F32), sds((16, D), BF16), sds((16, HQ), BF16)),
        in_specs=[SM] + [VM] * 8 + [HB] * 5,
        out_specs=(VM,) * 3,
        scratch_shapes=[
            pltpu.VMEM((D, HQ), BF16),
            pltpu.VMEM((TOK, HQ), BF16),
            pltpu.SemaphoreType.DMA((16,)),
        ],
        compiler_params=params(),
        cost_estimate=cost(),
        name="q_back",
    )(offs, dq0, dq1, cos, sin, b2, a1, mid, normed, *w)


def kv_back_kernel(offs, qpart, q_in, da0, da1, da2, db0, db1, db2, cos, sin, b2, a1, mid, normed, orep, *refs):
    pieces, (part, rep_o, out_o, w, dall, sem) = refs[:5], refs[5:]
    cs = piece_copies(offs, [p.at[:, :, pl.ds(HQ, 512)] for p in pieces], w, sem)
    for c in cs:
        c.start()
    cw = jnp.concatenate([cos[...], cos[...]], axis=1)
    sw = jnp.concatenate([sin[...], sin[...]], axis=1)
    both = []
    for i in range(2):
        own = jnp.concatenate([da0[i], db0[i]], axis=1)
        one = jnp.concatenate([da1[i], db1[i]], axis=1)
        two = jnp.concatenate([da2[i], db2[i]], axis=1)
        both.append(own + one.astype(F32) + two.astype(F32))
    dall[:, 0:256] = (both[0] * cw - half_swap(both[0]) * sw).astype(BF16)
    dall[:, 256:512] = both[1].astype(BF16)
    d = dall[...]
    mid_g = nt(d, b2[:, HQ:1280]).astype(BF16)
    mid_t = mid[...].astype(F32).T.astype(BF16)
    out_o[:, 0:256] = (2.0 * nn(mid_t[16:32], dall[:, 0:256])).astype(BF16)
    out_o[:, 256:512] = (2.0 * nn(mid_t[32:48], dall[:, 256:512])).astype(BF16)
    in_grads = nn(mid_g.astype(F32).T.astype(BF16)[16:48], normed[...]).astype(BF16)
    for c in range(2):
        cols = slice(c * 768, (c + 1) * 768)
        rep_o[c, 0:16] = q_in[:, cols]
        rep_o[c, 16:48] = in_grads[:, cols]
        rep_o[c, 48:64] = orep[c]
    for c in cs:
        c.wait()
    for n in range(3):
        cols = slice(n * 512, (n + 1) * 512)
        part[:, cols] = (qpart[:, cols] + nt(d, w[cols, :]) + nn(mid_g, a1[:, cols])).astype(BF16)


def kv_back_call(offs, qpart, q_in, da, db, cos, sin, b2, a1, mid, normed, orep, w):
    return pl.pallas_call(
        kv_back_kernel,
        out_shape=(sds((TOK, D), BF16), sds((2, 64, 768), BF16), sds((16, 512), BF16)),
        in_specs=[SM] + [VM] * 15 + [HB] * 5,
        out_specs=(VM,) * 3,
        scratch_shapes=[
            pltpu.VMEM((D, 512), BF16),
            pltpu.VMEM((TOK, 512), BF16),
            pltpu.SemaphoreType.DMA((16,)),
        ],
        compiler_params=params(),
        cost_estimate=cost(),
        name="kv_back",
    )(offs, qpart, q_in, *da, *db, cos, sin, b2, a1, mid, normed, orep, *w)


def token_grad_kernel(tok, rg, own, other, gain, out):
    x = tok[...].astype(F32)
    inv = lax.rsqrt(jnp.mean(x * x, axis=-1, keepdims=True) + EPS)
    wv = (own[...].astype(F32) + other[...].astype(F32)) * gain[...]
    dot = jnp.mean(wv * x, axis=-1, keepdims=True)
    out[...] = (rg[...] + inv * wv - x * (inv * inv * inv * dot)).astype(BF16)


def token_grad_call(tok, rg, own, other, gain):
    return pl.pallas_call(
        token_grad_kernel,
        grid=(4,),
        out_shape=sds((TOK, D), BF16),
        in_specs=[row_block(D)] * 4 + [all_block(1, D)],
        out_specs=row_block(D),
        compiler_params=params(),
        cost_estimate=cost(),
        name="token_grad",
    )(tok, rg, own, other, gain)


def pack_first_kernel(q, k, v, out):
    out[:, 0:768] = q[...]
    out[:, 768:1024] = k[...]
    out[:, 1024:1280] = v[...]


def pack_first_call(q, k, v):
    return pl.pallas_call(
        pack_first_kernel,
        out_shape=sds((96, 1280), BF16),
        in_specs=[VM] * 3,
        out_specs=VM,
        compiler_params=params(),
        cost_estimate=cost(),
        name="pack_qkv",
    )(q, k, v)


def pack_rest_kernel(o, g, u, d, yx, xy):
    yx[:, 0:HQ] = o[...]
    for i, w in enumerate((g, u, d)):
        yx[:, HQ + i * FA : HQ + (i + 1) * FA] = w[:, 0:FA]
        xy[:, i * FB : (i + 1) * FB] = w[:, FA:FH]


def pack_rest_call(o, g, u, d):
    return pl.pallas_call(
        pack_rest_kernel,
        out_shape=(
            sds((96, HQ + 3 * FA), BF16),
            sds((96, 3 * FB), BF16),
        ),
        in_specs=[VM] * 4,
        out_specs=(VM,) * 2,
        compiler_params=params(),
        cost_estimate=cost(),
        name="pack_rest",
    )(o, g, u, d)


def line_call(parts, head):
    n = parts[0].shape[1] - head

    def kernel(*refs):
        ins, outs = refs[:4], refs[4:]
        for i in range(4):
            if head:
                outs[0][i] = ins[i][:, 0:head]
            outs[-1][i] = ins[i][:, head:]

    shapes = (sds((4, 96, head), BF16),) * bool(head) + (sds((4, 96, n), BF16),)
    return pl.pallas_call(
        kernel,
        out_shape=shapes,
        in_specs=[VM] * 4,
        out_specs=(VM,) * len(shapes),
        compiler_params=params(),
        cost_estimate=cost(),
        name="line",
    )(*parts)


def own_half_kernel(idx, q, k, v, o, g, u, d, out):
    at = 0
    for ref in (q, k, v, o, g, u, d):
        n = ref.shape[2]
        out[:, at : at + n] = ref[0]
        at += n


def own_half_call(index, arrays):
    return pl.pallas_call(
        own_half_kernel,
        out_shape=sds((16, 7808), BF16),
        grid_spec=pltpu.PrefetchScalarGridSpec(
            num_scalar_prefetch=1,
            grid=(1,),
            in_specs=[
                pl.BlockSpec((1, 16, a.shape[2]), lambda i, idx: (idx[0], 0, 0)) for a in arrays
            ],
            out_specs=pl.BlockSpec((16, 7808), lambda i, idx: (0, 0)),
        ),
        compiler_params=params(),
        cost_estimate=cost(),
        name="pick_halves",
    )(index, *arrays)


def factors_kernel(
    idx, halves, aq, ak, av, ag, au, oo, do, a_qkv, b_qkv, a_gu, bg, bu, di, oi, oo2, do2
):
    for ref in (a_qkv, b_qkv, a_gu, bg, bu, di, oi, oo2, do2):
        ref[...] = jnp.zeros_like(ref)
    for i, ref in enumerate((aq, ak, av)):
        a_qkv[i * 16 : (i + 1) * 16] = ref[0]
    for i, ref in enumerate((ag, au)):
        a_gu[i * 16 : (i + 1) * 16] = ref[0]
    oo2[0:16] = 2 * oo[0]
    do2[0:16] = 2 * do[0]
    b_qkv[0:16, 0:768] = 2 * halves[:, 0:768]
    b_qkv[16:32, 768:1024] = 2 * halves[:, 768:1024]
    b_qkv[32:48, 1024:1280] = 2 * halves[:, 1024:1280]
    oi[0:16] = halves[:, 1280:2048]
    bg[0:16] = 2 * halves[:, 2048:3968]
    bu[16:32] = 2 * halves[:, 3968:5888]
    di[0:16] = halves[:, 5888:7808]


def factors_call(index, halves, arrays):
    widths = (D, 1280, D, FH, FH, FH, HQ, D, D)
    return pl.pallas_call(
        factors_kernel,
        out_shape=tuple(sds((128, w), BF16) for w in widths),
        grid_spec=pltpu.PrefetchScalarGridSpec(
            num_scalar_prefetch=1,
            grid=(1,),
            in_specs=[pl.BlockSpec((16, 7808), lambda i, idx: (0, 0))]
            + [pl.BlockSpec((1, 16, D), lambda i, idx: (idx[0], 0, 0))] * 7,
            out_specs=tuple(pl.BlockSpec((128, w), lambda i, idx: (0, 0)) for w in widths),
        ),
        compiler_params=params(),
        cost_estimate=cost(),
        name="factors",
    )(index, halves, *arrays)


def quarters_kernel(m, place, rep, got, *refs):
    parts, outs, buf = refs[:-5], refs[-5:-1], refs[-1]
    core, z = place[0], place[1]
    n_rep = rep.shape[1] // 16
    kept = (rep[core].astype(F32) + got[...].astype(F32)).astype(BF16)
    for i in range(n_rep):
        buf[:, i * 768 : (i + 1) * 768] = kept[i * 16 : (i + 1) * 16]
    at = n_rep * 768
    for p in parts:
        buf[:, at : at + p.shape[1]] = p[...]
        at += p.shape[1]
    if at < 4 * m:
        buf[:, at : 4 * m] = jnp.zeros((16, 4 * m - at), BF16)
    for k, out in enumerate(outs):
        quarter = lax.rem(z + k, 4)
        out[...] = buf[:, pl.ds(pl.multiple_of(quarter * m, 128), m)]


def quarters_call(m, place, rep, got, parts):
    def kernel(*refs):
        quarters_kernel(m, *refs)

    return pl.pallas_call(
        kernel,
        out_shape=(sds((16, m), BF16),) * 4,
        in_specs=[SM] + [VM] * (2 + len(parts)),
        out_specs=(VM,) * 4,
        scratch_shapes=[pltpu.VMEM((16, 4 * m), BF16)],
        compiler_params=params(),
        cost_estimate=cost(),
        name="quarters",
    )(place, rep, got, *parts)


def pack_early_kernel(place, rep, got, g, u, d, out):
    kept = (rep[place[0]].astype(F32) + got[...].astype(F32)).astype(BF16)
    for i in range(3):
        out[:, i * 768 : (i + 1) * 768] = kept[i * 16 : (i + 1) * 16]
    for i, ref in enumerate((g, u, d)):
        out[:, 2304 + i * FH : 2304 + (i + 1) * FH] = ref[...]
    out[:, 8064:8192] = jnp.zeros((16, 128), BF16)


def pack_early_call(place, rep, got, g, u, d):
    return pl.pallas_call(
        pack_early_kernel,
        out_shape=sds((16, 4 * EARLY), BF16),
        in_specs=[SM] + [VM] * 5,
        out_specs=VM,
        compiler_params=params(),
        cost_estimate=cost(),
        name="pack_early",
    )(place, rep, got, g, u, d)


def quarter_kernel(place, total, out):
    at = pl.multiple_of(place[1] * EARLY, 128)
    out[:, 0:EARLY] = total[:, pl.ds(at, EARLY)]
    out[:, EARLY : EARLY + 128] = (
        jnp.full((16, 128), place[2], jnp.int32).astype(F32).astype(BF16)
    )


def quarter_call(place, total):
    return pl.pallas_call(
        quarter_kernel,
        out_shape=sds((16, EARLY + 128), BF16),
        in_specs=[SM, VM],
        out_specs=VM,
        compiler_params=params(),
        cost_estimate=cost(),
        name="quarter",
    )(place, total)


def sum_kernel(place, a, b, c, d, out):
    m = a.shape[1]
    total = a[...].astype(F32) + b[...].astype(F32) + c[...].astype(F32) + d[...].astype(F32)
    out[:, 0:m] = total.astype(BF16)
    out[:, m : m + 128] = jnp.full((16, 128), place[2], jnp.int32).astype(F32).astype(BF16)


def sum_call(place, parts):
    m = parts[0].shape[1]
    return pl.pallas_call(
        sum_kernel,
        out_shape=sds((16, m + 128), BF16),
        in_specs=[SM] + [VM] * 4,
        out_specs=VM,
        compiler_params=params(),
        cost_estimate=cost(),
        name="sum_tokens",
    )(place, *parts)


def by_adapter_kernel(*refs):
    ins, out = refs[:-1], refs[-1]
    m = out.shape[2]
    rows = [(r, k) for r in ins for k in range(r.shape[0])]
    for a in range(8):
        total = jnp.zeros((16, m), F32)
        for r, k in rows:
            hit = r[k, :, m : m + 1].astype(F32) == float(a)
            total = total + jnp.where(hit, r[k, :, 0:m].astype(F32), 0.0)
        out[a] = total.astype(BF16)


def by_adapter_call(parts, m):
    return pl.pallas_call(
        by_adapter_kernel,
        out_shape=sds((8, 16, m), BF16),
        in_specs=[VM] * len(parts),
        out_specs=VM,
        compiler_params=params(),
        cost_estimate=cost(),
        name="by_adapter",
    )(*parts)


def spread(buf, outs, jobs, widths):
    at = 0
    for out, n in zip(outs, widths, strict=True):
        for c in range(2):
            out[:, :, c * n : (c + 1) * n] = buf[c, :, :, at : at + n].astype(F32)
        at += n


def unpack_early_kernel(src, *refs):
    outs, buf, sem = refs[:-2], refs[-2], refs[-1]
    copies = []
    for z in range(4):
        for c in range(2):
            copies.append(
                pltpu.make_async_copy(
                    src.at[2 * z + c], buf.at[c, :, :, pl.ds(z * EARLY, EARLY)], sem.at[2 * z + c]
                )
            )
    for c in copies:
        c.start()
    for c in copies:
        c.wait()
    spread(buf, outs, None, (768, 768, 768, FH, FH, FH))


def unpack_early_call(src):
    widths = (D, D, D, 2 * FH, 2 * FH, 2 * FH)
    return pl.pallas_call(
        unpack_early_kernel,
        out_shape=tuple(sds((8, 16, w), F32) for w in widths),
        in_specs=[HB],
        out_specs=(VM,) * 6,
        scratch_shapes=[pltpu.VMEM((2, 8, 16, 4 * EARLY), BF16), pltpu.SemaphoreType.DMA((8,))],
        compiler_params=params(),
        cost_estimate=cost(),
        name="unpack_early",
    )(src)


def unpack_late_kernel(place, *refs):
    srcs, outs, buf, sem = refs[:8], refs[8:-2], refs[-2], refs[-1]
    core, z = place[0], place[1]
    copies = []
    for i, src in enumerate(srcs):
        c = core if i < 4 else 1 - core
        at = lax.rem(z + REL[i % 4] + 4, 4) * LATE
        copies.append(
            pltpu.make_async_copy(
                src, buf.at[c, :, :, pl.ds(pl.multiple_of(at, 128), LATE)], sem.at[i]
            )
        )
    for c in copies:
        c.start()
    for c in copies:
        c.wait()
    spread(buf, outs, None, (768, 768, 768, 768, 768, 256, 256, 768))


def unpack_late_call(place, srcs):
    widths = (D, D, D, D, D, 512, 512, D)
    return pl.pallas_call(
        unpack_late_kernel,
        out_shape=tuple(sds((8, 16, w), F32) for w in widths),
        in_specs=[SM] + [HB] * 8,
        out_specs=(VM,) * 8,
        scratch_shapes=[pltpu.VMEM((2, 8, 16, 4 * LATE), BF16), pltpu.SemaphoreType.DMA((8,))],
        compiler_params=params(),
        cost_estimate=cost(),
        name="unpack_late",
    )(place, *srcs)


YLIN = (0, 2, 1, 3)


def go_x(v, step):
    return lax.ppermute(v, "x", [(i, (i + step) % 4) for i in range(4)])


def go_y(v, step):
    return lax.ppermute(
        v, ("tensor", "yh"), [(YLIN[i], YLIN[(i + step) % 4]) for i in range(4)]
    )


def go_z(v, step):
    return lax.ppermute(v, "seq", [(i, (i + step) % 4) for i in range(4)])


def go_core(v):
    return lax.ppermute(v, "core", [(0, 1), (1, 0)])


def to_role(v):
    return lax.ppermute(v, ("tensor", "core"), [(1, 2), (2, 1)])


REL = (0, -1, 1, 2)


def near_line(shard, near):
    return (shard, near(shard, 1), near(shard, -1), near(shard, 2))


def ring_start(line, far):
    return (line, far(line, 1), far(line, -1))


def ring_halves(below, above):
    return below[:2], above[2:]


class Order:
    def __init__(self):
        self.last = ()

    def gate(self, v):
        return lax.optimization_barrier((v, self.last))[0]

    def done(self, v):
        v = self.gate(v)
        self.last = jax.tree.leaves(v)
        return v

    def run(self, step, *args):
        out = step(*self.gate(args))
        self.last = jax.tree.leaves(out)
        return out


def offsets(x, y, path):
    near = np.tile(np.array(REL, np.int32), 4)
    far = np.repeat(np.array(REL, np.int32), 4)
    if path == "yx":
        return ((x + far + 4) % 4) * 4 + (y + near + 4) % 4
    if path == "xy":
        return np.tile(np.arange(4, dtype=np.int32), 4) * 4 + (y + far + 4) % 4
    return np.repeat(np.arange(4, dtype=np.int32), 4) * 4 + (y + near + 4) % 4


def halo_back(grads):
    two, one, own = grads
    one = lax.ppermute(one, "seq", [(1, 0), (2, 1), (3, 2)])
    return (own, one, lax.ppermute(two, "seq", [(2, 0), (3, 1)]))


def shards(
    tokens,
    output_gradient,
    document_length_table,
    sequence_adapter_index,
    sequence_window_length,
    attention_norm_gain,
    feedforward_norm_gain,
    query_projection_weight,
    key_projection_weight,
    value_projection_weight,
    output_projection_weight,
    gate_projection_weight,
    up_projection_weight,
    down_projection_weight,
    query_adapter_first,
    query_adapter_second,
    key_adapter_first,
    key_adapter_second,
    value_adapter_first,
    value_adapter_second,
    output_adapter_first,
    output_adapter_second,
    gate_adapter_first,
    gate_adapter_second,
    up_adapter_first,
    up_adapter_second,
    down_adapter_first,
    down_adapter_second,
):
    z = lax.axis_index("seq")
    yl = lax.axis_index("tensor")
    x = lax.axis_index("x")
    y = lax.axis_index("yh") * 2 + yl
    core = lax.axis_index("core")
    same = core == yl

    o = Order()
    t = lambda v: v.swapaxes(1, 2)
    mine = lambda own, got: jnp.where(same, own, got)
    offs_yx, offs_xy, offs_o = (offsets(x, y, p) for p in ("yx", "xy", "o"))
    gain1 = attention_norm_gain[None, :]
    gain2 = feedforward_norm_gain[None, :]

    own_qkv = o.run(
        pack_first_call, query_projection_weight, key_projection_weight, value_projection_weight
    )
    got_qkv = to_role(own_qkv)
    own_yx, own_b = o.run(
        pack_rest_call,
        output_projection_weight,
        gate_projection_weight,
        up_projection_weight,
        down_projection_weight,
    )
    got_b = to_role(own_b)
    meta = jnp.concatenate(
        [document_length_table[0], sequence_adapter_index, sequence_window_length]
    )
    meta_other = go_core(meta)
    near_qkv = near_line(o.run(mine, own_qkv, o.done(got_qkv)), go_y)
    own_halves = o.run(
        own_half_call,
        sequence_adapter_index,
        (
            query_adapter_second,
            key_adapter_second,
            value_adapter_second,
            output_adapter_first,
            gate_adapter_second,
            up_adapter_second,
            down_adapter_first,
        ),
    )
    own_b = o.run(mine, own_b, o.done(got_b))
    line_qkv = o.run(lambda *v: line_call(v, 0)[0], *o.done(near_qkv))
    below_qkv, above_qkv = go_x(line_qkv, 1), go_x(line_qkv, -1)
    tok_other = go_core(o.gate(tokens[0]))

    def tables(own, other):
        meta = mine(own, other)
        lengths, index, window = meta[:4], meta[4:5], meta[5]
        place = jnp.concatenate(
            [jnp.stack([core, z]), index, same[None]], dtype=jnp.int32
        )
        ends = jnp.cumsum(lengths, dtype=jnp.int32)
        begins = ends - lengths
        row = z * TOK + jnp.arange(TOK, dtype=jnp.int32)
        begin = jnp.max(jnp.where(row[:, None] >= begins[None, :], begins[None, :], 0), axis=1)
        low_key = (jnp.maximum(begin, row - window + 1) - (z * TOK - HALO))[None, :]
        lane = jnp.arange(128, dtype=jnp.int32) % HDIM
        frequency = ROPE_BASE ** (-((lane % 32).astype(F32) * (2.0 / HDIM)))
        angles = (row - begin).astype(F32)[:, None] * frequency[None, :]
        cos = jnp.cos(angles)
        sin = jnp.sin(angles) * jnp.where(lane < 32, -1.0, 1.0)[None, :]
        return index, place, low_key, cos, sin

    index, place, low_key, cos, sin = o.run(tables, meta, o.done(meta_other))
    got_halves, got_yx = to_role(o.gate(own_halves)), to_role(o.gate(own_yx))
    tok = o.run(mine, tokens[0], o.done(tok_other))
    halves = o.run(mine, own_halves, o.done(got_halves))
    a_qkv, b_qkv, a_gu, bg2, bu2, di_p, oi_p, oo2, do2 = o.run(
        factors_call,
        index,
        halves,
        (
            t(query_adapter_first),
            t(key_adapter_first),
            t(value_adapter_first),
            t(gate_adapter_first),
            t(up_adapter_first),
            output_adapter_second,
            down_adapter_second,
        ),
    )
    near_yx = near_line(o.run(mine, own_yx, o.done(got_yx)), go_y)
    low, high = o.run(ring_halves, *o.done((below_qkv, above_qkv)))
    far_qkv = (go_x(low, 1), go_x(high, -1))
    line_b = lax.all_gather(o.gate(own_b), "x", axis=0)
    full_qkv = (line_qkv, below_qkv, above_qkv) + o.done(far_qkv)

    normed, q, kv0, mid_qkv = o.run(
        qkv_call, offs_yx, tok, gain1, a_qkv, b_qkv, cos, sin, full_qkv
    )
    kv1 = lax.ppermute(kv0, "seq", [(0, 1), (1, 2), (2, 3)])
    kv2 = lax.ppermute(kv0, "seq", [(0, 2), (1, 3)])
    line_o, line_a = o.run(lambda *v: line_call(v, HQ), *o.done(near_yx))
    full_o = lax.all_gather(line_o, "x", axis=0, tiled=True)
    line_b = o.done(line_b)
    below_b, above_b = go_y(line_b, 1), go_y(line_b, -1)
    kv1, kv2 = o.done((kv1, kv2))
    line_a = o.gate(line_a)
    below_a, above_a = go_x(line_a, 1), go_x(line_a, -1)
    att, lse = o.run(attend_call, q, low_key, kv2, kv1, kv0)
    low, high = o.run(ring_halves, *o.done((below_b, above_b)))
    far_b = (go_y(low, 1), go_y(high, -1))
    full_o = o.done(full_o)
    attn_part, mid_att = o.run(out_proj_call, offs_o, att, oi_p, oo2, full_o)
    attn_other = go_core(attn_part)
    og_other = go_core(o.gate(output_gradient[0]))
    low, high = o.run(ring_halves, *o.done((below_a, above_a)))
    far_a = (go_x(low, 1), go_x(high, -1))
    resid, nf, mid_gu = o.run(ffn_in_call, tok, attn_part, o.done(attn_other), gain2, a_gu)
    og, fg, mid_dg = o.run(cot_call, place, output_gradient[0], o.done(og_other), do2)
    full_b = (line_b, below_b, above_b) + o.done(far_b)
    full_a = (line_a, below_a, above_a) + o.done(far_a)
    ffn_part, nfg_part, rep_e, g_out, u_out, d_in = o.run(
        ffn_call,
        offs_yx, offs_xy, nf, fg, mid_gu, mid_dg, bg2, bu2, di_p, a_gu, do2, full_a, full_b,
    )

    def exchange(rep):
        return go_core(lax.dynamic_index_in_dim(rep, 1 - core, 0, keepdims=False))

    nfg_other = go_core(nfg_part)
    got_e = exchange(rep_e)
    quarters = o.run(
        lambda *v: quarters_call(EARLY, place, v[0], v[1], v[2:]),
        rep_e, o.done(got_e), g_out, u_out, d_in,
    )
    sent = [go_z(quarters[k], k) for k in (1, 2, 3)]
    head = np.arange(16)
    head = np.where(head % 8 < 6, 6 * (head // 8) + head % 8, -1)
    hsel = jnp.asarray((np.arange(HQ) // HDIM)[None, :] == head[:, None], BF16)
    rg, do, delta, rep_o, o_in = o.run(
        out_back_call,
        offs_o, og, resid, nfg_part, o.done(nfg_other), gain2, oi_p, oo2, mid_att, att, hsel, full_o,
    )
    near = near_line(o.run(sum_call, place, [quarters[0]] + o.done(sent)), go_y)
    stats = (lse, delta, low_key, kv2, kv1, kv0)
    dqa, *da = o.run(lambda *v: attend_back_call(0, *v), q, do, *stats)
    plane = lax.all_gather(o.run(lambda *v: jnp.stack(v), *o.done(near)), "x", axis=0, tiled=True)
    ra = halo_back(da)
    ffn_other = go_core(o.gate(ffn_part))
    dqb, *db = o.run(lambda *v: attend_back_call(1, *v), q, do, *stats)
    ra = o.done(ra)
    rb = halo_back(db)
    qpart, q_in, q_out = o.run(
        q_back_call, offs_yx, dqa, dqb, cos, sin, b_qkv, a_qkv, mid_qkv, normed, full_qkv
    )
    out = o.run(
        lambda r, a, b: (r + RS * (a.astype(F32) + b.astype(F32))).astype(BF16),
        resid, ffn_part, o.done(ffn_other),
    )
    out_other = to_role(out)
    dense = o.run(lambda v: by_adapter_call([v], EARLY), o.done(plane))
    early = lax.all_gather(dense, ("seq", "core"), axis=0)
    rb = o.done(rb)
    na_part, rep_l, kv_out = o.run(
        kv_back_call,
        offs_yx, qpart, q_in, ra, rb, cos, sin, b_qkv, a_qkv, mid_qkv, normed, rep_o, full_qkv,
    )
    na_other = go_core(na_part)
    got_l = exchange(rep_l)

    quarters = o.run(
        lambda *v: quarters_call(LATE, place, v[0], v[1], v[2:]),
        rep_l, o.done(got_l), q_out, kv_out, o_in,
    )
    sent = [go_z(quarters[k], k) for k in (1, 2, 3)]
    near = near_line(o.run(sum_call, place, [quarters[0]] + o.done(sent)), go_y)
    na_other = o.done(na_other)
    line = o.run(lambda *v: jnp.stack(v), *o.done(near))
    output = o.run(mine, out, o.done(out_other))
    lines = [go_x(line, 1), go_x(line, -1), go_x(line, 2)]
    token_grad = o.run(token_grad_call, tok, rg, na_part, na_other, gain1)
    tg_other = to_role(token_grad)
    dense = o.run(lambda *v: by_adapter_call(v, LATE), line, *o.done(lines))
    zs = [go_z(dense, 1), go_z(dense, -1), go_z(dense, 2)]
    cores = [go_core(dense)]
    g_in, u_in, d_out, g_out, u_out, d_in = o.run(unpack_early_call, o.done(early))
    zs = o.done(zs)
    cores += [go_core(v) for v in zs]
    token_grad = o.run(mine, token_grad, o.done(tg_other))
    q_in, k_in, v_in, o_out, q_out, k_out, v_out, o_in = o.run(
        unpack_late_call, place, [dense] + zs + o.done(cores)
    )
    return (
        output[None],
        token_grad[None],
        t(q_in),
        q_out,
        t(k_in),
        k_out,
        t(v_in),
        v_out,
        o_in,
        o_out,
        t(g_in),
        g_out,
        t(u_in),
        u_out,
        d_in,
        d_out,
    )


def solution(mesh):
    fine = Mesh(mesh.devices.reshape(4, 2, 4, 2, 2), ("seq", "tensor", "x", "yh", "core"))
    fsdp = ("x", "yh", "core")
    weight = P(fsdp, "tensor")
    half = P(None, None, "tensor")
    return jax.shard_map(
        shards,
        mesh=fine,
        in_specs=(
            P(fsdp, "seq", None),
            P(fsdp, "seq", None),
            P(fsdp, None),
            P(fsdp),
            P(fsdp),
            P(),
            P(),
        )
        + (weight,) * 7
        + (P(), half, P(), half, P(), half, half, P(), P(), half, P(), half, half, P()),
        out_specs=(P(fsdp, "seq", None), P(fsdp, "seq", None)) + (P(),) * 14,
        check_vma=False,
    )
```

```python
import jax
import jax.numpy as jnp
import numpy as np
from jax import lax
from jax.experimental import pallas as pl
from jax.experimental.pallas import tpu as pltpu
from jax.sharding import Mesh
from jax.sharding import PartitionSpec as P

F32 = jnp.float32
BF16 = jnp.bfloat16
EPS = 1e-05
ROPE_BASE = 10000.0
RS = 1.4 / 52.0**0.5
MASKED = -1e30
TOK = 512
D = 1536
DX = D + 128
HQ = 768
HK = 256
HDIM = 64
SPAN = 1280
RT = 256
HALO = 1024
FH = 1920
FA, FB = 768, 1152
EARLY = 2048
LATE = 1280


def nn(a, b):
    return lax.dot_general(a, b, (((1,), (0,)), ((), ())), preferred_element_type=F32)


def nt(a, b):
    return lax.dot_general(a, b, (((1,), (1,)), ((), ())), preferred_element_type=F32)


def tn(a, b):
    return lax.dot_general(a, b, (((0,), (0,)), ((), ())), preferred_element_type=F32)


VM = pl.BlockSpec(memory_space=pltpu.VMEM)
SM = pl.BlockSpec(memory_space=pltpu.SMEM)
HB = pl.BlockSpec(memory_space=pl.ANY)


def row_block(width):
    return pl.BlockSpec((128, width), lambda i: (i, 0))


def all_block(rows, width):
    return pl.BlockSpec((rows, width), lambda i: (0, 0))


def params(mib=58):
    return pltpu.CompilerParams(vmem_limit_bytes=mib * 1024 * 1024)


def cost():
    return pl.CostEstimate(flops=1, bytes_accessed=1, transcendentals=0)


def sds(shape, dtype):
    return jax.ShapeDtypeStruct(shape, dtype)


def piece_copies(offs, refs, dst, sems):
    copies = []
    for ref in refs:
        for k in range(ref.shape[0]):
            row = pl.multiple_of(offs[len(copies)] * 96, 96)
            copies.append(
                pltpu.make_async_copy(ref.at[k], dst.at[pl.ds(row, 96)], sems.at[len(copies)])
            )
    return copies


def half_swap(v):
    lane = lax.broadcasted_iota(jnp.int32, v.shape, 1)
    width = v.shape[1]
    from_low = pltpu.roll(v, 32, 1)
    from_high = pltpu.roll(v, width - 32, 1)
    return jnp.where((lane % 64) < 32, from_high, from_low)


def qkv_kernel(offs, tok, gain, a1, b2, cos, sin, *refs):
    pieces, (normed_o, q_o, kv_o, mid_o, w, sem) = refs[:5], refs[5:]
    cs = piece_copies(offs, pieces, w, sem)
    for c in cs:
        c.start()
    for r in range(4):
        rows = pl.ds(r * 128, 128)
        x = tok[rows, :].astype(F32)
        inv = lax.rsqrt(jnp.mean(x * x, axis=-1, keepdims=True) + EPS)
        normed_o[rows, :] = (x * inv * gain[...]).astype(BF16)
    normed = normed_o[...]
    mid = nt(normed, a1[...]).astype(BF16)
    mid_o[...] = mid
    for c in cs:
        c.wait()
    cw = jnp.concatenate([cos[...], cos[...]], axis=1)
    sw = jnp.concatenate([sin[...], sin[...]], axis=1)
    for n in (3, 4, 0, 1, 2):
        cols = slice(n * 256, (n + 1) * 256)
        acc = nn(normed, w[:, cols]) + nn(mid, b2[:, cols])
        if n < 4:
            acc = acc * cw + half_swap(acc) * sw
        if n < 3:
            q_o[:, cols] = (acc.astype(BF16).astype(F32) * 0.125).astype(BF16)
        else:
            kv_o[n - 3] = acc.astype(BF16)


def qkv_call(offs, tok, gain, a1, b2, cos, sin, w):
    return pl.pallas_call(
        qkv_kernel,
        out_shape=(
            sds((TOK, D), BF16),
            sds((TOK, HQ), BF16),
            sds((2, TOK, HK), BF16),
            sds((TOK, 128), BF16),
        ),
        in_specs=[SM] + [VM] * 6 + [HB] * 5,
        out_specs=(VM,) * 4,
        scratch_shapes=[pltpu.VMEM((D, 1280), BF16), pltpu.SemaphoreType.DMA((16,))],
        compiler_params=params(),
        cost_estimate=cost(),
        name="norm_qkv",
    )(offs, tok, gain, a1, b2, cos, sin, *w)


HEADS_OF_PAIR = ((0, 0, 0), (0, 1, 0), (1, 0, 0), (1, 1, 1), (2, 0, 1), (2, 1, 1))


def bias_of(lo, r):
    key = lax.broadcasted_iota(jnp.int32, (SPAN, RT), 0) + r * RT
    row = lax.broadcasted_iota(jnp.int32, (SPAN, RT), 1) + r * RT + HALO
    return jnp.where((key >= lo) & (key <= row), 0.0, MASKED)


def variants(dst, src, other=0.0):
    lane = lax.broadcasted_iota(jnp.int32, src.shape, 1)
    srcf = src.astype(F32)
    rolled = pltpu.roll(srcf, 64, 1)
    low = lane < 64
    dst[0] = jnp.where(low, srcf, other).astype(BF16)
    dst[1] = jnp.where(low, other, rolled).astype(BF16)
    dst[2] = jnp.where(low, rolled, other).astype(BF16)
    dst[3] = jnp.where(low, other, srcf).astype(BF16)


def in_half(v, half, want):
    return v if half == want else pltpu.roll(v, 64, 1)


def attend_kernel(q, lo, kv2, kv1, kv0, out, lse, kvar, vvar, bias):
    r = pl.program_id(1)
    lane = lax.broadcasted_iota(jnp.int32, (RT, 128), 1)
    low = lane < 64

    @pl.when(r == 0)
    def _():
        variants(kvar, jnp.concatenate([kv2[0], kv1[0], kv0[0]], axis=0))
        variants(vvar, jnp.concatenate([kv2[1], kv1[1], kv0[1]], axis=0), 1.0)

    key = lax.broadcasted_iota(jnp.int32, (RT, SPAN), 1) + r * RT
    row = lax.broadcasted_iota(jnp.int32, (RT, SPAN), 0) + r * RT + HALO
    bias[...] = jnp.where((key >= lo[...]) & (key <= row), 0.0, MASKED)
    keys = pl.ds(pl.multiple_of(r * RT, RT), SPAN)
    stats = jnp.zeros((RT, 128), F32)
    for tile in range(3):
        qt = q[:, tile * 128 : (tile + 1) * 128]
        pair = []
        for i in (2 * tile, 2 * tile + 1):
            _, half, kv = HEADS_OF_PAIR[i]
            s = nt(qt, kvar[2 * kv + half, keys, :]) + bias[...]
            m = jnp.max(s, axis=1, keepdims=True)
            e = jnp.exp(s - m).astype(BF16)
            o = nn(e, vvar[2 * kv + half, keys, :])
            total = o[:, 64:65] if half == 0 else o[:, 0:1]
            stats = jnp.where(lane == i, m + jnp.log(total), stats)
            pair.append(o)
        total = pltpu.roll(jnp.where(low, pair[1], pair[0]), 64, 1)
        out[:, tile * 128 : (tile + 1) * 128] = (jnp.where(low, pair[0], pair[1]) / total).astype(BF16)
    lse[...] = stats.T[0:8]


def attend_call(q, lo, kv2, kv1, kv0):
    kvspec = pl.BlockSpec((2, TOK, 128), lambda p, r: (0, 0, p))
    return pl.pallas_call(
        attend_kernel,
        grid=(2, 2),
        out_shape=(sds((TOK, HQ), BF16), sds((16, TOK), F32)),
        in_specs=[
            pl.BlockSpec((RT, 384), lambda p, r: (r, p)),
            pl.BlockSpec((RT, 1), lambda p, r: (r, 0)),
            kvspec,
            kvspec,
            kvspec,
        ],
        out_specs=(
            pl.BlockSpec((RT, 384), lambda p, r: (r, p)),
            pl.BlockSpec((8, RT), lambda p, r: (p, r)),
        ),
        scratch_shapes=[
            pltpu.VMEM((4, HALO + TOK, 128), BF16),
            pltpu.VMEM((4, HALO + TOK, 128), BF16),
            pltpu.VMEM((RT, SPAN), F32),
        ],
        compiler_params=params(),
        cost_estimate=cost(),
        name="attend",
    )(q, lo.T, kv2, kv1, kv0)


def attend_back_kernel(
    q, do, lse, delta, lo, kv2, kv1, kv0, dq, d2, d1, d0, kvar, vvar, kt, bias, dqt, dk_acc, dv_acc
):
    r = pl.program_id(1)

    @pl.when(r == 0)
    def _():
        kcat = jnp.concatenate([kv2[0], kv1[0], kv0[0]], axis=0)
        variants(kvar, kcat)
        kt[...] = kcat.astype(F32).T.astype(BF16)
        vcat = jnp.concatenate([kv2[1], kv1[1], kv0[1]], axis=0)
        variants(vvar, vcat)
        for ref in (dk_acc, dv_acc):
            ref[...] = jnp.zeros_like(ref)

    bias[...] = bias_of(lo[...], r)
    keys = pl.ds(pl.multiple_of(r * RT, RT), SPAN)
    low = lax.broadcasted_iota(jnp.int32, (RT, 128), 1) < 64
    for u in range(2):
        ps, dss, qs, dos = [], [], [], []
        for i in range(3 * u, 3 * u + 3):
            cols = slice((i // 2) * 128, (i // 2 + 1) * 128)
            half = i % 2
            qt = q[:, cols]
            dt = do[:, cols]
            keep = low if u == 0 else ~low
            qs.append(jnp.where(keep, in_half(qt.astype(F32), half, u), 0.0).astype(BF16))
            dos.append(jnp.where(keep, in_half(dt.astype(F32), half, u), 0.0).astype(BF16))
            s = nt(kvar[2 * u + half, keys, :], qt) + bias[...]
            p = jnp.exp(s - lse[i : i + 1, :])
            dp = nt(vvar[2 * u + half, keys, :], dt)
            dss.append((p * (dp - delta[i : i + 1, :])).astype(BF16))
            ps.append(p.astype(BF16))
        ds = jnp.concatenate(dss, axis=1)
        dv_acc[keys, :] += nn(jnp.concatenate(ps, axis=1), jnp.concatenate(dos, axis=0))
        dk_acc[keys, :] += nn(ds, jnp.concatenate(qs, axis=0))
        dqu = nn(kt[u * 64 : (u + 1) * 64, keys], ds)
        for g in range(3):
            i = 3 * u + g
            dqt[i * 64 : (i + 1) * 64, :] = dqu[:, g * RT : (g + 1) * RT]
    dq[...] = dqt[...].T * 0.125

    @pl.when(r == 1)
    def _():
        dk, dv = dk_acc[...], dv_acc[...]
        d2[0] = dk[0:512].astype(BF16)
        d2[1] = dv[0:512].astype(BF16)
        d1[0] = dk[512:1024].astype(BF16)
        d1[1] = dv[512:1024].astype(BF16)
        d0[0] = dk[1024:1536]
        d0[1] = dv[1024:1536]


def attend_back_call(p, q, do, lse, delta, lo, kv2, kv1, kv0):
    kvspec = pl.BlockSpec((2, TOK, 128), lambda i, r: (0, 0, p))
    rowspec = pl.BlockSpec((RT, 384), lambda i, r: (r, p))
    statspec = pl.BlockSpec((8, RT), lambda i, r: (p, r))
    kvout = pl.BlockSpec((2, TOK, 128), lambda i, r: (0, 0, 0))
    acc = pltpu.VMEM((HALO + TOK, 128), F32)
    return pl.pallas_call(
        attend_back_kernel,
        grid=(1, 2),
        out_shape=(
            sds((TOK, 384), F32),
            sds((2, TOK, 128), BF16),
            sds((2, TOK, 128), BF16),
            sds((2, TOK, 128), F32),
        ),
        in_specs=[
            rowspec,
            rowspec,
            statspec,
            statspec,
            pl.BlockSpec((1, RT), lambda i, r: (0, r)),
            kvspec,
            kvspec,
            kvspec,
        ],
        out_specs=(pl.BlockSpec((RT, 384), lambda i, r: (r, 0)), kvout, kvout, kvout),
        scratch_shapes=[
            pltpu.VMEM((4, HALO + TOK, 128), BF16),
            pltpu.VMEM((4, HALO + TOK, 128), BF16),
            pltpu.VMEM((128, HALO + TOK), BF16),
            pltpu.VMEM((SPAN, RT), F32),
            pltpu.VMEM((384, RT), F32),
            acc,
            acc,
        ],
        compiler_params=params(),
        cost_estimate=cost(),
        name="attend_back",
    )(q, do, lse, delta, lo, kv2, kv1, kv0)


def out_proj_kernel(offs, att, oi, oo2, wo, part, mid_o, w, sem):
    cs = piece_copies(offs, (wo,), w, sem)
    for c in cs:
        c.start()
    a = att[...]
    mid = nt(a, oi[...]).astype(BF16)
    mid_o[...] = mid
    for c in cs:
        c.wait()
    for n in range(3):
        cols = slice(n * 512, (n + 1) * 512)
        part[:, cols] = (nt(a, w[cols, :]) + nn(mid, oo2[:, cols])).astype(BF16)


def out_proj_call(offs, att, oi, oo2, wo):
    return pl.pallas_call(
        out_proj_kernel,
        out_shape=(sds((TOK, D), BF16), sds((TOK, 128), BF16)),
        in_specs=[SM] + [VM] * 3 + [HB],
        out_specs=(VM, VM),
        scratch_shapes=[pltpu.VMEM((D, HQ), BF16), pltpu.SemaphoreType.DMA((16,))],
        compiler_params=params(),
        cost_estimate=cost(),
        name="out_proj",
    )(offs, att, oi, oo2, wo)


def ffn_in_kernel(tok, own, other, gain, a_gu, resid_o, nf_o, mid_o):
    branch = own[...].astype(F32) + other[...].astype(F32)
    x = tok[...].astype(F32) + RS * branch
    resid_o[...] = x
    inv = lax.rsqrt(jnp.mean(x * x, axis=-1, keepdims=True) + EPS)
    nf_o[...] = (x * inv * gain[...]).astype(BF16)
    mid_o[...] = nt(nf_o[...], a_gu[...]).astype(BF16)


def ffn_in_call(tok, own, other, gain, a_gu):
    return pl.pallas_call(
        ffn_in_kernel,
        grid=(4,),
        out_shape=(sds((TOK, D), F32), sds((TOK, D), BF16), sds((TOK, 128), BF16)),
        in_specs=[row_block(D)] * 3 + [all_block(1, D), all_block(128, D)],
        out_specs=(row_block(D), row_block(D), row_block(128)),
        compiler_params=params(16),
        cost_estimate=cost(),
        name="ffn_norm",
    )(tok, own, other, gain, a_gu)


def cot_kernel(place, own, other, do2, og_o, fg_o, mid_o):
    @pl.when(place[3] == 1)
    def _():
        og_o[...] = own[...]

    @pl.when(place[3] == 0)
    def _():
        og_o[...] = other[...]

    fg_o[...] = (RS * og_o[...].astype(F32)).astype(BF16)
    mid_o[...] = nt(fg_o[...], do2[...]).astype(BF16)


def cot_call(place, own, other, do2):
    return pl.pallas_call(
        cot_kernel,
        out_shape=(sds((TOK, D), BF16), sds((TOK, D), BF16), sds((TOK, 128), BF16)),
        in_specs=[SM] + [VM] * 3,
        out_specs=(VM,) * 3,
        compiler_params=params(16),
        cost_estimate=cost(),
        name="branch_cotangent",
    )(place, own, other, do2)


SPLIT = ((0, FA, 0, 0, FA), (1, FB, FA, 0, FB))
NCUT = ((0, 512), (512, 1024), (1024, DX))


def ffn_kernel(split, offs_a, offs_b, nf, fg, mid_gu, mid_dg, bg, bu, di, a_gu, do2, *refs):
    pa, pb = refs[:5], refs[5:10]
    part_f, part_n, rep_o, gout, uout, din = refs[10:16]
    wa, wb, xn, xf, accf, accn, sem_a, sem_b, sem = refs[16:]

    def adapter_rows(w, start, total, at):
        blk = pl.ds(start, total)
        return [
            pltpu.make_async_copy(src.at[:, blk], w.at[pl.ds(D, 128), pl.ds(k * total, total)], sem.at[at + k])
            for k, src in enumerate((bg, bu, di))
        ]

    first = piece_copies(offs_a, pa, wa, sem_a) + adapter_rows(wa, 0, FA, 0)
    inputs = [
        pltpu.make_async_copy(nf, xn.at[:, pl.ds(0, D)], sem.at[6]),
        pltpu.make_async_copy(mid_gu, xn.at[:, pl.ds(D, 128)], sem.at[7]),
        pltpu.make_async_copy(fg, xf.at[:, pl.ds(0, D)], sem.at[8]),
        pltpu.make_async_copy(mid_dg, xf.at[:, pl.ds(D, 128)], sem.at[9]),
    ]
    for c in inputs + first:
        c.start()
    for c in inputs:
        c.wait()
    mid_t = xn[:, D:DX].astype(F32).T.astype(BF16)[0:32]
    dg_t = xf[:, D:DX].astype(F32).T.astype(BF16)[0:16]
    for c in first:
        c.wait()
    second = piece_copies(offs_b, pb, wb, sem_b) + adapter_rows(wb, FA, FB, 3)
    for c in second:
        c.start()
    for w, total, start, at, n in split:
        if w == 0:
            w = wa
        else:
            w = wb
            if at == 0:
                for c in second:
                    c.wait()
        blk = slice(start, start + n)
        gc, uc, dc = (slice(k * total + at, k * total + at + n) for k in range(3))
        if n == total:
            gu = nn(xn[...], w[:, 0 : 2 * n])
            g, u = gu[:, 0:n], gu[:, n : 2 * n]
        else:
            g = nn(xn[...], w[:, gc])
            u = nn(xn[...], w[:, uc])
        hg = nn(xf[...], w[:, dc])
        sig = 1.0 / (1.0 + jnp.exp(-g))
        si = g * sig
        hid = (si * u).astype(BF16)
        gg = (hg * u * (sig * (1.0 + g * (1.0 - sig)))).astype(BF16)
        ug = (hg * si).astype(BF16)
        both = jnp.concatenate([gg, ug], axis=1)
        terms = 2.0 * nn(mid_t, both)
        gout[:, blk] = terms[0:16, 0:n].astype(BF16)
        uout[:, blk] = terms[16:32, n : 2 * n].astype(BF16)
        din[:, blk] = nn(dg_t, hid).astype(BF16)
        for c0, c1 in NCUT:
            cols = slice(c0, c1)
            f = nt(hid, w[cols, dc])
            if n == total:
                d = nt(both, w[cols, 0 : 2 * n])
            else:
                d = nt(gg, w[cols, gc]) + nt(ug, w[cols, uc])
            if start == 0:
                accf[:, cols] = f
                accn[:, cols] = d
            else:
                accf[:, cols] += f
                accn[:, cols] += d
    midd, midg = accf[:, D:DX], accn[:, D:DX]
    midd_b = midd.astype(BF16)
    midg_b = midg.astype(BF16)
    for c0 in range(0, D, 512):
        cols = slice(c0, c0 + 512)
        part_n[:, cols] = (accn[:, cols] + nn(midg_b, a_gu[:, cols])).astype(BF16)
        part_f[:, cols] = (accf[:, cols] + nn(midd_b, do2[:, cols])).astype(BF16)
    gu_in = nn(midg.T.astype(BF16)[0:32], xn[:, 0:D])
    d_out = 2.0 * nn(midd.T.astype(BF16)[0:16], xf[:, 0:D])
    for c in range(2):
        half = slice(c * 768, (c + 1) * 768)
        rep_o[c, 0:32] = gu_in[:, half].astype(BF16)
        rep_o[c, 32:48] = d_out[:, half].astype(BF16)


def ffn_call(offs_a, offs_b, nf, fg, mid_gu, mid_dg, bg, bu, di, a_gu, do2, wa, wb):
    def kernel(*refs):
        ffn_kernel(SPLIT, *refs)

    return pl.pallas_call(
        kernel,
        out_shape=(sds((TOK, D), BF16), sds((TOK, D), BF16), sds((2, 48, 768), BF16))
        + (sds((16, FH), BF16),) * 3,
        in_specs=[SM, SM] + [HB] * 7 + [VM] * 2 + [HB] * 10,
        out_specs=(VM,) * 6,
        scratch_shapes=[
            pltpu.VMEM((DX, 3 * FA), BF16),
            pltpu.VMEM((DX, 3 * FB), BF16),
            pltpu.VMEM((TOK, DX), BF16),
            pltpu.VMEM((TOK, DX), BF16),
            pltpu.VMEM((TOK, DX), F32),
            pltpu.VMEM((TOK, DX), F32),
            pltpu.SemaphoreType.DMA((16,)),
            pltpu.SemaphoreType.DMA((16,)),
            pltpu.SemaphoreType.DMA((10,)),
        ],
        compiler_params=params(),
        cost_estimate=cost(),
        name="ffn_both",
    )(offs_a, offs_b, nf, fg, mid_gu, mid_dg, bg, bu, di, a_gu, do2, *wa, *wb)


def out_back_kernel(
    offs, og, resid, own, other, gain, oi, oo2, mid_att, att, hsel, wo,
    rg_o, do_o, delta_o, rep_o, oin_o, w, abg, sem,
):
    cs = piece_copies(offs, (wo,), w, sem)
    for c in cs:
        c.start()
    for r in range(4):
        rows = pl.ds(r * 128, 128)
        x = resid[rows, :]
        inv = lax.rsqrt(jnp.mean(x * x, axis=-1, keepdims=True) + EPS)
        wv = (own[rows, :].astype(F32) + other[rows, :].astype(F32)) * gain[...]
        dot = jnp.mean(wv * x, axis=-1, keepdims=True)
        rg = og[rows, :].astype(F32) + inv * wv - x * (inv * inv * inv * dot)
        rg_o[rows, :] = rg
        abg[rows, :] = (RS * rg).astype(BF16)
    g = abg[...]
    mid_g = nt(g, oo2[...]).astype(BF16)
    for c in cs:
        c.wait()
    delta = jnp.zeros((16, TOK), F32)
    for n in range(3):
        cols = slice(n * 256, (n + 1) * 256)
        dd = (nn(g, w[:, cols]) + nn(mid_g, oi[:, cols])).astype(BF16)
        do_o[:, cols] = dd
        prod = dd.astype(F32) * att[:, cols].astype(F32)
        high = prod.astype(BF16)
        low = (prod - high.astype(F32)).astype(BF16)
        delta = delta + nt(hsel[:, cols], high) + nt(hsel[:, cols], low)
    delta_o[...] = delta
    o_out = 2.0 * nn(mid_att[...].astype(F32).T.astype(BF16)[0:16], g)
    for c in range(2):
        rep_o[c] = o_out[:, c * 768 : (c + 1) * 768].astype(BF16)
    oin_o[...] = nn(mid_g.astype(F32).T.astype(BF16)[0:16], att[...]).astype(BF16)


def out_back_call(offs, og, resid, own, other, gain, oi, oo2, mid_att, att, hsel, wo):
    return pl.pallas_call(
        out_back_kernel,
        out_shape=(
            sds((TOK, D), F32),
            sds((TOK, HQ), BF16),
            sds((16, TOK), F32),
            sds((2, 16, 768), BF16),
            sds((16, HQ), BF16),
        ),
        in_specs=[SM] + [VM] * 10 + [HB],
        out_specs=(VM,) * 5,
        scratch_shapes=[
            pltpu.VMEM((D, HQ), BF16),
            pltpu.VMEM((TOK, D), BF16),
            pltpu.SemaphoreType.DMA((16,)),
        ],
        compiler_params=params(),
        cost_estimate=cost(),
        name="out_proj_back",
    )(offs, og, resid, own, other, gain, oi, oo2, mid_att, att, hsel, wo)


def q_back_kernel(offs, dq0, dq1, cos, sin, b2, a1, mid, normed, *refs):
    pieces, (part, in_o, out_o, w, dall, sem) = refs[:5], refs[5:]
    cs = piece_copies(offs, [p.at[:, :, pl.ds(0, HQ)] for p in pieces], w, sem)
    for c in cs:
        c.start()
    cw = jnp.concatenate([cos[...], cos[...]], axis=1)
    sw = jnp.concatenate([sin[...], sin[...]], axis=1)
    dq = jnp.concatenate([dq0[...], dq1[...]], axis=1)
    for n in range(3):
        g = dq[:, n * 256 : (n + 1) * 256]
        dall[:, n * 256 : (n + 1) * 256] = (g * cw - half_swap(g) * sw).astype(BF16)
    d = dall[...]
    mid_g = nt(d, b2[:, 0:HQ]).astype(BF16)
    mid_t = mid[...].astype(F32).T.astype(BF16)
    out_o[...] = (2.0 * nn(mid_t[0:16], d)).astype(BF16)
    in_o[...] = nn(mid_g.astype(F32).T.astype(BF16)[0:16], normed[...]).astype(BF16)
    for c in cs:
        c.wait()
    for n in range(3):
        cols = slice(n * 512, (n + 1) * 512)
        part[:, cols] = nt(d, w[cols, :]) + nn(mid_g, a1[:, cols])


def q_back_call(offs, dq0, dq1, cos, sin, b2, a1, mid, normed, w):
    return pl.pallas_call(
        q_back_kernel,
        out_shape=(sds((TOK, D), F32), sds((16, D), BF16), sds((16, HQ), BF16)),
        in_specs=[SM] + [VM] * 8 + [HB] * 5,
        out_specs=(VM,) * 3,
        scratch_shapes=[
            pltpu.VMEM((D, HQ), BF16),
            pltpu.VMEM((TOK, HQ), BF16),
            pltpu.SemaphoreType.DMA((16,)),
        ],
        compiler_params=params(),
        cost_estimate=cost(),
        name="q_back",
    )(offs, dq0, dq1, cos, sin, b2, a1, mid, normed, *w)


def kv_back_kernel(offs, qpart, q_in, da0, da1, da2, db0, db1, db2, cos, sin, b2, a1, mid, normed, orep, *refs):
    pieces, (part, rep_o, out_o, w, dall, sem) = refs[:5], refs[5:]
    cs = piece_copies(offs, [p.at[:, :, pl.ds(HQ, 512)] for p in pieces], w, sem)
    for c in cs:
        c.start()
    cw = jnp.concatenate([cos[...], cos[...]], axis=1)
    sw = jnp.concatenate([sin[...], sin[...]], axis=1)
    both = []
    for i in range(2):
        own = jnp.concatenate([da0[i], db0[i]], axis=1)
        one = jnp.concatenate([da1[i], db1[i]], axis=1)
        two = jnp.concatenate([da2[i], db2[i]], axis=1)
        both.append(own + one.astype(F32) + two.astype(F32))
    dall[:, 0:256] = (both[0] * cw - half_swap(both[0]) * sw).astype(BF16)
    dall[:, 256:512] = both[1].astype(BF16)
    d = dall[...]
    mid_g = nt(d, b2[:, HQ:1280]).astype(BF16)
    mid_t = mid[...].astype(F32).T.astype(BF16)
    out_o[:, 0:256] = (2.0 * nn(mid_t[16:32], dall[:, 0:256])).astype(BF16)
    out_o[:, 256:512] = (2.0 * nn(mid_t[32:48], dall[:, 256:512])).astype(BF16)
    in_grads = nn(mid_g.astype(F32).T.astype(BF16)[16:48], normed[...]).astype(BF16)
    for c in range(2):
        cols = slice(c * 768, (c + 1) * 768)
        rep_o[c, 0:16] = q_in[:, cols]
        rep_o[c, 16:48] = in_grads[:, cols]
        rep_o[c, 48:64] = orep[c]
    for c in cs:
        c.wait()
    for n in range(3):
        cols = slice(n * 512, (n + 1) * 512)
        part[:, cols] = (qpart[:, cols] + nt(d, w[cols, :]) + nn(mid_g, a1[:, cols])).astype(BF16)


def kv_back_call(offs, qpart, q_in, da, db, cos, sin, b2, a1, mid, normed, orep, w):
    return pl.pallas_call(
        kv_back_kernel,
        out_shape=(sds((TOK, D), BF16), sds((2, 64, 768), BF16), sds((16, 512), BF16)),
        in_specs=[SM] + [VM] * 15 + [HB] * 5,
        out_specs=(VM,) * 3,
        scratch_shapes=[
            pltpu.VMEM((D, 512), BF16),
            pltpu.VMEM((TOK, 512), BF16),
            pltpu.SemaphoreType.DMA((16,)),
        ],
        compiler_params=params(),
        cost_estimate=cost(),
        name="kv_back",
    )(offs, qpart, q_in, *da, *db, cos, sin, b2, a1, mid, normed, orep, *w)


def token_grad_kernel(tok, rg, own, other, gain, out):
    x = tok[...].astype(F32)
    inv = lax.rsqrt(jnp.mean(x * x, axis=-1, keepdims=True) + EPS)
    wv = (own[...].astype(F32) + other[...].astype(F32)) * gain[...]
    dot = jnp.mean(wv * x, axis=-1, keepdims=True)
    out[...] = (rg[...] + inv * wv - x * (inv * inv * inv * dot)).astype(BF16)


def token_grad_call(tok, rg, own, other, gain):
    return pl.pallas_call(
        token_grad_kernel,
        grid=(4,),
        out_shape=sds((TOK, D), BF16),
        in_specs=[row_block(D)] * 4 + [all_block(1, D)],
        out_specs=row_block(D),
        compiler_params=params(16),
        cost_estimate=cost(),
        name="token_grad",
    )(tok, rg, own, other, gain)


def pack_first_kernel(q, k, v, out):
    out[:, 0:768] = q[...]
    out[:, 768:1024] = k[...]
    out[:, 1024:1280] = v[...]


def pack_first_call(q, k, v):
    return pl.pallas_call(
        pack_first_kernel,
        out_shape=sds((96, 1280), BF16),
        in_specs=[VM] * 3,
        out_specs=VM,
        compiler_params=params(),
        cost_estimate=cost(),
        name="pack_qkv",
    )(q, k, v)


def pack_rest_kernel(o, g, u, d, yx, xy):
    yx[:, 0:HQ] = o[...]
    for i, w in enumerate((g, u, d)):
        yx[:, HQ + i * FA : HQ + (i + 1) * FA] = w[:, 0:FA]
        xy[:, i * FB : (i + 1) * FB] = w[:, FA:FH]


def pack_rest_call(o, g, u, d):
    return pl.pallas_call(
        pack_rest_kernel,
        out_shape=(
            sds((96, HQ + 3 * FA), BF16),
            sds((96, 3 * FB), BF16),
        ),
        in_specs=[VM] * 4,
        out_specs=(VM,) * 2,
        compiler_params=params(),
        cost_estimate=cost(),
        name="pack_rest",
    )(o, g, u, d)


def line_call(parts, head):
    n = parts[0].shape[1] - head

    def kernel(*refs):
        ins, outs = refs[:4], refs[4:]
        for i in range(4):
            if head:
                outs[0][i] = ins[i][:, 0:head]
            outs[-1][i] = ins[i][:, head:]

    shapes = (sds((4, 96, head), BF16),) * bool(head) + (sds((4, 96, n), BF16),)
    return pl.pallas_call(
        kernel,
        out_shape=shapes,
        in_specs=[VM] * 4,
        out_specs=(VM,) * len(shapes),
        compiler_params=params(),
        cost_estimate=cost(),
        name="line",
    )(*parts)


def own_half_kernel(idx, q, k, v, o, g, u, d, out):
    at = 0
    for ref in (q, k, v, o, g, u, d):
        n = ref.shape[2]
        out[:, at : at + n] = ref[0]
        at += n


def own_half_call(index, arrays):
    return pl.pallas_call(
        own_half_kernel,
        out_shape=sds((16, 7808), BF16),
        grid_spec=pltpu.PrefetchScalarGridSpec(
            num_scalar_prefetch=1,
            grid=(1,),
            in_specs=[
                pl.BlockSpec((1, 16, a.shape[2]), lambda i, idx: (idx[0], 0, 0)) for a in arrays
            ],
            out_specs=pl.BlockSpec((16, 7808), lambda i, idx: (0, 0)),
        ),
        compiler_params=params(),
        cost_estimate=cost(),
        name="pick_halves",
    )(index, *arrays)


def factors_kernel(
    idx, halves, aq, ak, av, ag, au, oo, do, a_qkv, b_qkv, a_gu, bg, bu, di, oi, oo2, do2
):
    for ref in (a_qkv, b_qkv, a_gu, bg, bu, di, oi, oo2, do2):
        ref[...] = jnp.zeros_like(ref)
    for i, ref in enumerate((aq, ak, av)):
        a_qkv[i * 16 : (i + 1) * 16] = ref[0]
    for i, ref in enumerate((ag, au)):
        a_gu[i * 16 : (i + 1) * 16] = ref[0]
    oo2[0:16] = 2 * oo[0]
    do2[0:16] = 2 * do[0]
    b_qkv[0:16, 0:768] = 2 * halves[:, 0:768]
    b_qkv[16:32, 768:1024] = 2 * halves[:, 768:1024]
    b_qkv[32:48, 1024:1280] = 2 * halves[:, 1024:1280]
    oi[0:16] = halves[:, 1280:2048]
    bg[0:16] = 2 * halves[:, 2048:3968]
    bu[16:32] = 2 * halves[:, 3968:5888]
    di[0:16] = halves[:, 5888:7808]


def factors_call(index, halves, arrays):
    widths = (D, 1280, D, FH, FH, FH, HQ, D, D)
    return pl.pallas_call(
        factors_kernel,
        out_shape=tuple(sds((128, w), BF16) for w in widths),
        grid_spec=pltpu.PrefetchScalarGridSpec(
            num_scalar_prefetch=1,
            grid=(1,),
            in_specs=[pl.BlockSpec((16, 7808), lambda i, idx: (0, 0))]
            + [pl.BlockSpec((1, 16, D), lambda i, idx: (idx[0], 0, 0))] * 7,
            out_specs=tuple(pl.BlockSpec((128, w), lambda i, idx: (0, 0)) for w in widths),
        ),
        compiler_params=params(),
        cost_estimate=cost(),
        name="factors",
    )(index, halves, *arrays)


def quarters_kernel(m, place, rep, got, *refs):
    parts, outs, buf = refs[:-5], refs[-5:-1], refs[-1]
    core, z = place[0], place[1]
    n_rep = rep.shape[1] // 16
    kept = (rep[core].astype(F32) + got[...].astype(F32)).astype(BF16)
    for i in range(n_rep):
        buf[:, i * 768 : (i + 1) * 768] = kept[i * 16 : (i + 1) * 16]
    at = n_rep * 768
    for p in parts:
        buf[:, at : at + p.shape[1]] = p[...]
        at += p.shape[1]
    if at < 4 * m:
        buf[:, at : 4 * m] = jnp.zeros((16, 4 * m - at), BF16)
    for k, out in enumerate(outs):
        quarter = lax.rem(z + k, 4)
        out[...] = buf[:, pl.ds(pl.multiple_of(quarter * m, 128), m)]


def quarters_call(m, place, rep, got, parts):
    def kernel(*refs):
        quarters_kernel(m, *refs)

    return pl.pallas_call(
        kernel,
        out_shape=(sds((16, m), BF16),) * 4,
        in_specs=[SM] + [VM] * (2 + len(parts)),
        out_specs=(VM,) * 4,
        scratch_shapes=[pltpu.VMEM((16, 4 * m), BF16)],
        compiler_params=params(),
        cost_estimate=cost(),
        name="quarters",
    )(place, rep, got, *parts)


def pack_early_kernel(place, rep, got, g, u, d, out):
    kept = (rep[place[0]].astype(F32) + got[...].astype(F32)).astype(BF16)
    for i in range(3):
        out[:, i * 768 : (i + 1) * 768] = kept[i * 16 : (i + 1) * 16]
    for i, ref in enumerate((g, u, d)):
        out[:, 2304 + i * FH : 2304 + (i + 1) * FH] = ref[...]
    out[:, 8064:8192] = jnp.zeros((16, 128), BF16)


def pack_early_call(place, rep, got, g, u, d):
    return pl.pallas_call(
        pack_early_kernel,
        out_shape=sds((16, 4 * EARLY), BF16),
        in_specs=[SM] + [VM] * 5,
        out_specs=VM,
        compiler_params=params(),
        cost_estimate=cost(),
        name="pack_early",
    )(place, rep, got, g, u, d)


def quarter_kernel(place, total, out):
    at = pl.multiple_of(place[1] * EARLY, 128)
    out[:, 0:EARLY] = total[:, pl.ds(at, EARLY)]
    out[:, EARLY : EARLY + 128] = (
        jnp.full((16, 128), place[2], jnp.int32).astype(F32).astype(BF16)
    )


def quarter_call(place, total):
    return pl.pallas_call(
        quarter_kernel,
        out_shape=sds((16, EARLY + 128), BF16),
        in_specs=[SM, VM],
        out_specs=VM,
        compiler_params=params(),
        cost_estimate=cost(),
        name="quarter",
    )(place, total)


def sum_kernel(place, a, b, c, d, out):
    m = a.shape[1]
    total = a[...].astype(F32) + b[...].astype(F32) + c[...].astype(F32) + d[...].astype(F32)
    out[:, 0:m] = total.astype(BF16)
    out[:, m : m + 128] = jnp.full((16, 128), place[2], jnp.int32).astype(F32).astype(BF16)


def sum_call(place, parts):
    m = parts[0].shape[1]
    return pl.pallas_call(
        sum_kernel,
        out_shape=sds((16, m + 128), BF16),
        in_specs=[SM] + [VM] * 4,
        out_specs=VM,
        compiler_params=params(),
        cost_estimate=cost(),
        name="sum_tokens",
    )(place, *parts)


def by_adapter_kernel(*refs):
    ins, out = refs[:-1], refs[-1]
    m = out.shape[2]
    rows = [(r, k) for r in ins for k in range(r.shape[0])]
    for a in range(8):
        total = jnp.zeros((16, m), F32)
        for r, k in rows:
            hit = r[k, :, m : m + 1].astype(F32) == float(a)
            total = total + jnp.where(hit, r[k, :, 0:m].astype(F32), 0.0)
        out[a] = total.astype(BF16)


def by_adapter_call(parts, m):
    return pl.pallas_call(
        by_adapter_kernel,
        out_shape=sds((8, 16, m), BF16),
        in_specs=[VM] * len(parts),
        out_specs=VM,
        compiler_params=params(),
        cost_estimate=cost(),
        name="by_adapter",
    )(*parts)


def spread(buf, outs, jobs, widths):
    at = 0
    for out, n in zip(outs, widths, strict=True):
        for c in range(2):
            out[:, :, c * n : (c + 1) * n] = buf[c, :, :, at : at + n].astype(F32)
        at += n


def unpack_early_kernel(src, *refs):
    outs, buf, sem = refs[:-2], refs[-2], refs[-1]
    copies = []
    for z in range(4):
        for c in range(2):
            copies.append(
                pltpu.make_async_copy(
                    src.at[2 * z + c], buf.at[c, :, :, pl.ds(z * EARLY, EARLY)], sem.at[2 * z + c]
                )
            )
    for c in copies:
        c.start()
    for c in copies:
        c.wait()
    spread(buf, outs, None, (768, 768, 768, FH, FH, FH))


def unpack_early_call(src):
    widths = (D, D, D, 2 * FH, 2 * FH, 2 * FH)
    return pl.pallas_call(
        unpack_early_kernel,
        out_shape=tuple(sds((8, 16, w), F32) for w in widths),
        in_specs=[HB],
        out_specs=(VM,) * 6,
        scratch_shapes=[pltpu.VMEM((2, 8, 16, 4 * EARLY), BF16), pltpu.SemaphoreType.DMA((8,))],
        compiler_params=params(),
        cost_estimate=cost(),
        name="unpack_early",
    )(src)


def unpack_late_kernel(place, *refs):
    srcs, outs, buf, sem = refs[:8], refs[8:-2], refs[-2], refs[-1]
    core, z = place[0], place[1]
    copies = []
    for i, src in enumerate(srcs):
        c = core if i < 4 else 1 - core
        at = lax.rem(z + REL[i % 4] + 4, 4) * LATE
        copies.append(
            pltpu.make_async_copy(
                src, buf.at[c, :, :, pl.ds(pl.multiple_of(at, 128), LATE)], sem.at[i]
            )
        )
    for c in copies:
        c.start()
    for c in copies:
        c.wait()
    spread(buf, outs, None, (768, 768, 768, 768, 768, 256, 256, 768))


def unpack_late_call(place, srcs):
    widths = (D, D, D, D, D, 512, 512, D)
    return pl.pallas_call(
        unpack_late_kernel,
        out_shape=tuple(sds((8, 16, w), F32) for w in widths),
        in_specs=[SM] + [HB] * 8,
        out_specs=(VM,) * 8,
        scratch_shapes=[pltpu.VMEM((2, 8, 16, 4 * LATE), BF16), pltpu.SemaphoreType.DMA((8,))],
        compiler_params=params(),
        cost_estimate=cost(),
        name="unpack_late",
    )(place, *srcs)


YLIN = (0, 2, 1, 3)


def go_x(v, step):
    return lax.ppermute(v, "x", [(i, (i + step) % 4) for i in range(4)])


def go_y(v, step):
    return lax.ppermute(
        v, ("tensor", "yh"), [(YLIN[i], YLIN[(i + step) % 4]) for i in range(4)]
    )


def go_z(v, step):
    return lax.ppermute(v, "seq", [(i, (i + step) % 4) for i in range(4)])


def go_core(v):
    return lax.ppermute(v, "core", [(0, 1), (1, 0)])


def to_role(v):
    return lax.ppermute(v, ("tensor", "core"), [(1, 2), (2, 1)])


REL = (0, -1, 1, 2)


def near_line(shard, near):
    return (shard, near(shard, 1), near(shard, -1), near(shard, 2))


def ring_start(line, far):
    return (line, far(line, 1), far(line, -1))


def ring_halves(below, above):
    return below[:2], above[2:]


class Order:
    def __init__(self):
        self.last = ()

    def gate(self, v):
        return lax.optimization_barrier((v, self.last))[0]

    def done(self, v):
        v = self.gate(v)
        self.last = jax.tree.leaves(v)
        return v

    def run(self, step, *args):
        out = step(*self.gate(args))
        self.last = jax.tree.leaves(out)
        return out


def offsets(x, y, path):
    near = np.tile(np.array(REL, np.int32), 4)
    far = np.repeat(np.array(REL, np.int32), 4)
    if path == "yx":
        return ((x + far + 4) % 4) * 4 + (y + near + 4) % 4
    if path == "xy":
        return np.tile(np.arange(4, dtype=np.int32), 4) * 4 + (y + far + 4) % 4
    return np.repeat(np.arange(4, dtype=np.int32), 4) * 4 + (y + near + 4) % 4


def halo_back(grads):
    two, one, own = grads
    one = lax.ppermute(one, "seq", [(1, 0), (2, 1), (3, 2)])
    return (own, one, lax.ppermute(two, "seq", [(2, 0), (3, 1)]))


def shards(
    tokens,
    output_gradient,
    document_length_table,
    sequence_adapter_index,
    sequence_window_length,
    attention_norm_gain,
    feedforward_norm_gain,
    query_projection_weight,
    key_projection_weight,
    value_projection_weight,
    output_projection_weight,
    gate_projection_weight,
    up_projection_weight,
    down_projection_weight,
    query_adapter_first,
    query_adapter_second,
    key_adapter_first,
    key_adapter_second,
    value_adapter_first,
    value_adapter_second,
    output_adapter_first,
    output_adapter_second,
    gate_adapter_first,
    gate_adapter_second,
    up_adapter_first,
    up_adapter_second,
    down_adapter_first,
    down_adapter_second,
):
    z = lax.axis_index("seq")
    yl = lax.axis_index("tensor")
    x = lax.axis_index("x")
    y = lax.axis_index("yh") * 2 + yl
    core = lax.axis_index("core")
    same = core == yl

    o = Order()
    t = lambda v: v.swapaxes(1, 2)
    mine = lambda own, got: jnp.where(same, own, got)
    offs_yx, offs_xy, offs_o = (offsets(x, y, p) for p in ("yx", "xy", "o"))
    gain1 = attention_norm_gain[None, :]
    gain2 = feedforward_norm_gain[None, :]

    own_qkv = o.run(
        pack_first_call, query_projection_weight, key_projection_weight, value_projection_weight
    )
    got_qkv = to_role(own_qkv)
    own_yx, own_b = o.run(
        pack_rest_call,
        output_projection_weight,
        gate_projection_weight,
        up_projection_weight,
        down_projection_weight,
    )
    meta = jnp.concatenate(
        [document_length_table[0], sequence_adapter_index, sequence_window_length]
    )
    meta_other = go_core(meta)
    tok_other = go_core(tokens[0])
    near_qkv = near_line(o.run(mine, own_qkv, o.done(got_qkv)), go_y)
    own_halves = o.run(
        own_half_call,
        sequence_adapter_index,
        (
            query_adapter_second,
            key_adapter_second,
            value_adapter_second,
            output_adapter_first,
            gate_adapter_second,
            up_adapter_second,
            down_adapter_first,
        ),
    )
    line_qkv = o.run(lambda *v: line_call(v, 0)[0], *o.done(near_qkv))
    below_qkv, above_qkv = go_x(line_qkv, 1), go_x(line_qkv, -1)

    def tables(own, other):
        meta = mine(own, other)
        lengths, index, window = meta[:4], meta[4:5], meta[5]
        place = jnp.concatenate(
            [jnp.stack([core, z]), index, same[None]], dtype=jnp.int32
        )
        ends = jnp.cumsum(lengths, dtype=jnp.int32)
        begins = ends - lengths
        row = z * TOK + jnp.arange(TOK, dtype=jnp.int32)
        begin = jnp.max(jnp.where(row[:, None] >= begins[None, :], begins[None, :], 0), axis=1)
        low_key = (jnp.maximum(begin, row - window + 1) - (z * TOK - HALO))[None, :]
        lane = jnp.arange(128, dtype=jnp.int32) % HDIM
        frequency = ROPE_BASE ** (-((lane % 32).astype(F32) * (2.0 / HDIM)))
        angles = (row - begin).astype(F32)[:, None] * frequency[None, :]
        cos = jnp.cos(angles)
        sin = jnp.sin(angles) * jnp.where(lane < 32, -1.0, 1.0)[None, :]
        return index, place, low_key, cos, sin

    index, place, low_key, cos, sin = o.run(tables, meta, o.done(meta_other))
    got_halves, got_yx, got_b = (to_role(o.gate(v)) for v in (own_halves, own_yx, own_b))
    tok = o.run(mine, tokens[0], o.done(tok_other))
    halves = o.run(mine, own_halves, o.done(got_halves))
    a_qkv, b_qkv, a_gu, bg2, bu2, di_p, oi_p, oo2, do2 = o.run(
        factors_call,
        index,
        halves,
        (
            t(query_adapter_first),
            t(key_adapter_first),
            t(value_adapter_first),
            t(gate_adapter_first),
            t(up_adapter_first),
            output_adapter_second,
            down_adapter_second,
        ),
    )
    near_yx = near_line(o.run(mine, own_yx, o.done(got_yx)), go_y)
    own_b = o.run(mine, own_b, o.done(got_b))
    low, high = o.run(ring_halves, *o.done((below_qkv, above_qkv)))
    far_qkv = (go_x(low, 1), go_x(high, -1))
    line_b = lax.all_gather(o.gate(own_b), "x", axis=0)
    full_qkv = (line_qkv, below_qkv, above_qkv) + o.done(far_qkv)

    normed, q, kv0, mid_qkv = o.run(
        qkv_call, offs_yx, tok, gain1, a_qkv, b_qkv, cos, sin, full_qkv
    )
    kv1 = lax.ppermute(kv0, "seq", [(0, 1), (1, 2), (2, 3)])
    kv2 = lax.ppermute(kv0, "seq", [(0, 2), (1, 3)])
    line_o, line_a = o.run(lambda *v: line_call(v, HQ), *o.done(near_yx))
    full_o = lax.all_gather(line_o, "x", axis=0, tiled=True)
    line_b = o.done(line_b)
    below_b, above_b = go_y(line_b, 1), go_y(line_b, -1)
    kv1, kv2 = o.done((kv1, kv2))
    line_a = o.gate(line_a)
    below_a, above_a = go_x(line_a, 1), go_x(line_a, -1)
    att, lse = o.run(attend_call, q, low_key, kv2, kv1, kv0)
    low, high = o.run(ring_halves, *o.done((below_b, above_b)))
    far_b = (go_y(low, 1), go_y(high, -1))
    full_o = o.done(full_o)
    attn_part, mid_att = o.run(out_proj_call, offs_o, att, oi_p, oo2, full_o)
    attn_other = go_core(attn_part)
    og_other = go_core(o.gate(output_gradient[0]))
    low, high = o.run(ring_halves, *o.done((below_a, above_a)))
    far_a = (go_x(low, 1), go_x(high, -1))
    resid, nf, mid_gu = o.run(ffn_in_call, tok, attn_part, o.done(attn_other), gain2, a_gu)
    full_b = (line_b, below_b, above_b) + o.done(far_b)
    og, fg, mid_dg = o.run(cot_call, place, output_gradient[0], o.done(og_other), do2)
    full_a = (line_a, below_a, above_a) + o.done(far_a)
    ffn_part, nfg_part, rep_e, g_out, u_out, d_in = o.run(
        ffn_call,
        offs_yx, offs_xy, nf, fg, mid_gu, mid_dg, bg2, bu2, di_p, a_gu, do2, full_a, full_b,
    )

    def exchange(rep):
        return go_core(lax.dynamic_index_in_dim(rep, 1 - core, 0, keepdims=False))

    nfg_other = go_core(nfg_part)
    got_e = exchange(rep_e)
    quarters = o.run(
        lambda *v: quarters_call(EARLY, place, v[0], v[1], v[2:]),
        rep_e, o.done(got_e), g_out, u_out, d_in,
    )
    sent = [go_z(quarters[k], k) for k in (1, 2, 3)]
    head = np.arange(16)
    head = np.where(head % 8 < 6, 6 * (head // 8) + head % 8, -1)
    hsel = jnp.asarray((np.arange(HQ) // HDIM)[None, :] == head[:, None], BF16)
    rg, do, delta, rep_o, o_in = o.run(
        out_back_call,
        offs_o, og, resid, nfg_part, o.done(nfg_other), gain2, oi_p, oo2, mid_att, att, hsel, full_o,
    )
    near = near_line(o.run(sum_call, place, [quarters[0]] + o.done(sent)), go_y)
    stats = (lse, delta, low_key, kv2, kv1, kv0)
    dqa, *da = o.run(lambda *v: attend_back_call(0, *v), q, do, *stats)
    plane = lax.all_gather(o.run(lambda *v: jnp.stack(v), *o.done(near)), "x", axis=0, tiled=True)
    ra = halo_back(da)
    ffn_other = go_core(o.gate(ffn_part))
    dqb, *db = o.run(lambda *v: attend_back_call(1, *v), q, do, *stats)
    ra = o.done(ra)
    rb = halo_back(db)
    qpart, q_in, q_out = o.run(
        q_back_call, offs_yx, dqa, dqb, cos, sin, b_qkv, a_qkv, mid_qkv, normed, full_qkv
    )
    rb = o.done(rb)
    na_part, rep_l, kv_out = o.run(
        kv_back_call,
        offs_yx, qpart, q_in, ra, rb, cos, sin, b_qkv, a_qkv, mid_qkv, normed, rep_o, full_qkv,
    )
    na_other = go_core(na_part)
    got_l = exchange(rep_l)

    out = o.run(
        lambda r, a, b: (r + RS * (a.astype(F32) + b.astype(F32))).astype(BF16),
        resid, ffn_part, o.done(ffn_other),
    )
    out_other = to_role(out)
    quarters = o.run(
        lambda *v: quarters_call(LATE, place, v[0], v[1], v[2:]),
        rep_l, o.done(got_l), q_out, kv_out, o_in,
    )
    sent = [go_z(quarters[k], k) for k in (1, 2, 3)]
    dense = o.run(lambda v: by_adapter_call([v], EARLY), o.done(plane))
    early = lax.all_gather(dense, ("seq", "core"), axis=0)
    near = near_line(o.run(sum_call, place, [quarters[0]] + o.done(sent)), go_y)
    na_other = o.done(na_other)
    line = o.run(lambda *v: jnp.stack(v), *o.done(near))
    output = o.run(mine, out, o.done(out_other))
    lines = [go_x(line, 1), go_x(line, -1), go_x(line, 2)]
    token_grad = o.run(token_grad_call, tok, rg, na_part, na_other, gain1)
    tg_other = to_role(token_grad)
    dense = o.run(lambda *v: by_adapter_call(v, LATE), line, *o.done(lines))
    zs = [go_z(dense, 1), go_z(dense, -1), go_z(dense, 2)]
    cores = [go_core(dense)]
    g_in, u_in, d_out, g_out, u_out, d_in = o.run(unpack_early_call, o.done(early))
    zs = o.done(zs)
    cores += [go_core(v) for v in zs]
    token_grad = o.run(mine, token_grad, o.done(tg_other))
    q_in, k_in, v_in, o_out, q_out, k_out, v_out, o_in = o.run(
        unpack_late_call, place, [dense] + zs + o.done(cores)
    )
    return (
        output[None],
        token_grad[None],
        t(q_in),
        q_out,
        t(k_in),
        k_out,
        t(v_in),
        v_out,
        o_in,
        o_out,
        t(g_in),
        g_out,
        t(u_in),
        u_out,
        d_in,
        d_out,
    )


def solution(mesh):
    fine = Mesh(mesh.devices.reshape(4, 2, 4, 2, 2), ("seq", "tensor", "x", "yh", "core"))
    fsdp = ("x", "yh", "core")
    weight = P(fsdp, "tensor")
    half = P(None, None, "tensor")
    return jax.shard_map(
        shards,
        mesh=fine,
        in_specs=(
            P(fsdp, "seq", None),
            P(fsdp, "seq", None),
            P(fsdp, None),
            P(fsdp),
            P(fsdp),
            P(),
            P(),
        )
        + (weight,) * 7
        + (P(), half, P(), half, P(), half, half, P(), P(), half, P(), half, half, P()),
        out_specs=(P(fsdp, "seq", None), P(fsdp, "seq", None)) + (P(),) * 14,
        check_vma=False,
    )
```

```python
import jax
import jax.numpy as jnp
import numpy as np
from jax import lax
from jax.experimental import pallas as pl
from jax.experimental.pallas import tpu as pltpu
from jax.sharding import Mesh
from jax.sharding import PartitionSpec as P

F32 = jnp.float32
BF16 = jnp.bfloat16
EPS = 1e-05
ROPE_BASE = 10000.0
RS = 1.4 / 52.0**0.5
MASKED = -1e30
TOK = 512
D = 1536
DX = D + 128
HQ = 768
HK = 256
HDIM = 64
SPAN = 1280
RT = 256
HALO = 1024
FH = 1920
FA, FB = 896, 1024
EARLY = 2048
LATE = 1280


def nn(a, b):
    return lax.dot_general(a, b, (((1,), (0,)), ((), ())), preferred_element_type=F32)


def nt(a, b):
    return lax.dot_general(a, b, (((1,), (1,)), ((), ())), preferred_element_type=F32)


def tn(a, b):
    return lax.dot_general(a, b, (((0,), (0,)), ((), ())), preferred_element_type=F32)


VM = pl.BlockSpec(memory_space=pltpu.VMEM)
SM = pl.BlockSpec(memory_space=pltpu.SMEM)
HB = pl.BlockSpec(memory_space=pl.ANY)


def row_block(width):
    return pl.BlockSpec((128, width), lambda i: (i, 0))


def all_block(rows, width):
    return pl.BlockSpec((rows, width), lambda i: (0, 0))


def params(mib=58):
    return pltpu.CompilerParams(vmem_limit_bytes=mib * 1024 * 1024)


def cost():
    return pl.CostEstimate(flops=1, bytes_accessed=1, transcendentals=0)


def sds(shape, dtype):
    return jax.ShapeDtypeStruct(shape, dtype)


def piece_copies(offs, refs, dst, sems):
    copies = []
    for ref in refs:
        for k in range(ref.shape[0]):
            row = pl.multiple_of(offs[len(copies)] * 96, 96)
            copies.append(
                pltpu.make_async_copy(ref.at[k], dst.at[pl.ds(row, 96)], sems.at[len(copies)])
            )
    return copies


def half_swap(v):
    lane = lax.broadcasted_iota(jnp.int32, v.shape, 1)
    width = v.shape[1]
    from_low = pltpu.roll(v, 32, 1)
    from_high = pltpu.roll(v, width - 32, 1)
    return jnp.where((lane % 64) < 32, from_high, from_low)


def qkv_kernel(offs, tok, gain, a1, b2, cos, sin, *refs):
    pieces, (normed_o, q_o, kv_o, mid_o, w, sem) = refs[:5], refs[5:]
    cs = piece_copies(offs, pieces, w, sem)
    for c in cs:
        c.start()
    for r in range(4):
        rows = pl.ds(r * 128, 128)
        x = tok[rows, :].astype(F32)
        inv = lax.rsqrt(jnp.mean(x * x, axis=-1, keepdims=True) + EPS)
        normed_o[rows, :] = (x * inv * gain[...]).astype(BF16)
    normed = normed_o[...]
    mid = nt(normed, a1[...]).astype(BF16)
    mid_o[...] = mid
    for c in cs:
        c.wait()
    cw = jnp.concatenate([cos[...], cos[...]], axis=1)
    sw = jnp.concatenate([sin[...], sin[...]], axis=1)
    for n in (3, 4, 0, 1, 2):
        cols = slice(n * 256, (n + 1) * 256)
        acc = nn(normed, w[:, cols]) + nn(mid, b2[:, cols])
        if n < 4:
            acc = acc * cw + half_swap(acc) * sw
        if n < 3:
            q_o[:, cols] = (acc.astype(BF16).astype(F32) * 0.125).astype(BF16)
        else:
            kv_o[n - 3] = acc.astype(BF16)


def qkv_call(offs, tok, gain, a1, b2, cos, sin, w):
    return pl.pallas_call(
        qkv_kernel,
        out_shape=(
            sds((TOK, D), BF16),
            sds((TOK, HQ), BF16),
            sds((2, TOK, HK), BF16),
            sds((TOK, 128), BF16),
        ),
        in_specs=[SM] + [VM] * 6 + [HB] * 5,
        out_specs=(VM,) * 4,
        scratch_shapes=[pltpu.VMEM((D, 1280), BF16), pltpu.SemaphoreType.DMA((16,))],
        compiler_params=params(),
        cost_estimate=cost(),
        name="norm_qkv",
    )(offs, tok, gain, a1, b2, cos, sin, *w)


HEADS_OF_PAIR = ((0, 0, 0), (0, 1, 0), (1, 0, 0), (1, 1, 1), (2, 0, 1), (2, 1, 1))


def bias_of(lo, r):
    key = lax.broadcasted_iota(jnp.int32, (SPAN, RT), 0) + r * RT
    row = lax.broadcasted_iota(jnp.int32, (SPAN, RT), 1) + r * RT + HALO
    return jnp.where((key >= lo) & (key <= row), 0.0, MASKED)


def variants(dst, src, other=0.0):
    lane = lax.broadcasted_iota(jnp.int32, src.shape, 1)
    srcf = src.astype(F32)
    rolled = pltpu.roll(srcf, 64, 1)
    low = lane < 64
    dst[0] = jnp.where(low, srcf, other).astype(BF16)
    dst[1] = jnp.where(low, other, rolled).astype(BF16)
    dst[2] = jnp.where(low, rolled, other).astype(BF16)
    dst[3] = jnp.where(low, other, srcf).astype(BF16)


def in_half(v, half, want):
    return v if half == want else pltpu.roll(v, 64, 1)


def attend_kernel(q, lo, kv2, kv1, kv0, out, lse, kvar, vvar, bias):
    r = pl.program_id(1)
    lane = lax.broadcasted_iota(jnp.int32, (RT, 128), 1)
    low = lane < 64

    @pl.when(r == 0)
    def _():
        variants(kvar, jnp.concatenate([kv2[0], kv1[0], kv0[0]], axis=0))
        variants(vvar, jnp.concatenate([kv2[1], kv1[1], kv0[1]], axis=0), 1.0)

    key = lax.broadcasted_iota(jnp.int32, (RT, SPAN), 1) + r * RT
    row = lax.broadcasted_iota(jnp.int32, (RT, SPAN), 0) + r * RT + HALO
    bias[...] = jnp.where((key >= lo[...]) & (key <= row), 0.0, MASKED)
    keys = pl.ds(pl.multiple_of(r * RT, RT), SPAN)
    stats = jnp.zeros((RT, 128), F32)
    for tile in range(3):
        qt = q[:, tile * 128 : (tile + 1) * 128]
        pair = []
        for i in (2 * tile, 2 * tile + 1):
            _, half, kv = HEADS_OF_PAIR[i]
            s = nt(qt, kvar[2 * kv + half, keys, :]) + bias[...]
            m = jnp.max(s, axis=1, keepdims=True)
            e = jnp.exp(s - m).astype(BF16)
            o = nn(e, vvar[2 * kv + half, keys, :])
            total = o[:, 64:65] if half == 0 else o[:, 0:1]
            stats = jnp.where(lane == i, m + jnp.log(total), stats)
            pair.append(o)
        total = pltpu.roll(jnp.where(low, pair[1], pair[0]), 64, 1)
        out[:, tile * 128 : (tile + 1) * 128] = (jnp.where(low, pair[0], pair[1]) / total).astype(BF16)
    lse[...] = stats.T[0:8]


def attend_call(q, lo, kv2, kv1, kv0):
    kvspec = pl.BlockSpec((2, TOK, 128), lambda p, r: (0, 0, p))
    return pl.pallas_call(
        attend_kernel,
        grid=(2, 2),
        out_shape=(sds((TOK, HQ), BF16), sds((16, TOK), F32)),
        in_specs=[
            pl.BlockSpec((RT, 384), lambda p, r: (r, p)),
            pl.BlockSpec((RT, 1), lambda p, r: (r, 0)),
            kvspec,
            kvspec,
            kvspec,
        ],
        out_specs=(
            pl.BlockSpec((RT, 384), lambda p, r: (r, p)),
            pl.BlockSpec((8, RT), lambda p, r: (p, r)),
        ),
        scratch_shapes=[
            pltpu.VMEM((4, HALO + TOK, 128), BF16),
            pltpu.VMEM((4, HALO + TOK, 128), BF16),
            pltpu.VMEM((RT, SPAN), F32),
        ],
        compiler_params=params(),
        cost_estimate=cost(),
        name="attend",
    )(q, lo.T, kv2, kv1, kv0)


def attend_back_kernel(
    q, do, lse, delta, lo, kv2, kv1, kv0, dq, d2, d1, d0, kvar, vvar, kt, bias, dqt, dk_acc, dv_acc
):
    r = pl.program_id(1)

    @pl.when(r == 0)
    def _():
        kcat = jnp.concatenate([kv2[0], kv1[0], kv0[0]], axis=0)
        variants(kvar, kcat)
        kt[...] = kcat.astype(F32).T.astype(BF16)
        vcat = jnp.concatenate([kv2[1], kv1[1], kv0[1]], axis=0)
        variants(vvar, vcat)
        for ref in (dk_acc, dv_acc):
            ref[...] = jnp.zeros_like(ref)

    bias[...] = bias_of(lo[...], r)
    keys = pl.ds(pl.multiple_of(r * RT, RT), SPAN)
    low = lax.broadcasted_iota(jnp.int32, (RT, 128), 1) < 64
    for u in range(2):
        ps, dss, qs, dos = [], [], [], []
        for i in range(3 * u, 3 * u + 3):
            cols = slice((i // 2) * 128, (i // 2 + 1) * 128)
            half = i % 2
            qt = q[:, cols]
            dt = do[:, cols]
            keep = low if u == 0 else ~low
            qs.append(jnp.where(keep, in_half(qt.astype(F32), half, u), 0.0).astype(BF16))
            dos.append(jnp.where(keep, in_half(dt.astype(F32), half, u), 0.0).astype(BF16))
            s = nt(kvar[2 * u + half, keys, :], qt) + bias[...]
            p = jnp.exp(s - lse[i : i + 1, :])
            dp = nt(vvar[2 * u + half, keys, :], dt)
            dss.append((p * (dp - delta[i : i + 1, :])).astype(BF16))
            ps.append(p.astype(BF16))
        ds = jnp.concatenate(dss, axis=1)
        dv_acc[keys, :] += nn(jnp.concatenate(ps, axis=1), jnp.concatenate(dos, axis=0))
        dk_acc[keys, :] += nn(ds, jnp.concatenate(qs, axis=0))
        dqu = nn(kt[u * 64 : (u + 1) * 64, keys], ds)
        for g in range(3):
            i = 3 * u + g
            dqt[i * 64 : (i + 1) * 64, :] = dqu[:, g * RT : (g + 1) * RT]
    dq[...] = dqt[...].T * 0.125

    @pl.when(r == 1)
    def _():
        dk, dv = dk_acc[...], dv_acc[...]
        d2[0] = dk[0:512].astype(BF16)
        d2[1] = dv[0:512].astype(BF16)
        d1[0] = dk[512:1024].astype(BF16)
        d1[1] = dv[512:1024].astype(BF16)
        d0[0] = dk[1024:1536]
        d0[1] = dv[1024:1536]


def attend_back_call(p, q, do, lse, delta, lo, kv2, kv1, kv0):
    kvspec = pl.BlockSpec((2, TOK, 128), lambda i, r: (0, 0, p))
    rowspec = pl.BlockSpec((RT, 384), lambda i, r: (r, p))
    statspec = pl.BlockSpec((8, RT), lambda i, r: (p, r))
    kvout = pl.BlockSpec((2, TOK, 128), lambda i, r: (0, 0, 0))
    acc = pltpu.VMEM((HALO + TOK, 128), F32)
    return pl.pallas_call(
        attend_back_kernel,
        grid=(1, 2),
        out_shape=(
            sds((TOK, 384), F32),
            sds((2, TOK, 128), BF16),
            sds((2, TOK, 128), BF16),
            sds((2, TOK, 128), F32),
        ),
        in_specs=[
            rowspec,
            rowspec,
            statspec,
            statspec,
            pl.BlockSpec((1, RT), lambda i, r: (0, r)),
            kvspec,
            kvspec,
            kvspec,
        ],
        out_specs=(pl.BlockSpec((RT, 384), lambda i, r: (r, 0)), kvout, kvout, kvout),
        scratch_shapes=[
            pltpu.VMEM((4, HALO + TOK, 128), BF16),
            pltpu.VMEM((4, HALO + TOK, 128), BF16),
            pltpu.VMEM((128, HALO + TOK), BF16),
            pltpu.VMEM((SPAN, RT), F32),
            pltpu.VMEM((384, RT), F32),
            acc,
            acc,
        ],
        compiler_params=params(),
        cost_estimate=cost(),
        name="attend_back",
    )(q, do, lse, delta, lo, kv2, kv1, kv0)


def out_proj_kernel(offs, att, oi, oo2, wo, part, mid_o, w, sem):
    cs = piece_copies(offs, (wo,), w, sem)
    for c in cs:
        c.start()
    a = att[...]
    mid = nt(a, oi[...]).astype(BF16)
    mid_o[...] = mid
    for c in cs:
        c.wait()
    for n in range(3):
        cols = slice(n * 512, (n + 1) * 512)
        part[:, cols] = (nt(a, w[cols, :]) + nn(mid, oo2[:, cols])).astype(BF16)


def out_proj_call(offs, att, oi, oo2, wo):
    return pl.pallas_call(
        out_proj_kernel,
        out_shape=(sds((TOK, D), BF16), sds((TOK, 128), BF16)),
        in_specs=[SM] + [VM] * 3 + [HB],
        out_specs=(VM, VM),
        scratch_shapes=[pltpu.VMEM((D, HQ), BF16), pltpu.SemaphoreType.DMA((16,))],
        compiler_params=params(),
        cost_estimate=cost(),
        name="out_proj",
    )(offs, att, oi, oo2, wo)


def ffn_in_kernel(tok, own, other, gain, a_gu, resid_o, nf_o, mid_o):
    branch = own[...].astype(F32) + other[...].astype(F32)
    x = tok[...].astype(F32) + RS * branch
    resid_o[...] = x
    inv = lax.rsqrt(jnp.mean(x * x, axis=-1, keepdims=True) + EPS)
    nf_o[...] = (x * inv * gain[...]).astype(BF16)
    mid_o[...] = nt(nf_o[...], a_gu[...]).astype(BF16)


def ffn_in_call(tok, own, other, gain, a_gu):
    return pl.pallas_call(
        ffn_in_kernel,
        grid=(4,),
        out_shape=(sds((TOK, D), F32), sds((TOK, D), BF16), sds((TOK, 128), BF16)),
        in_specs=[row_block(D)] * 3 + [all_block(1, D), all_block(128, D)],
        out_specs=(row_block(D), row_block(D), row_block(128)),
        compiler_params=params(16),
        cost_estimate=cost(),
        name="ffn_norm",
    )(tok, own, other, gain, a_gu)


def cot_kernel(place, own, other, do2, og_o, fg_o, mid_o):
    @pl.when(place[3] == 1)
    def _():
        og_o[...] = own[...]

    @pl.when(place[3] == 0)
    def _():
        og_o[...] = other[...]

    fg_o[...] = (RS * og_o[...].astype(F32)).astype(BF16)
    mid_o[...] = nt(fg_o[...], do2[...]).astype(BF16)


def cot_call(place, own, other, do2):
    return pl.pallas_call(
        cot_kernel,
        out_shape=(sds((TOK, D), BF16), sds((TOK, D), BF16), sds((TOK, 128), BF16)),
        in_specs=[SM] + [VM] * 3,
        out_specs=(VM,) * 3,
        compiler_params=params(16),
        cost_estimate=cost(),
        name="branch_cotangent",
    )(place, own, other, do2)


SPLIT = ((0, FA, 0, 0, FA), (1, FB, FA, 0, FB))
NCUT = ((0, 512), (512, 1024), (1024, DX))


def ffn_kernel(split, offs_a, offs_b, nf, fg, mid_gu, mid_dg, bg, bu, di, a_gu, do2, *refs):
    pa, pb = refs[:5], refs[5:10]
    part_f, part_n, rep_o, gout, uout, din = refs[10:16]
    wa, wb, xn, xf, accf, accn, sem_a, sem_b, sem = refs[16:]

    def adapter_rows(w, start, total, at):
        blk = pl.ds(start, total)
        return [
            pltpu.make_async_copy(src.at[:, blk], w.at[pl.ds(D, 128), pl.ds(k * total, total)], sem.at[at + k])
            for k, src in enumerate((bg, bu, di))
        ]

    first = piece_copies(offs_a, pa, wa, sem_a) + adapter_rows(wa, 0, FA, 0)
    inputs = [
        pltpu.make_async_copy(nf, xn.at[:, pl.ds(0, D)], sem.at[6]),
        pltpu.make_async_copy(mid_gu, xn.at[:, pl.ds(D, 128)], sem.at[7]),
        pltpu.make_async_copy(fg, xf.at[:, pl.ds(0, D)], sem.at[8]),
        pltpu.make_async_copy(mid_dg, xf.at[:, pl.ds(D, 128)], sem.at[9]),
    ]
    for c in inputs + first:
        c.start()
    for c in inputs:
        c.wait()
    mid_t = xn[:, D:DX].astype(F32).T.astype(BF16)[0:32]
    dg_t = xf[:, D:DX].astype(F32).T.astype(BF16)[0:16]
    for c in first:
        c.wait()
    second = piece_copies(offs_b, pb, wb, sem_b) + adapter_rows(wb, FA, FB, 3)
    for c in second:
        c.start()
    for w, total, start, at, n in split:
        if w == 0:
            w = wa
        else:
            w = wb
            if at == 0:
                for c in second:
                    c.wait()
        blk = slice(start, start + n)
        gc, uc, dc = (slice(k * total + at, k * total + at + n) for k in range(3))
        if n == total:
            gu = nn(xn[...], w[:, 0 : 2 * n])
            g, u = gu[:, 0:n], gu[:, n : 2 * n]
        else:
            g = nn(xn[...], w[:, gc])
            u = nn(xn[...], w[:, uc])
        hg = nn(xf[...], w[:, dc])
        sig = 1.0 / (1.0 + jnp.exp(-g))
        si = g * sig
        hid = (si * u).astype(BF16)
        gg = (hg * u * (sig * (1.0 + g * (1.0 - sig)))).astype(BF16)
        ug = (hg * si).astype(BF16)
        both = jnp.concatenate([gg, ug], axis=1)
        terms = 2.0 * nn(mid_t, both)
        gout[:, blk] = terms[0:16, 0:n].astype(BF16)
        uout[:, blk] = terms[16:32, n : 2 * n].astype(BF16)
        din[:, blk] = nn(dg_t, hid).astype(BF16)
        for c0, c1 in NCUT:
            cols = slice(c0, c1)
            f = nt(hid, w[cols, dc])
            if n == total:
                d = nt(both, w[cols, 0 : 2 * n])
            else:
                d = nt(gg, w[cols, gc]) + nt(ug, w[cols, uc])
            if start == 0:
                accf[:, cols] = f
                accn[:, cols] = d
            else:
                accf[:, cols] += f
                accn[:, cols] += d
    midd, midg = accf[:, D:DX], accn[:, D:DX]
    midd_b = midd.astype(BF16)
    midg_b = midg.astype(BF16)
    for c0 in range(0, D, 512):
        cols = slice(c0, c0 + 512)
        part_n[:, cols] = (accn[:, cols] + nn(midg_b, a_gu[:, cols])).astype(BF16)
        part_f[:, cols] = (accf[:, cols] + nn(midd_b, do2[:, cols])).astype(BF16)
    gu_in = nn(midg.T.astype(BF16)[0:32], xn[:, 0:D])
    d_out = 2.0 * nn(midd.T.astype(BF16)[0:16], xf[:, 0:D])
    for c in range(2):
        half = slice(c * 768, (c + 1) * 768)
        rep_o[c, 0:32] = gu_in[:, half].astype(BF16)
        rep_o[c, 32:48] = d_out[:, half].astype(BF16)


def ffn_call(offs_a, offs_b, nf, fg, mid_gu, mid_dg, bg, bu, di, a_gu, do2, wa, wb):
    def kernel(*refs):
        ffn_kernel(SPLIT, *refs)

    return pl.pallas_call(
        kernel,
        out_shape=(sds((TOK, D), BF16), sds((TOK, D), BF16), sds((2, 48, 768), BF16))
        + (sds((16, FH), BF16),) * 3,
        in_specs=[SM, SM] + [HB] * 7 + [VM] * 2 + [HB] * 10,
        out_specs=(VM,) * 6,
        scratch_shapes=[
            pltpu.VMEM((DX, 3 * FA), BF16),
            pltpu.VMEM((DX, 3 * FB), BF16),
            pltpu.VMEM((TOK, DX), BF16),
            pltpu.VMEM((TOK, DX), BF16),
            pltpu.VMEM((TOK, DX), F32),
            pltpu.VMEM((TOK, DX), F32),
            pltpu.SemaphoreType.DMA((16,)),
            pltpu.SemaphoreType.DMA((16,)),
            pltpu.SemaphoreType.DMA((10,)),
        ],
        compiler_params=params(),
        cost_estimate=cost(),
        name="ffn_both",
    )(offs_a, offs_b, nf, fg, mid_gu, mid_dg, bg, bu, di, a_gu, do2, *wa, *wb)


def out_back_kernel(
    offs, og, resid, own, other, gain, oi, oo2, mid_att, att, hsel, wo,
    rg_o, do_o, delta_o, rep_o, oin_o, w, abg, sem,
):
    cs = piece_copies(offs, (wo,), w, sem)
    for c in cs:
        c.start()
    for r in range(4):
        rows = pl.ds(r * 128, 128)
        x = resid[rows, :]
        inv = lax.rsqrt(jnp.mean(x * x, axis=-1, keepdims=True) + EPS)
        wv = (own[rows, :].astype(F32) + other[rows, :].astype(F32)) * gain[...]
        dot = jnp.mean(wv * x, axis=-1, keepdims=True)
        rg = og[rows, :].astype(F32) + inv * wv - x * (inv * inv * inv * dot)
        rg_o[rows, :] = rg
        abg[rows, :] = (RS * rg).astype(BF16)
    g = abg[...]
    mid_g = nt(g, oo2[...]).astype(BF16)
    for c in cs:
        c.wait()
    delta = jnp.zeros((16, TOK), F32)
    for n in range(3):
        cols = slice(n * 256, (n + 1) * 256)
        dd = (nn(g, w[:, cols]) + nn(mid_g, oi[:, cols])).astype(BF16)
        do_o[:, cols] = dd
        prod = dd.astype(F32) * att[:, cols].astype(F32)
        high = prod.astype(BF16)
        low = (prod - high.astype(F32)).astype(BF16)
        delta = delta + nt(hsel[:, cols], high) + nt(hsel[:, cols], low)
    delta_o[...] = delta
    o_out = 2.0 * nn(mid_att[...].astype(F32).T.astype(BF16)[0:16], g)
    for c in range(2):
        rep_o[c] = o_out[:, c * 768 : (c + 1) * 768].astype(BF16)
    oin_o[...] = nn(mid_g.astype(F32).T.astype(BF16)[0:16], att[...]).astype(BF16)


def out_back_call(offs, og, resid, own, other, gain, oi, oo2, mid_att, att, hsel, wo):
    return pl.pallas_call(
        out_back_kernel,
        out_shape=(
            sds((TOK, D), F32),
            sds((TOK, HQ), BF16),
            sds((16, TOK), F32),
            sds((2, 16, 768), BF16),
            sds((16, HQ), BF16),
        ),
        in_specs=[SM] + [VM] * 10 + [HB],
        out_specs=(VM,) * 5,
        scratch_shapes=[
            pltpu.VMEM((D, HQ), BF16),
            pltpu.VMEM((TOK, D), BF16),
            pltpu.SemaphoreType.DMA((16,)),
        ],
        compiler_params=params(),
        cost_estimate=cost(),
        name="out_proj_back",
    )(offs, og, resid, own, other, gain, oi, oo2, mid_att, att, hsel, wo)


def q_back_kernel(offs, dq0, dq1, cos, sin, b2, a1, mid, normed, *refs):
    pieces, (part, in_o, out_o, w, dall, sem) = refs[:5], refs[5:]
    cs = piece_copies(offs, [p.at[:, :, pl.ds(0, HQ)] for p in pieces], w, sem)
    for c in cs:
        c.start()
    cw = jnp.concatenate([cos[...], cos[...]], axis=1)
    sw = jnp.concatenate([sin[...], sin[...]], axis=1)
    dq = jnp.concatenate([dq0[...], dq1[...]], axis=1)
    for n in range(3):
        g = dq[:, n * 256 : (n + 1) * 256]
        dall[:, n * 256 : (n + 1) * 256] = (g * cw - half_swap(g) * sw).astype(BF16)
    d = dall[...]
    mid_g = nt(d, b2[:, 0:HQ]).astype(BF16)
    mid_t = mid[...].astype(F32).T.astype(BF16)
    out_o[...] = (2.0 * nn(mid_t[0:16], d)).astype(BF16)
    in_o[...] = nn(mid_g.astype(F32).T.astype(BF16)[0:16], normed[...]).astype(BF16)
    for c in cs:
        c.wait()
    for n in range(3):
        cols = slice(n * 512, (n + 1) * 512)
        part[:, cols] = nt(d, w[cols, :]) + nn(mid_g, a1[:, cols])


def q_back_call(offs, dq0, dq1, cos, sin, b2, a1, mid, normed, w):
    return pl.pallas_call(
        q_back_kernel,
        out_shape=(sds((TOK, D), F32), sds((16, D), BF16), sds((16, HQ), BF16)),
        in_specs=[SM] + [VM] * 8 + [HB] * 5,
        out_specs=(VM,) * 3,
        scratch_shapes=[
            pltpu.VMEM((D, HQ), BF16),
            pltpu.VMEM((TOK, HQ), BF16),
            pltpu.SemaphoreType.DMA((16,)),
        ],
        compiler_params=params(),
        cost_estimate=cost(),
        name="q_back",
    )(offs, dq0, dq1, cos, sin, b2, a1, mid, normed, *w)


def kv_back_kernel(offs, qpart, q_in, da0, da1, da2, db0, db1, db2, cos, sin, b2, a1, mid, normed, orep, *refs):
    pieces, (part, rep_o, out_o, w, dall, sem) = refs[:5], refs[5:]
    cs = piece_copies(offs, [p.at[:, :, pl.ds(HQ, 512)] for p in pieces], w, sem)
    for c in cs:
        c.start()
    cw = jnp.concatenate([cos[...], cos[...]], axis=1)
    sw = jnp.concatenate([sin[...], sin[...]], axis=1)
    both = []
    for i in range(2):
        own = jnp.concatenate([da0[i], db0[i]], axis=1)
        one = jnp.concatenate([da1[i], db1[i]], axis=1)
        two = jnp.concatenate([da2[i], db2[i]], axis=1)
        both.append(own + one.astype(F32) + two.astype(F32))
    dall[:, 0:256] = (both[0] * cw - half_swap(both[0]) * sw).astype(BF16)
    dall[:, 256:512] = both[1].astype(BF16)
    d = dall[...]
    mid_g = nt(d, b2[:, HQ:1280]).astype(BF16)
    mid_t = mid[...].astype(F32).T.astype(BF16)
    out_o[:, 0:256] = (2.0 * nn(mid_t[16:32], dall[:, 0:256])).astype(BF16)
    out_o[:, 256:512] = (2.0 * nn(mid_t[32:48], dall[:, 256:512])).astype(BF16)
    in_grads = nn(mid_g.astype(F32).T.astype(BF16)[16:48], normed[...]).astype(BF16)
    for c in range(2):
        cols = slice(c * 768, (c + 1) * 768)
        rep_o[c, 0:16] = q_in[:, cols]
        rep_o[c, 16:48] = in_grads[:, cols]
        rep_o[c, 48:64] = orep[c]
    for c in cs:
        c.wait()
    for n in range(3):
        cols = slice(n * 512, (n + 1) * 512)
        part[:, cols] = (qpart[:, cols] + nt(d, w[cols, :]) + nn(mid_g, a1[:, cols])).astype(BF16)


def kv_back_call(offs, qpart, q_in, da, db, cos, sin, b2, a1, mid, normed, orep, w):
    return pl.pallas_call(
        kv_back_kernel,
        out_shape=(sds((TOK, D), BF16), sds((2, 64, 768), BF16), sds((16, 512), BF16)),
        in_specs=[SM] + [VM] * 15 + [HB] * 5,
        out_specs=(VM,) * 3,
        scratch_shapes=[
            pltpu.VMEM((D, 512), BF16),
            pltpu.VMEM((TOK, 512), BF16),
            pltpu.SemaphoreType.DMA((16,)),
        ],
        compiler_params=params(),
        cost_estimate=cost(),
        name="kv_back",
    )(offs, qpart, q_in, *da, *db, cos, sin, b2, a1, mid, normed, orep, *w)


def token_grad_kernel(tok, rg, own, other, gain, out):
    x = tok[...].astype(F32)
    inv = lax.rsqrt(jnp.mean(x * x, axis=-1, keepdims=True) + EPS)
    wv = (own[...].astype(F32) + other[...].astype(F32)) * gain[...]
    dot = jnp.mean(wv * x, axis=-1, keepdims=True)
    out[...] = (rg[...] + inv * wv - x * (inv * inv * inv * dot)).astype(BF16)


def token_grad_call(tok, rg, own, other, gain):
    return pl.pallas_call(
        token_grad_kernel,
        grid=(4,),
        out_shape=sds((TOK, D), BF16),
        in_specs=[row_block(D)] * 4 + [all_block(1, D)],
        out_specs=row_block(D),
        compiler_params=params(16),
        cost_estimate=cost(),
        name="token_grad",
    )(tok, rg, own, other, gain)


def pack_first_kernel(q, k, v, out):
    out[:, 0:768] = q[...]
    out[:, 768:1024] = k[...]
    out[:, 1024:1280] = v[...]


def pack_first_call(q, k, v):
    return pl.pallas_call(
        pack_first_kernel,
        out_shape=sds((96, 1280), BF16),
        in_specs=[VM] * 3,
        out_specs=VM,
        compiler_params=params(),
        cost_estimate=cost(),
        name="pack_qkv",
    )(q, k, v)


def pack_rest_kernel(o, g, u, d, yx, xy):
    yx[:, 0:HQ] = o[...]
    for i, w in enumerate((g, u, d)):
        yx[:, HQ + i * FA : HQ + (i + 1) * FA] = w[:, 0:FA]
        xy[:, i * FB : (i + 1) * FB] = w[:, FA:FH]


def pack_rest_call(o, g, u, d):
    return pl.pallas_call(
        pack_rest_kernel,
        out_shape=(
            sds((96, HQ + 3 * FA), BF16),
            sds((96, 3 * FB), BF16),
        ),
        in_specs=[VM] * 4,
        out_specs=(VM,) * 2,
        compiler_params=params(),
        cost_estimate=cost(),
        name="pack_rest",
    )(o, g, u, d)


def line_call(parts, head):
    n = parts[0].shape[1] - head

    def kernel(*refs):
        ins, outs = refs[:4], refs[4:]
        for i in range(4):
            if head:
                outs[0][i] = ins[i][:, 0:head]
            outs[-1][i] = ins[i][:, head:]

    shapes = (sds((4, 96, head), BF16),) * bool(head) + (sds((4, 96, n), BF16),)
    return pl.pallas_call(
        kernel,
        out_shape=shapes,
        in_specs=[VM] * 4,
        out_specs=(VM,) * len(shapes),
        compiler_params=params(),
        cost_estimate=cost(),
        name="line",
    )(*parts)


def own_half_kernel(idx, q, k, v, o, g, u, d, out):
    at = 0
    for ref in (q, k, v, o, g, u, d):
        n = ref.shape[2]
        out[:, at : at + n] = ref[0]
        at += n


def own_half_call(index, arrays):
    return pl.pallas_call(
        own_half_kernel,
        out_shape=sds((16, 7808), BF16),
        grid_spec=pltpu.PrefetchScalarGridSpec(
            num_scalar_prefetch=1,
            grid=(1,),
            in_specs=[
                pl.BlockSpec((1, 16, a.shape[2]), lambda i, idx: (idx[0], 0, 0)) for a in arrays
            ],
            out_specs=pl.BlockSpec((16, 7808), lambda i, idx: (0, 0)),
        ),
        compiler_params=params(),
        cost_estimate=cost(),
        name="pick_halves",
    )(index, *arrays)


def factors_kernel(
    idx, halves, aq, ak, av, ag, au, oo, do, a_qkv, b_qkv, a_gu, bg, bu, di, oi, oo2, do2
):
    for ref in (a_qkv, b_qkv, a_gu, bg, bu, di, oi, oo2, do2):
        ref[...] = jnp.zeros_like(ref)
    for i, ref in enumerate((aq, ak, av)):
        a_qkv[i * 16 : (i + 1) * 16] = ref[0]
    for i, ref in enumerate((ag, au)):
        a_gu[i * 16 : (i + 1) * 16] = ref[0]
    oo2[0:16] = 2 * oo[0]
    do2[0:16] = 2 * do[0]
    b_qkv[0:16, 0:768] = 2 * halves[:, 0:768]
    b_qkv[16:32, 768:1024] = 2 * halves[:, 768:1024]
    b_qkv[32:48, 1024:1280] = 2 * halves[:, 1024:1280]
    oi[0:16] = halves[:, 1280:2048]
    bg[0:16] = 2 * halves[:, 2048:3968]
    bu[16:32] = 2 * halves[:, 3968:5888]
    di[0:16] = halves[:, 5888:7808]


def factors_call(index, halves, arrays):
    widths = (D, 1280, D, FH, FH, FH, HQ, D, D)
    return pl.pallas_call(
        factors_kernel,
        out_shape=tuple(sds((128, w), BF16) for w in widths),
        grid_spec=pltpu.PrefetchScalarGridSpec(
            num_scalar_prefetch=1,
            grid=(1,),
            in_specs=[pl.BlockSpec((16, 7808), lambda i, idx: (0, 0))]
            + [pl.BlockSpec((1, 16, D), lambda i, idx: (idx[0], 0, 0))] * 7,
            out_specs=tuple(pl.BlockSpec((128, w), lambda i, idx: (0, 0)) for w in widths),
        ),
        compiler_params=params(),
        cost_estimate=cost(),
        name="factors",
    )(index, halves, *arrays)


def quarters_kernel(m, place, rep, got, *refs):
    parts, outs, buf = refs[:-5], refs[-5:-1], refs[-1]
    core, z = place[0], place[1]
    n_rep = rep.shape[1] // 16
    kept = (rep[core].astype(F32) + got[...].astype(F32)).astype(BF16)
    for i in range(n_rep):
        buf[:, i * 768 : (i + 1) * 768] = kept[i * 16 : (i + 1) * 16]
    at = n_rep * 768
    for p in parts:
        buf[:, at : at + p.shape[1]] = p[...]
        at += p.shape[1]
    if at < 4 * m:
        buf[:, at : 4 * m] = jnp.zeros((16, 4 * m - at), BF16)
    for k, out in enumerate(outs):
        quarter = lax.rem(z + k, 4)
        out[...] = buf[:, pl.ds(pl.multiple_of(quarter * m, 128), m)]


def quarters_call(m, place, rep, got, parts):
    def kernel(*refs):
        quarters_kernel(m, *refs)

    return pl.pallas_call(
        kernel,
        out_shape=(sds((16, m), BF16),) * 4,
        in_specs=[SM] + [VM] * (2 + len(parts)),
        out_specs=(VM,) * 4,
        scratch_shapes=[pltpu.VMEM((16, 4 * m), BF16)],
        compiler_params=params(6 if m == LATE else 58),
        cost_estimate=cost(),
        name="quarters",
    )(place, rep, got, *parts)


def pack_early_kernel(place, rep, got, g, u, d, out):
    kept = (rep[place[0]].astype(F32) + got[...].astype(F32)).astype(BF16)
    for i in range(3):
        out[:, i * 768 : (i + 1) * 768] = kept[i * 16 : (i + 1) * 16]
    for i, ref in enumerate((g, u, d)):
        out[:, 2304 + i * FH : 2304 + (i + 1) * FH] = ref[...]
    out[:, 8064:8192] = jnp.zeros((16, 128), BF16)


def pack_early_call(place, rep, got, g, u, d):
    return pl.pallas_call(
        pack_early_kernel,
        out_shape=sds((16, 4 * EARLY), BF16),
        in_specs=[SM] + [VM] * 5,
        out_specs=VM,
        compiler_params=params(),
        cost_estimate=cost(),
        name="pack_early",
    )(place, rep, got, g, u, d)


def quarter_kernel(place, total, out):
    out[:, 0:EARLY] = total[...]
    out[:, EARLY : EARLY + 128] = (
        jnp.full((16, 128), place[2], jnp.int32).astype(F32).astype(BF16)
    )


def quarter_call(place, total):
    return pl.pallas_call(
        quarter_kernel,
        out_shape=sds((16, EARLY + 128), BF16),
        in_specs=[SM, VM],
        out_specs=VM,
        compiler_params=params(),
        cost_estimate=cost(),
        name="quarter",
    )(place, total)


def sum_kernel(place, a, b, c, d, out):
    m = a.shape[1]
    total = a[...].astype(F32) + b[...].astype(F32) + c[...].astype(F32) + d[...].astype(F32)
    out[:, 0:m] = total.astype(BF16)
    out[:, m : m + 128] = jnp.full((16, 128), place[2], jnp.int32).astype(F32).astype(BF16)


def sum_call(place, parts):
    m = parts[0].shape[1]
    return pl.pallas_call(
        sum_kernel,
        out_shape=sds((16, m + 128), BF16),
        in_specs=[SM] + [VM] * 4,
        out_specs=VM,
        compiler_params=params(6),
        cost_estimate=cost(),
        name="sum_tokens",
    )(place, *parts)


def by_adapter_kernel(*refs):
    ins, out, total = refs[:-2], refs[-2], refs[-1]
    m = out.shape[2]
    total[...] = jnp.zeros_like(total)
    for r in ins:
        for k in range(r.shape[0]):
            adapter = jnp.max(r[k, :, m : m + 128].astype(F32)).astype(jnp.int32)
            total[adapter] += r[k, :, 0:m].astype(F32)
    out[...] = total[...].astype(BF16)


def by_adapter_call(parts, m):
    return pl.pallas_call(
        by_adapter_kernel,
        out_shape=sds((8, 16, m), BF16),
        in_specs=[VM] * len(parts),
        out_specs=VM,
        scratch_shapes=[pltpu.VMEM((8, 16, m), F32)],
        compiler_params=params(14),
        cost_estimate=cost(),
        name="by_adapter",
    )(*parts)


def spread(buf, outs, jobs, widths):
    at = 0
    for out, n in zip(outs, widths, strict=True):
        for c in range(2):
            out[:, :, c * n : (c + 1) * n] = buf[c, :, :, at : at + n].astype(F32)
        at += n


def unpack_early_kernel(src, *refs):
    outs, buf, sem = refs[:-2], refs[-2], refs[-1]
    copies = []
    for z in range(4):
        for c in range(2):
            copies.append(
                pltpu.make_async_copy(
                    src.at[2 * z + c], buf.at[c, :, :, pl.ds(z * EARLY, EARLY)], sem.at[2 * z + c]
                )
            )
    for c in copies:
        c.start()
    for c in copies:
        c.wait()
    spread(buf, outs, None, (768, 768, 768, FH, FH, FH))


def unpack_early_call(src):
    widths = (D, D, D, 2 * FH, 2 * FH, 2 * FH)
    return pl.pallas_call(
        unpack_early_kernel,
        out_shape=tuple(sds((8, 16, w), F32) for w in widths),
        in_specs=[HB],
        out_specs=(VM,) * 6,
        scratch_shapes=[pltpu.VMEM((2, 8, 16, 4 * EARLY), BF16), pltpu.SemaphoreType.DMA((8,))],
        compiler_params=params(),
        cost_estimate=cost(),
        name="unpack_early",
    )(src)


def unpack_late_kernel(place, *refs):
    srcs, outs, buf, sem = refs[:8], refs[8:-2], refs[-2], refs[-1]
    core, z = place[0], place[1]
    copies = []
    for i, src in enumerate(srcs):
        c = core if i < 4 else 1 - core
        at = lax.rem(z + REL[i % 4] + 4, 4) * LATE
        copies.append(
            pltpu.make_async_copy(
                src, buf.at[c, :, :, pl.ds(pl.multiple_of(at, 128), LATE)], sem.at[i]
            )
        )
    for c in copies:
        c.start()
    for c in copies:
        c.wait()
    spread(buf, outs, None, (768, 768, 768, 768, 768, 256, 256, 768))


def unpack_late_call(place, srcs):
    widths = (D, D, D, D, D, 512, 512, D)
    return pl.pallas_call(
        unpack_late_kernel,
        out_shape=tuple(sds((8, 16, w), F32) for w in widths),
        in_specs=[SM] + [HB] * 8,
        out_specs=(VM,) * 8,
        scratch_shapes=[pltpu.VMEM((2, 8, 16, 4 * LATE), BF16), pltpu.SemaphoreType.DMA((8,))],
        compiler_params=params(24),
        cost_estimate=cost(),
        name="unpack_late",
    )(place, *srcs)


YLIN = (0, 2, 1, 3)


def go_x(v, step):
    return lax.ppermute(v, "x", [(i, (i + step) % 4) for i in range(4)])


def go_y(v, step):
    return lax.ppermute(
        v, ("tensor", "yh"), [(YLIN[i], YLIN[(i + step) % 4]) for i in range(4)]
    )


def go_z(v, step):
    return lax.ppermute(v, "seq", [(i, (i + step) % 4) for i in range(4)])


def go_core(v):
    return lax.ppermute(v, "core", [(0, 1), (1, 0)])


def to_role(v):
    return lax.ppermute(v, ("tensor", "core"), [(1, 2), (2, 1)])


REL = (0, -1, 1, 2)


def near_line(shard, near):
    return (shard, near(shard, 1), near(shard, -1), near(shard, 2))


def ring_start(line, far):
    return (line, far(line, 1), far(line, -1))


def ring_halves(below, above):
    return below[:2], above[2:]


class Order:
    def __init__(self):
        self.last = ()

    def gate(self, v):
        return lax.optimization_barrier((v, self.last))[0]

    def done(self, v):
        v = self.gate(v)
        self.last = jax.tree.leaves(v)
        return v

    def run(self, step, *args):
        out = step(*self.gate(args))
        self.last = jax.tree.leaves(out)
        return out


def offsets(x, y, path):
    near = np.tile(np.array(REL, np.int32), 4)
    far = np.repeat(np.array(REL, np.int32), 4)
    if path == "yx":
        return ((x + far + 4) % 4) * 4 + (y + near + 4) % 4
    if path == "xy":
        return np.tile(np.arange(4, dtype=np.int32), 4) * 4 + (y + far + 4) % 4
    return np.repeat(np.arange(4, dtype=np.int32), 4) * 4 + (y + near + 4) % 4


def halo_back(grads):
    two, one, own = grads
    one = lax.ppermute(one, "seq", [(1, 0), (2, 1), (3, 2)])
    return (own, one, lax.ppermute(two, "seq", [(2, 0), (3, 1)]))


def shards(
    tokens,
    output_gradient,
    document_length_table,
    sequence_adapter_index,
    sequence_window_length,
    attention_norm_gain,
    feedforward_norm_gain,
    query_projection_weight,
    key_projection_weight,
    value_projection_weight,
    output_projection_weight,
    gate_projection_weight,
    up_projection_weight,
    down_projection_weight,
    query_adapter_first,
    query_adapter_second,
    key_adapter_first,
    key_adapter_second,
    value_adapter_first,
    value_adapter_second,
    output_adapter_first,
    output_adapter_second,
    gate_adapter_first,
    gate_adapter_second,
    up_adapter_first,
    up_adapter_second,
    down_adapter_first,
    down_adapter_second,
):
    z = lax.axis_index("seq")
    yl = lax.axis_index("tensor")
    x = lax.axis_index("x")
    y = lax.axis_index("yh") * 2 + yl
    core = lax.axis_index("core")
    same = core == yl

    o = Order()
    t = lambda v: v.swapaxes(1, 2)
    mine = lambda own, got: jnp.where(same, own, got)
    offs_yx, offs_xy, offs_o = (offsets(x, y, p) for p in ("yx", "xy", "o"))
    gain1 = attention_norm_gain[None, :]
    gain2 = feedforward_norm_gain[None, :]

    own_qkv = o.run(
        pack_first_call, query_projection_weight, key_projection_weight, value_projection_weight
    )
    got_qkv = to_role(own_qkv)
    own_yx, own_b = o.run(
        pack_rest_call,
        output_projection_weight,
        gate_projection_weight,
        up_projection_weight,
        down_projection_weight,
    )
    meta = jnp.concatenate(
        [document_length_table[0], sequence_adapter_index, sequence_window_length]
    )
    meta_other = go_core(meta)
    tok_other = go_core(tokens[0])
    near_qkv = near_line(o.run(mine, own_qkv, o.done(got_qkv)), go_y)
    own_halves = o.run(
        own_half_call,
        sequence_adapter_index,
        (
            query_adapter_second,
            key_adapter_second,
            value_adapter_second,
            output_adapter_first,
            gate_adapter_second,
            up_adapter_second,
            down_adapter_first,
        ),
    )
    line_qkv = o.run(lambda *v: line_call(v, 0)[0], *o.done(near_qkv))
    below_qkv, above_qkv = go_x(line_qkv, 1), go_x(line_qkv, -1)

    def tables(own, other):
        meta = mine(own, other)
        lengths, index, window = meta[:4], meta[4:5], meta[5]
        place = jnp.concatenate(
            [jnp.stack([core, z]), index, same[None]], dtype=jnp.int32
        )
        ends = jnp.cumsum(lengths, dtype=jnp.int32)
        begins = ends - lengths
        row = z * TOK + jnp.arange(TOK, dtype=jnp.int32)
        begin = jnp.max(jnp.where(row[:, None] >= begins[None, :], begins[None, :], 0), axis=1)
        low_key = (jnp.maximum(begin, row - window + 1) - (z * TOK - HALO))[None, :]
        lane = jnp.arange(128, dtype=jnp.int32) % HDIM
        frequency = ROPE_BASE ** (-((lane % 32).astype(F32) * (2.0 / HDIM)))
        angles = (row - begin).astype(F32)[:, None] * frequency[None, :]
        cos = jnp.cos(angles)
        sin = jnp.sin(angles) * jnp.where(lane < 32, -1.0, 1.0)[None, :]
        return index, place, low_key, cos, sin

    index, place, low_key, cos, sin = o.run(tables, meta, o.done(meta_other))
    got_halves, got_yx, got_b = (to_role(o.gate(v)) for v in (own_halves, own_yx, own_b))
    tok = o.run(mine, tokens[0], o.done(tok_other))
    halves = o.run(mine, own_halves, o.done(got_halves))
    a_qkv, b_qkv, a_gu, bg2, bu2, di_p, oi_p, oo2, do2 = o.run(
        factors_call,
        index,
        halves,
        (
            t(query_adapter_first),
            t(key_adapter_first),
            t(value_adapter_first),
            t(gate_adapter_first),
            t(up_adapter_first),
            output_adapter_second,
            down_adapter_second,
        ),
    )
    near_yx = near_line(o.run(mine, own_yx, o.done(got_yx)), go_y)
    own_b = o.run(mine, own_b, o.done(got_b))
    low, high = o.run(ring_halves, *o.done((below_qkv, above_qkv)))
    far_qkv = (go_x(low, 1), go_x(high, -1))
    line_b = lax.all_gather(o.gate(own_b), "x", axis=0)
    full_qkv = (line_qkv, below_qkv, above_qkv) + o.done(far_qkv)

    normed, q, kv0, mid_qkv = o.run(
        qkv_call, offs_yx, tok, gain1, a_qkv, b_qkv, cos, sin, full_qkv
    )
    kv1 = lax.ppermute(kv0, "seq", [(0, 1), (1, 2), (2, 3)])
    kv2 = lax.ppermute(kv0, "seq", [(0, 2), (1, 3)])
    line_o, line_a = o.run(lambda *v: line_call(v, HQ), *o.done(near_yx))
    full_o = lax.all_gather(line_o, "x", axis=0, tiled=True)
    line_b = o.done(line_b)
    below_b, above_b = go_y(line_b, 1), go_y(line_b, -1)
    kv1, kv2 = o.done((kv1, kv2))
    line_a = o.gate(line_a)
    below_a, above_a = go_x(line_a, 1), go_x(line_a, -1)
    og_other = go_core(o.gate(output_gradient[0]))
    att, lse = o.run(attend_call, q, low_key, kv2, kv1, kv0)
    og_other = o.done(og_other)
    low, high = o.run(ring_halves, *o.done((below_b, above_b)))
    far_b = (go_y(low, 1), go_y(high, -1))
    full_o = o.done(full_o)
    attn_part, mid_att = o.run(out_proj_call, offs_o, att, oi_p, oo2, full_o)
    attn_other = go_core(attn_part)
    low, high = o.run(ring_halves, *o.done((below_a, above_a)))
    far_a = (go_x(low, 1), go_x(high, -1))
    resid, nf, mid_gu = o.run(ffn_in_call, tok, attn_part, o.done(attn_other), gain2, a_gu)
    full_b = (line_b, below_b, above_b) + o.done(far_b)
    og, fg, mid_dg = o.run(cot_call, place, output_gradient[0], og_other, do2)
    full_a = (line_a, below_a, above_a) + o.done(far_a)
    ffn_part, nfg_part, rep_e, g_out, u_out, d_in = o.run(
        ffn_call,
        offs_yx, offs_xy, nf, fg, mid_gu, mid_dg, bg2, bu2, di_p, a_gu, do2, full_a, full_b,
    )

    def exchange(rep):
        return go_core(lax.dynamic_index_in_dim(rep, 1 - core, 0, keepdims=False))

    nfg_other = go_core(nfg_part)
    got_e = exchange(rep_e)
    packed = o.run(pack_early_call, place, rep_e, o.done(got_e), g_out, u_out, d_in)
    summed = lax.psum_scatter(packed, "seq", scatter_dimension=1, tiled=True)
    head = np.arange(16)
    head = np.where(head % 8 < 6, 6 * (head // 8) + head % 8, -1)
    hsel = jnp.asarray((np.arange(HQ) // HDIM)[None, :] == head[:, None], BF16)
    rg, do, delta, rep_o, o_in = o.run(
        out_back_call,
        offs_o, og, resid, nfg_part, o.done(nfg_other), gain2, oi_p, oo2, mid_att, att, hsel, full_o,
    )
    stats = (lse, delta, low_key, kv2, kv1, kv0)
    dqa, *da = o.run(lambda *v: attend_back_call(0, *v), q, do, *stats)
    near = near_line(o.run(quarter_call, place, o.done(summed)), go_y)
    ra = halo_back(da)
    dqb, *db = o.run(lambda *v: attend_back_call(1, *v), q, do, *stats)
    ra = o.done(ra)
    plane = lax.all_gather(o.run(lambda *v: jnp.stack(v), *o.done(near)), "x", axis=0, tiled=True)
    rb = halo_back(db)
    ffn_other = go_core(o.gate(ffn_part))
    qpart, q_in, q_out = o.run(
        q_back_call, offs_yx, dqa, dqb, cos, sin, b_qkv, a_qkv, mid_qkv, normed, full_qkv
    )
    rb = o.done(rb)
    na_part, rep_l, kv_out = o.run(
        kv_back_call,
        offs_yx, qpart, q_in, ra, rb, cos, sin, b_qkv, a_qkv, mid_qkv, normed, rep_o, full_qkv,
    )
    na_other = go_core(na_part)
    got_l = exchange(rep_l)
    ffn_other = o.done(ffn_other)

    out = o.run(
        lambda r, a, b: (r + RS * (a.astype(F32) + b.astype(F32))).astype(BF16),
        resid, ffn_part, ffn_other,
    )
    out_other = to_role(out)
    quarters = o.run(
        lambda *v: quarters_call(LATE, place, v[0], v[1], v[2:]),
        rep_l, o.done(got_l), q_out, kv_out, o_in,
    )
    sent = [go_z(quarters[k], k) for k in (1, 2, 3)]
    dense = o.run(lambda v: by_adapter_call([v], EARLY), o.done(plane))
    early = lax.all_gather(dense, ("seq", "core"), axis=0)
    near = near_line(o.run(sum_call, place, [quarters[0]] + o.done(sent)), go_y)
    na_other = o.done(na_other)
    line = o.run(lambda *v: jnp.stack(v), *o.done(near))
    lines = [go_x(line, 1), go_x(line, -1), go_x(line, 2)]
    token_grad = o.run(token_grad_call, tok, rg, na_part, na_other, gain1)
    tg_other = to_role(token_grad)
    dense = o.run(lambda *v: by_adapter_call(v, LATE), line, *o.done(lines))
    zs = [go_z(dense, 1), go_z(dense, -1), go_z(dense, 2)]
    cores = [go_core(dense)]
    g_in, u_in, d_out, g_out, u_out, d_in = o.run(unpack_early_call, o.done(early))
    output = o.run(mine, out, o.done(out_other))
    token_grad = o.run(mine, token_grad, o.done(tg_other))
    zs = o.done(zs)
    cores += [go_core(v) for v in zs]
    q_in, k_in, v_in, o_out, q_out, k_out, v_out, o_in = o.run(
        unpack_late_call, place, [dense] + zs + o.done(cores)
    )
    return (
        output[None],
        token_grad[None],
        t(q_in),
        q_out,
        t(k_in),
        k_out,
        t(v_in),
        v_out,
        o_in,
        o_out,
        t(g_in),
        g_out,
        t(u_in),
        u_out,
        d_in,
        d_out,
    )


def solution(mesh):
    fine = Mesh(mesh.devices.reshape(4, 2, 4, 2, 2), ("seq", "tensor", "x", "yh", "core"))
    fsdp = ("x", "yh", "core")
    weight = P(fsdp, "tensor")
    half = P(None, None, "tensor")
    return jax.shard_map(
        shards,
        mesh=fine,
        in_specs=(
            P(fsdp, "seq", None),
            P(fsdp, "seq", None),
            P(fsdp, None),
            P(fsdp),
            P(fsdp),
            P(),
            P(),
        )
        + (weight,) * 7
        + (P(), half, P(), half, P(), half, half, P(), P(), half, P(), half, half, P()),
        out_specs=(P(fsdp, "seq", None), P(fsdp, "seq", None)) + (P(),) * 14,
        check_vma=False,
    )
```

```python
import jax
import jax.numpy as jnp
import numpy as np
from jax import lax
from jax.experimental import pallas as pl
from jax.experimental.pallas import tpu as pltpu
from jax.sharding import Mesh
from jax.sharding import PartitionSpec as P

F32 = jnp.float32
BF16 = jnp.bfloat16
EPS = 1e-05
ROPE_BASE = 10000.0
RS = 1.4 / 52.0**0.5
MASKED = -1e30
TOK = 512
D = 1536
DX = D + 128
HQ = 768
HK = 256
HDIM = 64
SPAN = 1280
RT = 256
HALO = 1024
FH = 1920
FA, FB = 896, 1024
EARLY = 2048
LATE = 1280


def nn(a, b):
    return lax.dot_general(a, b, (((1,), (0,)), ((), ())), preferred_element_type=F32)


def nt(a, b):
    return lax.dot_general(a, b, (((1,), (1,)), ((), ())), preferred_element_type=F32)


VM = pl.BlockSpec(memory_space=pltpu.VMEM)
SM = pl.BlockSpec(memory_space=pltpu.SMEM)
HB = pl.BlockSpec(memory_space=pl.ANY)


def row_block(width):
    return pl.BlockSpec((128, width), lambda i: (i, 0))


def all_block(rows, width):
    return pl.BlockSpec((rows, width), lambda i: (0, 0))


def params(mib=58):
    return pltpu.CompilerParams(vmem_limit_bytes=mib * 1024 * 1024)


def cost():
    return pl.CostEstimate(flops=1, bytes_accessed=1, transcendentals=0)


def sds(shape, dtype):
    return jax.ShapeDtypeStruct(shape, dtype)


def piece_copies(offs, refs, dst, sems):
    copies = []
    for ref in refs:
        for k in range(ref.shape[0]):
            row = pl.multiple_of(offs[len(copies)] * 96, 96)
            copies.append(
                pltpu.make_async_copy(ref.at[k], dst.at[pl.ds(row, 96)], sems.at[len(copies)])
            )
    return copies


def half_swap(v):
    lane = lax.broadcasted_iota(jnp.int32, v.shape, 1)
    width = v.shape[1]
    from_low = pltpu.roll(v, 32, 1)
    from_high = pltpu.roll(v, width - 32, 1)
    return jnp.where((lane % 64) < 32, from_high, from_low)


def qkv_kernel(offs, tok, gain, a1, b2, cos, sin, *refs):
    pieces, (normed_o, q_o, kv_o, mid_o, w, sem) = refs[:5], refs[5:]
    cs = piece_copies(offs, pieces, w, sem)
    for c in cs:
        c.start()
    for r in range(4):
        rows = pl.ds(r * 128, 128)
        x = tok[rows, :].astype(F32)
        inv = lax.rsqrt(jnp.mean(x * x, axis=-1, keepdims=True) + EPS)
        normed_o[rows, :] = (x * inv * gain[...]).astype(BF16)
    normed = normed_o[...]
    mid = nt(normed, a1[...]).astype(BF16)
    mid_o[...] = mid
    for c in cs:
        c.wait()
    cw = jnp.concatenate([cos[...], cos[...]], axis=1)
    sw = jnp.concatenate([sin[...], sin[...]], axis=1)
    for n in (3, 4, 0, 1, 2):
        cols = slice(n * 256, (n + 1) * 256)
        acc = nn(normed, w[:, cols]) + nn(mid, b2[:, cols])
        if n < 4:
            acc = acc * cw + half_swap(acc) * sw
        if n < 3:
            q_o[:, cols] = (acc.astype(BF16).astype(F32) * 0.125).astype(BF16)
        else:
            kv_o[n - 3] = acc.astype(BF16)


def qkv_call(offs, tok, gain, a1, b2, cos, sin, w):
    return pl.pallas_call(
        qkv_kernel,
        out_shape=(
            sds((TOK, D), BF16),
            sds((TOK, HQ), BF16),
            sds((2, TOK, HK), BF16),
            sds((TOK, 128), BF16),
        ),
        in_specs=[SM] + [VM] * 6 + [HB] * 5,
        out_specs=(VM,) * 4,
        scratch_shapes=[pltpu.VMEM((D, 1280), BF16), pltpu.SemaphoreType.DMA((16,))],
        compiler_params=params(),
        cost_estimate=cost(),
        name="norm_qkv",
    )(offs, tok, gain, a1, b2, cos, sin, *w)


HEADS_OF_PAIR = ((0, 0, 0), (0, 1, 0), (1, 0, 0), (1, 1, 1), (2, 0, 1), (2, 1, 1))


def bias_of(lo, r):
    key = lax.broadcasted_iota(jnp.int32, (SPAN, RT), 0) + r * RT
    row = lax.broadcasted_iota(jnp.int32, (SPAN, RT), 1) + r * RT + HALO
    return jnp.where((key >= lo) & (key <= row), 0.0, MASKED)


def variants(dst, src, other=0.0):
    lane = lax.broadcasted_iota(jnp.int32, src.shape, 1)
    srcf = src.astype(F32)
    rolled = pltpu.roll(srcf, 64, 1)
    low = lane < 64
    dst[0] = jnp.where(low, srcf, other).astype(BF16)
    dst[1] = jnp.where(low, other, rolled).astype(BF16)
    dst[2] = jnp.where(low, rolled, other).astype(BF16)
    dst[3] = jnp.where(low, other, srcf).astype(BF16)


def in_half(v, half, want):
    return v if half == want else pltpu.roll(v, 64, 1)


def attend_kernel(q, lo, kv2, kv1, kv0, out, lse, kvar, vvar, bias):
    r = pl.program_id(1)
    lane = lax.broadcasted_iota(jnp.int32, (RT, 128), 1)
    low = lane < 64

    @pl.when(r == 0)
    def _():
        variants(kvar, jnp.concatenate([kv2[0], kv1[0], kv0[0]], axis=0))
        variants(vvar, jnp.concatenate([kv2[1], kv1[1], kv0[1]], axis=0), 1.0)

    key = lax.broadcasted_iota(jnp.int32, (RT, SPAN), 1) + r * RT
    row = lax.broadcasted_iota(jnp.int32, (RT, SPAN), 0) + r * RT + HALO
    bias[...] = jnp.where((key >= lo[...]) & (key <= row), 0.0, MASKED)
    keys = pl.ds(pl.multiple_of(r * RT, RT), SPAN)
    stats = jnp.zeros((RT, 128), F32)
    for tile in range(3):
        qt = q[:, tile * 128 : (tile + 1) * 128]
        pair = []
        for i in (2 * tile, 2 * tile + 1):
            _, half, kv = HEADS_OF_PAIR[i]
            s = nt(qt, kvar[2 * kv + half, keys, :]) + bias[...]
            m = jnp.max(s, axis=1, keepdims=True)
            e = jnp.exp(s - m).astype(BF16)
            o = nn(e, vvar[2 * kv + half, keys, :])
            total = o[:, 64:65] if half == 0 else o[:, 0:1]
            stats = jnp.where(lane == i, m + jnp.log(total), stats)
            pair.append(o)
        total = pltpu.roll(jnp.where(low, pair[1], pair[0]), 64, 1)
        out[:, tile * 128 : (tile + 1) * 128] = (jnp.where(low, pair[0], pair[1]) / total).astype(BF16)
    lse[...] = stats.T[0:8]


def attend_call(q, lo, kv2, kv1, kv0):
    kvspec = pl.BlockSpec((2, TOK, 128), lambda p, r: (0, 0, p))
    return pl.pallas_call(
        attend_kernel,
        grid=(2, 2),
        out_shape=(sds((TOK, HQ), BF16), sds((16, TOK), F32)),
        in_specs=[
            pl.BlockSpec((RT, 384), lambda p, r: (r, p)),
            pl.BlockSpec((RT, 1), lambda p, r: (r, 0)),
            kvspec,
            kvspec,
            kvspec,
        ],
        out_specs=(
            pl.BlockSpec((RT, 384), lambda p, r: (r, p)),
            pl.BlockSpec((8, RT), lambda p, r: (p, r)),
        ),
        scratch_shapes=[
            pltpu.VMEM((4, HALO + TOK, 128), BF16),
            pltpu.VMEM((4, HALO + TOK, 128), BF16),
            pltpu.VMEM((RT, SPAN), F32),
        ],
        compiler_params=params(),
        cost_estimate=cost(),
        name="attend",
    )(q, lo.T, kv2, kv1, kv0)


def attend_back_kernel(
    q, do, lse, delta, lo, kv2, kv1, kv0, dq, d2, d1, d0, kvar, vvar, kt, bias, dqt, dk_acc, dv_acc
):
    r = pl.program_id(1)

    @pl.when(r == 0)
    def _():
        kcat = jnp.concatenate([kv2[0], kv1[0], kv0[0]], axis=0)
        variants(kvar, kcat)
        kt[...] = kcat.astype(F32).T.astype(BF16)
        vcat = jnp.concatenate([kv2[1], kv1[1], kv0[1]], axis=0)
        variants(vvar, vcat)
        for ref in (dk_acc, dv_acc):
            ref[...] = jnp.zeros_like(ref)

    bias[...] = bias_of(lo[...], r)
    keys = pl.ds(pl.multiple_of(r * RT, RT), SPAN)
    low = lax.broadcasted_iota(jnp.int32, (RT, 128), 1) < 64
    for u in range(2):
        ps, dss, qs, dos = [], [], [], []
        for i in range(3 * u, 3 * u + 3):
            cols = slice((i // 2) * 128, (i // 2 + 1) * 128)
            half = i % 2
            qt = q[:, cols]
            dt = do[:, cols]
            keep = low if u == 0 else ~low
            qs.append(jnp.where(keep, in_half(qt.astype(F32), half, u), 0.0).astype(BF16))
            dos.append(jnp.where(keep, in_half(dt.astype(F32), half, u), 0.0).astype(BF16))
            s = nt(kvar[2 * u + half, keys, :], qt) + bias[...]
            p = jnp.exp(s - lse[i : i + 1, :])
            dp = nt(vvar[2 * u + half, keys, :], dt)
            dss.append((p * (dp - delta[i : i + 1, :])).astype(BF16))
            ps.append(p.astype(BF16))
        ds = jnp.concatenate(dss, axis=1)
        dv_acc[keys, :] += nn(jnp.concatenate(ps, axis=1), jnp.concatenate(dos, axis=0))
        dk_acc[keys, :] += nn(ds, jnp.concatenate(qs, axis=0))
        dqu = nn(kt[u * 64 : (u + 1) * 64, keys], ds)
        for g in range(3):
            i = 3 * u + g
            dqt[i * 64 : (i + 1) * 64, :] = dqu[:, g * RT : (g + 1) * RT]
    dq[...] = dqt[...].T * 0.125

    @pl.when(r == 1)
    def _():
        dk, dv = dk_acc[...], dv_acc[...]
        d2[0] = dk[0:512].astype(BF16)
        d2[1] = dv[0:512].astype(BF16)
        d1[0] = dk[512:1024].astype(BF16)
        d1[1] = dv[512:1024].astype(BF16)
        d0[0] = dk[1024:1536]
        d0[1] = dv[1024:1536]


def attend_back_call(p, q, do, lse, delta, lo, kv2, kv1, kv0):
    kvspec = pl.BlockSpec((2, TOK, 128), lambda i, r: (0, 0, p))
    rowspec = pl.BlockSpec((RT, 384), lambda i, r: (r, p))
    statspec = pl.BlockSpec((8, RT), lambda i, r: (p, r))
    kvout = pl.BlockSpec((2, TOK, 128), lambda i, r: (0, 0, 0))
    acc = pltpu.VMEM((HALO + TOK, 128), F32)
    return pl.pallas_call(
        attend_back_kernel,
        grid=(1, 2),
        out_shape=(
            sds((TOK, 384), F32),
            sds((2, TOK, 128), BF16),
            sds((2, TOK, 128), BF16),
            sds((2, TOK, 128), F32),
        ),
        in_specs=[
            rowspec,
            rowspec,
            statspec,
            statspec,
            pl.BlockSpec((1, RT), lambda i, r: (0, r)),
            kvspec,
            kvspec,
            kvspec,
        ],
        out_specs=(pl.BlockSpec((RT, 384), lambda i, r: (r, 0)), kvout, kvout, kvout),
        scratch_shapes=[
            pltpu.VMEM((4, HALO + TOK, 128), BF16),
            pltpu.VMEM((4, HALO + TOK, 128), BF16),
            pltpu.VMEM((128, HALO + TOK), BF16),
            pltpu.VMEM((SPAN, RT), F32),
            pltpu.VMEM((384, RT), F32),
            acc,
            acc,
        ],
        compiler_params=params(),
        cost_estimate=cost(),
        name="attend_back",
    )(q, do, lse, delta, lo, kv2, kv1, kv0)


def out_proj_kernel(offs, att, oi, oo2, wo, part, mid_o, w, sem):
    cs = piece_copies(offs, (wo,), w, sem)
    for c in cs:
        c.start()
    a = att[...]
    mid = nt(a, oi[...]).astype(BF16)
    mid_o[...] = mid
    for c in cs:
        c.wait()
    for n in range(3):
        cols = slice(n * 512, (n + 1) * 512)
        part[:, cols] = (nt(a, w[cols, :]) + nn(mid, oo2[:, cols])).astype(BF16)


def out_proj_call(offs, att, oi, oo2, wo):
    return pl.pallas_call(
        out_proj_kernel,
        out_shape=(sds((TOK, D), BF16), sds((TOK, 128), BF16)),
        in_specs=[SM] + [VM] * 3 + [HB],
        out_specs=(VM, VM),
        scratch_shapes=[pltpu.VMEM((D, HQ), BF16), pltpu.SemaphoreType.DMA((16,))],
        compiler_params=params(),
        cost_estimate=cost(),
        name="out_proj",
    )(offs, att, oi, oo2, wo)


def ffn_in_kernel(tok, own, other, gain, a_gu, resid_o, nf_o, mid_o):
    branch = own[...].astype(F32) + other[...].astype(F32)
    x = tok[...].astype(F32) + RS * branch
    resid_o[...] = x
    inv = lax.rsqrt(jnp.mean(x * x, axis=-1, keepdims=True) + EPS)
    nf_o[...] = (x * inv * gain[...]).astype(BF16)
    mid_o[...] = nt(nf_o[...], a_gu[...]).astype(BF16)


def ffn_in_call(tok, own, other, gain, a_gu):
    return pl.pallas_call(
        ffn_in_kernel,
        grid=(4,),
        out_shape=(sds((TOK, D), F32), sds((TOK, D), BF16), sds((TOK, 128), BF16)),
        in_specs=[row_block(D)] * 3 + [all_block(1, D), all_block(128, D)],
        out_specs=(row_block(D), row_block(D), row_block(128)),
        compiler_params=params(16),
        cost_estimate=cost(),
        name="ffn_norm",
    )(tok, own, other, gain, a_gu)


def cot_kernel(place, own, other, do2, og_o, fg_o, mid_o):
    @pl.when(place[3] == 1)
    def _():
        og_o[...] = own[...]

    @pl.when(place[3] == 0)
    def _():
        og_o[...] = other[...]

    fg_o[...] = (RS * og_o[...].astype(F32)).astype(BF16)
    mid_o[...] = nt(fg_o[...], do2[...]).astype(BF16)


def cot_call(place, own, other, do2):
    return pl.pallas_call(
        cot_kernel,
        out_shape=(sds((TOK, D), BF16), sds((TOK, D), BF16), sds((TOK, 128), BF16)),
        in_specs=[SM] + [VM] * 3,
        out_specs=(VM,) * 3,
        compiler_params=params(16),
        cost_estimate=cost(),
        name="branch_cotangent",
    )(place, own, other, do2)


SPLIT = ((0, FA, 0, 0, FA), (1, FB, FA, 0, FB))
NCUT = ((0, 512), (512, 1024), (1024, DX))


def keep_and_send(place, keep, send, rows, full):
    low, high = full[:, 0:768].astype(BF16), full[:, 768:1536].astype(BF16)

    @pl.when(place[0] == 0)
    def _():
        keep[rows, :] = low
        send[rows, :] = high

    @pl.when(place[0] == 1)
    def _():
        keep[rows, :] = high
        send[rows, :] = low


def ffn_kernel(split, place, offs_a, offs_b, nf, fg, mid_gu, mid_dg, bg, bu, di, a_gu, do2, *refs):
    pa, pb = refs[:5], refs[5:10]
    part_f, part_n, keep_o, send_o, gout, uout, din = refs[10:17]
    wa, wb, xn, xf, accf, accn, sem_a, sem_b, sem = refs[17:]

    def adapter_rows(w, start, total, at):
        blk = pl.ds(start, total)
        return [
            pltpu.make_async_copy(src.at[:, blk], w.at[pl.ds(D, 128), pl.ds(k * total, total)], sem.at[at + k])
            for k, src in enumerate((bg, bu, di))
        ]

    first = piece_copies(offs_a, pa, wa, sem_a) + adapter_rows(wa, 0, FA, 0)
    inputs = [
        pltpu.make_async_copy(nf, xn.at[:, pl.ds(0, D)], sem.at[6]),
        pltpu.make_async_copy(mid_gu, xn.at[:, pl.ds(D, 128)], sem.at[7]),
        pltpu.make_async_copy(fg, xf.at[:, pl.ds(0, D)], sem.at[8]),
        pltpu.make_async_copy(mid_dg, xf.at[:, pl.ds(D, 128)], sem.at[9]),
    ]
    for c in inputs + first:
        c.start()
    for c in inputs:
        c.wait()
    mid_t = xn[:, D:DX].astype(F32).T.astype(BF16)[0:32]
    dg_t = xf[:, D:DX].astype(F32).T.astype(BF16)[0:16]
    for c in first:
        c.wait()
    second = piece_copies(offs_b, pb, wb, sem_b) + adapter_rows(wb, FA, FB, 3)
    for c in second:
        c.start()
    for w, total, start, at, n in split:
        if w == 0:
            w = wa
        else:
            w = wb
            if at == 0:
                for c in second:
                    c.wait()
        blk = slice(start, start + n)
        gc, uc, dc = (slice(k * total + at, k * total + at + n) for k in range(3))
        if n == total:
            gu = nn(xn[...], w[:, 0 : 2 * n])
            g, u = gu[:, 0:n], gu[:, n : 2 * n]
        else:
            g = nn(xn[...], w[:, gc])
            u = nn(xn[...], w[:, uc])
        hg = nn(xf[...], w[:, dc])
        sig = 1.0 / (1.0 + jnp.exp(-g))
        si = g * sig
        hid = (si * u).astype(BF16)
        gg = (hg * u * (sig * (1.0 + g * (1.0 - sig)))).astype(BF16)
        ug = (hg * si).astype(BF16)
        both = jnp.concatenate([gg, ug], axis=1)
        terms = 2.0 * nn(mid_t, both)
        gout[:, blk] = terms[0:16, 0:n].astype(BF16)
        uout[:, blk] = terms[16:32, n : 2 * n].astype(BF16)
        din[:, blk] = nn(dg_t, hid).astype(BF16)
        for c0, c1 in NCUT:
            cols = slice(c0, c1)
            f = nt(hid, w[cols, dc])
            if n == total:
                d = nt(both, w[cols, 0 : 2 * n])
            else:
                d = nt(gg, w[cols, gc]) + nt(ug, w[cols, uc])
            if start == 0:
                accf[:, cols] = f
                accn[:, cols] = d
            else:
                accf[:, cols] += f
                accn[:, cols] += d
    midd, midg = accf[:, D:DX], accn[:, D:DX]
    midd_b = midd.astype(BF16)
    midg_b = midg.astype(BF16)
    for c0 in range(0, D, 512):
        cols = slice(c0, c0 + 512)
        part_n[:, cols] = (accn[:, cols] + nn(midg_b, a_gu[:, cols])).astype(BF16)
        part_f[:, cols] = (accf[:, cols] + nn(midd_b, do2[:, cols])).astype(BF16)
    gu_in = nn(midg.T.astype(BF16)[0:32], xn[:, 0:D])
    d_out = 2.0 * nn(midd.T.astype(BF16)[0:16], xf[:, 0:D])
    keep_and_send(place, keep_o, send_o, slice(0, 32), gu_in)
    keep_and_send(place, keep_o, send_o, slice(32, 48), d_out)


def ffn_call(place, offs_a, offs_b, nf, fg, mid_gu, mid_dg, bg, bu, di, a_gu, do2, wa, wb):
    def kernel(*refs):
        ffn_kernel(SPLIT, *refs)

    return pl.pallas_call(
        kernel,
        out_shape=(sds((TOK, D), BF16),) * 2
        + (sds((48, 768), BF16),) * 2
        + (sds((16, FH), BF16),) * 3,
        in_specs=[SM, SM, SM] + [HB] * 7 + [VM] * 2 + [HB] * 10,
        out_specs=(VM,) * 7,
        scratch_shapes=[
            pltpu.VMEM((DX, 3 * FA), BF16),
            pltpu.VMEM((DX, 3 * FB), BF16),
            pltpu.VMEM((TOK, DX), BF16),
            pltpu.VMEM((TOK, DX), BF16),
            pltpu.VMEM((TOK, DX), F32),
            pltpu.VMEM((TOK, DX), F32),
            pltpu.SemaphoreType.DMA((16,)),
            pltpu.SemaphoreType.DMA((16,)),
            pltpu.SemaphoreType.DMA((10,)),
        ],
        compiler_params=params(),
        cost_estimate=cost(),
        name="ffn_both",
    )(place, offs_a, offs_b, nf, fg, mid_gu, mid_dg, bg, bu, di, a_gu, do2, *wa, *wb)


def out_back_kernel(
    offs, og, resid, own, other, gain, oi, oo2, mid_att, att, hsel, wo,
    rg_o, do_o, delta_o, rep_o, oin_o, w, abg, sem,
):
    cs = piece_copies(offs, (wo,), w, sem)
    for c in cs:
        c.start()
    for r in range(4):
        rows = pl.ds(r * 128, 128)
        x = resid[rows, :]
        inv = lax.rsqrt(jnp.mean(x * x, axis=-1, keepdims=True) + EPS)
        wv = (own[rows, :].astype(F32) + other[rows, :].astype(F32)) * gain[...]
        dot = jnp.mean(wv * x, axis=-1, keepdims=True)
        rg = og[rows, :].astype(F32) + inv * wv - x * (inv * inv * inv * dot)
        rg_o[rows, :] = rg
        abg[rows, :] = (RS * rg).astype(BF16)
    g = abg[...]
    mid_g = nt(g, oo2[...]).astype(BF16)
    for c in cs:
        c.wait()
    delta = jnp.zeros((16, TOK), F32)
    for n in range(3):
        cols = slice(n * 256, (n + 1) * 256)
        dd = (nn(g, w[:, cols]) + nn(mid_g, oi[:, cols])).astype(BF16)
        do_o[:, cols] = dd
        prod = dd.astype(F32) * att[:, cols].astype(F32)
        high = prod.astype(BF16)
        low = (prod - high.astype(F32)).astype(BF16)
        delta = delta + nt(hsel[:, cols], high) + nt(hsel[:, cols], low)
    delta_o[...] = delta
    o_out = 2.0 * nn(mid_att[...].astype(F32).T.astype(BF16)[0:16], g)
    rep_o[...] = o_out.astype(BF16)
    oin_o[...] = nn(mid_g.astype(F32).T.astype(BF16)[0:16], att[...]).astype(BF16)


def out_back_call(offs, og, resid, own, other, gain, oi, oo2, mid_att, att, hsel, wo):
    return pl.pallas_call(
        out_back_kernel,
        out_shape=(
            sds((TOK, D), F32),
            sds((TOK, HQ), BF16),
            sds((16, TOK), F32),
            sds((16, D), BF16),
            sds((16, HQ), BF16),
        ),
        in_specs=[SM] + [VM] * 10 + [HB],
        out_specs=(VM,) * 5,
        scratch_shapes=[
            pltpu.VMEM((D, HQ), BF16),
            pltpu.VMEM((TOK, D), BF16),
            pltpu.SemaphoreType.DMA((16,)),
        ],
        compiler_params=params(),
        cost_estimate=cost(),
        name="out_proj_back",
    )(offs, og, resid, own, other, gain, oi, oo2, mid_att, att, hsel, wo)


def q_back_kernel(offs, dq0, dq1, cos, sin, b2, a1, mid, normed, *refs):
    pieces, (part, in_o, out_o, w, dall, sem) = refs[:5], refs[5:]
    cs = piece_copies(offs, [p.at[:, :, pl.ds(0, HQ)] for p in pieces], w, sem)
    for c in cs:
        c.start()
    cw = jnp.concatenate([cos[...], cos[...]], axis=1)
    sw = jnp.concatenate([sin[...], sin[...]], axis=1)
    dq = jnp.concatenate([dq0[...], dq1[...]], axis=1)
    for n in range(3):
        g = dq[:, n * 256 : (n + 1) * 256]
        dall[:, n * 256 : (n + 1) * 256] = (g * cw - half_swap(g) * sw).astype(BF16)
    d = dall[...]
    mid_g = nt(d, b2[:, 0:HQ]).astype(BF16)
    mid_t = mid[...].astype(F32).T.astype(BF16)
    out_o[...] = (2.0 * nn(mid_t[0:16], d)).astype(BF16)
    in_o[...] = nn(mid_g.astype(F32).T.astype(BF16)[0:16], normed[...]).astype(BF16)
    for c in cs:
        c.wait()
    for n in range(3):
        cols = slice(n * 512, (n + 1) * 512)
        part[:, cols] = nt(d, w[cols, :]) + nn(mid_g, a1[:, cols])


def q_back_call(offs, dq0, dq1, cos, sin, b2, a1, mid, normed, w):
    return pl.pallas_call(
        q_back_kernel,
        out_shape=(sds((TOK, D), F32), sds((16, D), BF16), sds((16, HQ), BF16)),
        in_specs=[SM] + [VM] * 8 + [HB] * 5,
        out_specs=(VM,) * 3,
        scratch_shapes=[
            pltpu.VMEM((D, HQ), BF16),
            pltpu.VMEM((TOK, HQ), BF16),
            pltpu.SemaphoreType.DMA((16,)),
        ],
        compiler_params=params(),
        cost_estimate=cost(),
        name="q_back",
    )(offs, dq0, dq1, cos, sin, b2, a1, mid, normed, *w)


def kv_back_kernel(place, offs, qpart, q_in, da0, da1, da2, db0, db1, db2, cos, sin, b2, a1, mid, normed, orep, *refs):
    pieces, (part, keep_o, send_o, out_o, w, dall, sem) = refs[:5], refs[5:]
    cs = piece_copies(offs, [p.at[:, :, pl.ds(HQ, 512)] for p in pieces], w, sem)
    for c in cs:
        c.start()
    cw = jnp.concatenate([cos[...], cos[...]], axis=1)
    sw = jnp.concatenate([sin[...], sin[...]], axis=1)
    both = []
    for i in range(2):
        own = jnp.concatenate([da0[i], db0[i]], axis=1)
        one = jnp.concatenate([da1[i], db1[i]], axis=1)
        two = jnp.concatenate([da2[i], db2[i]], axis=1)
        both.append(own + one.astype(F32) + two.astype(F32))
    dall[:, 0:256] = (both[0] * cw - half_swap(both[0]) * sw).astype(BF16)
    dall[:, 256:512] = both[1].astype(BF16)
    d = dall[...]
    mid_g = nt(d, b2[:, HQ:1280]).astype(BF16)
    mid_t = mid[...].astype(F32).T.astype(BF16)
    out_o[:, 0:256] = (2.0 * nn(mid_t[16:32], dall[:, 0:256])).astype(BF16)
    out_o[:, 256:512] = (2.0 * nn(mid_t[32:48], dall[:, 256:512])).astype(BF16)
    in_grads = nn(mid_g.astype(F32).T.astype(BF16)[16:48], normed[...])
    keep_and_send(place, keep_o, send_o, slice(0, 16), q_in[...])
    keep_and_send(place, keep_o, send_o, slice(16, 48), in_grads)
    keep_and_send(place, keep_o, send_o, slice(48, 64), orep[...])
    for c in cs:
        c.wait()
    for n in range(3):
        cols = slice(n * 512, (n + 1) * 512)
        part[:, cols] = (qpart[:, cols] + nt(d, w[cols, :]) + nn(mid_g, a1[:, cols])).astype(BF16)


def kv_back_call(place, offs, qpart, q_in, da, db, cos, sin, b2, a1, mid, normed, orep, w):
    return pl.pallas_call(
        kv_back_kernel,
        out_shape=(sds((TOK, D), BF16),) + (sds((64, 768), BF16),) * 2 + (sds((16, 512), BF16),),
        in_specs=[SM, SM] + [VM] * 15 + [HB] * 5,
        out_specs=(VM,) * 4,
        scratch_shapes=[
            pltpu.VMEM((D, 512), BF16),
            pltpu.VMEM((TOK, 512), BF16),
            pltpu.SemaphoreType.DMA((16,)),
        ],
        compiler_params=params(),
        cost_estimate=cost(),
        name="kv_back",
    )(place, offs, qpart, q_in, *da, *db, cos, sin, b2, a1, mid, normed, orep, *w)


def token_grad_kernel(tok, rg, own, other, gain, out):
    x = tok[...].astype(F32)
    inv = lax.rsqrt(jnp.mean(x * x, axis=-1, keepdims=True) + EPS)
    wv = (own[...].astype(F32) + other[...].astype(F32)) * gain[...]
    dot = jnp.mean(wv * x, axis=-1, keepdims=True)
    out[...] = (rg[...] + inv * wv - x * (inv * inv * inv * dot)).astype(BF16)


def token_grad_call(tok, rg, own, other, gain):
    return pl.pallas_call(
        token_grad_kernel,
        grid=(4,),
        out_shape=sds((TOK, D), BF16),
        in_specs=[row_block(D)] * 4 + [all_block(1, D)],
        out_specs=row_block(D),
        compiler_params=params(16),
        cost_estimate=cost(),
        name="token_grad",
    )(tok, rg, own, other, gain)


def pack_first_kernel(q, k, v, out):
    out[:, 0:768] = q[...]
    out[:, 768:1024] = k[...]
    out[:, 1024:1280] = v[...]


def pack_first_call(q, k, v):
    return pl.pallas_call(
        pack_first_kernel,
        out_shape=sds((96, 1280), BF16),
        in_specs=[VM] * 3,
        out_specs=VM,
        compiler_params=params(),
        cost_estimate=cost(),
        name="pack_qkv",
    )(q, k, v)


def pack_rest_kernel(o, g, u, d, yx, xy):
    yx[:, 0:HQ] = o[...]
    for i, w in enumerate((g, u, d)):
        yx[:, HQ + i * FA : HQ + (i + 1) * FA] = w[:, 0:FA]
        xy[:, i * FB : (i + 1) * FB] = w[:, FA:FH]


def pack_rest_call(o, g, u, d):
    return pl.pallas_call(
        pack_rest_kernel,
        out_shape=(
            sds((96, HQ + 3 * FA), BF16),
            sds((96, 3 * FB), BF16),
        ),
        in_specs=[VM] * 4,
        out_specs=(VM,) * 2,
        compiler_params=params(),
        cost_estimate=cost(),
        name="pack_rest",
    )(o, g, u, d)


def line_call(parts, head):
    n = parts[0].shape[1] - head

    def kernel(*refs):
        ins, outs = refs[:4], refs[4:]
        for i in range(4):
            if head:
                outs[0][i] = ins[i][:, 0:head]
            outs[-1][i] = ins[i][:, head:]

    shapes = (sds((4, 96, head), BF16),) * bool(head) + (sds((4, 96, n), BF16),)
    return pl.pallas_call(
        kernel,
        out_shape=shapes,
        in_specs=[VM] * 4,
        out_specs=(VM,) * len(shapes),
        compiler_params=params(),
        cost_estimate=cost(),
        name="line",
    )(*parts)


def own_half_kernel(idx, q, k, v, o, g, u, d, out):
    at = 0
    for ref in (q, k, v, o, g, u, d):
        n = ref.shape[2]
        out[:, at : at + n] = ref[0]
        at += n


def own_half_call(index, arrays):
    return pl.pallas_call(
        own_half_kernel,
        out_shape=sds((16, 7808), BF16),
        grid_spec=pltpu.PrefetchScalarGridSpec(
            num_scalar_prefetch=1,
            grid=(1,),
            in_specs=[
                pl.BlockSpec((1, 16, a.shape[2]), lambda i, idx: (idx[0], 0, 0)) for a in arrays
            ],
            out_specs=pl.BlockSpec((16, 7808), lambda i, idx: (0, 0)),
        ),
        compiler_params=params(),
        cost_estimate=cost(),
        name="pick_halves",
    )(index, *arrays)


def factors_kernel(
    idx, halves, aq, ak, av, ag, au, oo, do, a_qkv, b_qkv, a_gu, bg, bu, di, oi, oo2, do2
):
    for ref in (a_qkv, b_qkv, a_gu, bg, bu, di, oi, oo2, do2):
        ref[...] = jnp.zeros_like(ref)
    for i, ref in enumerate((aq, ak, av)):
        a_qkv[i * 16 : (i + 1) * 16] = ref[0]
    for i, ref in enumerate((ag, au)):
        a_gu[i * 16 : (i + 1) * 16] = ref[0]
    oo2[0:16] = 2 * oo[0]
    do2[0:16] = 2 * do[0]
    b_qkv[0:16, 0:768] = 2 * halves[:, 0:768]
    b_qkv[16:32, 768:1024] = 2 * halves[:, 768:1024]
    b_qkv[32:48, 1024:1280] = 2 * halves[:, 1024:1280]
    oi[0:16] = halves[:, 1280:2048]
    bg[0:16] = 2 * halves[:, 2048:3968]
    bu[16:32] = 2 * halves[:, 3968:5888]
    di[0:16] = halves[:, 5888:7808]


def factors_call(index, halves, arrays):
    widths = (D, 1280, D, FH, FH, FH, HQ, D, D)
    return pl.pallas_call(
        factors_kernel,
        out_shape=tuple(sds((128, w), BF16) for w in widths),
        grid_spec=pltpu.PrefetchScalarGridSpec(
            num_scalar_prefetch=1,
            grid=(1,),
            in_specs=[pl.BlockSpec((16, 7808), lambda i, idx: (0, 0))]
            + [pl.BlockSpec((1, 16, D), lambda i, idx: (idx[0], 0, 0))] * 7,
            out_specs=tuple(pl.BlockSpec((128, w), lambda i, idx: (0, 0)) for w in widths),
        ),
        compiler_params=params(),
        cost_estimate=cost(),
        name="factors",
    )(index, halves, *arrays)


def quarters_kernel(m, place, rep, got, *refs):
    parts, outs, buf = refs[:-5], refs[-5:-1], refs[-1]
    z = place[1]
    n_rep = rep.shape[0] // 16
    kept = (rep[...].astype(F32) + got[...].astype(F32)).astype(BF16)
    for i in range(n_rep):
        buf[:, i * 768 : (i + 1) * 768] = kept[i * 16 : (i + 1) * 16]
    at = n_rep * 768
    for p in parts:
        buf[:, at : at + p.shape[1]] = p[...]
        at += p.shape[1]
    if at < 4 * m:
        buf[:, at : 4 * m] = jnp.zeros((16, 4 * m - at), BF16)
    for k, out in enumerate(outs):
        quarter = lax.rem(z + k, 4)
        out[...] = buf[:, pl.ds(pl.multiple_of(quarter * m, 128), m)]


def quarters_call(m, place, rep, got, parts):
    def kernel(*refs):
        quarters_kernel(m, *refs)

    return pl.pallas_call(
        kernel,
        out_shape=(sds((16, m), BF16),) * 4,
        in_specs=[SM] + [VM] * (2 + len(parts)),
        out_specs=(VM,) * 4,
        scratch_shapes=[pltpu.VMEM((16, 4 * m), BF16)],
        compiler_params=params(6 if m == LATE else 58),
        cost_estimate=cost(),
        name="quarters",
    )(place, rep, got, *parts)


def pack_early_kernel(keep, got, g, u, d, out):
    kept = (keep[...].astype(F32) + got[...].astype(F32)).astype(BF16)
    for i in range(3):
        out[:, i * 768 : (i + 1) * 768] = kept[i * 16 : (i + 1) * 16]
    for i, ref in enumerate((g, u, d)):
        out[:, 2304 + i * FH : 2304 + (i + 1) * FH] = ref[...]
    out[:, 8064:8192] = jnp.zeros((16, 128), BF16)


def pack_early_call(keep, got, g, u, d):
    return pl.pallas_call(
        pack_early_kernel,
        out_shape=sds((16, 4 * EARLY), BF16),
        in_specs=[VM] * 5,
        out_specs=VM,
        compiler_params=params(),
        cost_estimate=cost(),
        name="pack_early",
    )(keep, got, g, u, d)


def quarter_kernel(place, total, out):
    out[:, 0:EARLY] = total[...]
    out[:, EARLY : EARLY + 128] = (
        jnp.full((16, 128), place[2], jnp.int32).astype(F32).astype(BF16)
    )


def quarter_call(place, total):
    return pl.pallas_call(
        quarter_kernel,
        out_shape=sds((16, EARLY + 128), BF16),
        in_specs=[SM, VM],
        out_specs=VM,
        compiler_params=params(),
        cost_estimate=cost(),
        name="quarter",
    )(place, total)


def sum_kernel(place, a, b, c, d, out):
    m = a.shape[1]
    total = a[...].astype(F32) + b[...].astype(F32) + c[...].astype(F32) + d[...].astype(F32)
    out[:, 0:m] = total.astype(BF16)
    out[:, m : m + 128] = jnp.full((16, 128), place[2], jnp.int32).astype(F32).astype(BF16)


def sum_call(place, parts):
    m = parts[0].shape[1]
    return pl.pallas_call(
        sum_kernel,
        out_shape=sds((16, m + 128), BF16),
        in_specs=[SM] + [VM] * 4,
        out_specs=VM,
        compiler_params=params(6),
        cost_estimate=cost(),
        name="sum_tokens",
    )(place, *parts)


def by_adapter_kernel(*refs):
    ins, out, total = refs[:-2], refs[-2], refs[-1]
    m = out.shape[2]
    total[...] = jnp.zeros_like(total)
    for r in ins:
        for k in range(r.shape[0]):
            adapter = jnp.max(r[k, :, m : m + 128].astype(F32)).astype(jnp.int32)
            total[adapter] += r[k, :, 0:m].astype(F32)
    out[...] = total[...].astype(BF16)


def by_adapter_call(parts, m):
    return pl.pallas_call(
        by_adapter_kernel,
        out_shape=sds((8, 16, m), BF16),
        in_specs=[VM] * len(parts),
        out_specs=VM,
        scratch_shapes=[pltpu.VMEM((8, 16, m), F32)],
        compiler_params=params(14),
        cost_estimate=cost(),
        name="by_adapter",
    )(*parts)


def spread(buf, outs, jobs, widths):
    at = 0
    for out, n in zip(outs, widths, strict=True):
        for c in range(2):
            out[:, :, c * n : (c + 1) * n] = buf[c, :, :, at : at + n].astype(F32)
        at += n


def unpack_early_kernel(src, *refs):
    outs, buf, sem = refs[:-2], refs[-2], refs[-1]
    copies = []
    for z in range(4):
        for c in range(2):
            copies.append(
                pltpu.make_async_copy(
                    src.at[2 * z + c], buf.at[c, :, :, pl.ds(z * EARLY, EARLY)], sem.at[2 * z + c]
                )
            )
    for c in copies:
        c.start()
    for c in copies:
        c.wait()
    spread(buf, outs, None, (768, 768, 768, FH, FH, FH))


def unpack_early_call(src):
    widths = (D, D, D, 2 * FH, 2 * FH, 2 * FH)
    return pl.pallas_call(
        unpack_early_kernel,
        out_shape=tuple(sds((8, 16, w), F32) for w in widths),
        in_specs=[HB],
        out_specs=(VM,) * 6,
        scratch_shapes=[pltpu.VMEM((2, 8, 16, 4 * EARLY), BF16), pltpu.SemaphoreType.DMA((8,))],
        compiler_params=params(),
        cost_estimate=cost(),
        name="unpack_early",
    )(src)


def unpack_late_kernel(place, *refs):
    srcs, outs, buf, sem = refs[:8], refs[8:-2], refs[-2], refs[-1]
    core, z = place[0], place[1]
    copies = []
    for i, src in enumerate(srcs):
        c = core if i < 4 else 1 - core
        at = lax.rem(z + REL[i % 4] + 4, 4) * LATE
        copies.append(
            pltpu.make_async_copy(
                src, buf.at[c, :, :, pl.ds(pl.multiple_of(at, 128), LATE)], sem.at[i]
            )
        )
    for c in copies:
        c.start()
    for c in copies:
        c.wait()
    spread(buf, outs, None, (768, 768, 768, 768, 768, 256, 256, 768))


def unpack_late_call(place, srcs):
    widths = (D, D, D, D, D, 512, 512, D)
    return pl.pallas_call(
        unpack_late_kernel,
        out_shape=tuple(sds((8, 16, w), F32) for w in widths),
        in_specs=[SM] + [HB] * 8,
        out_specs=(VM,) * 8,
        scratch_shapes=[pltpu.VMEM((2, 8, 16, 4 * LATE), BF16), pltpu.SemaphoreType.DMA((8,))],
        compiler_params=params(24),
        cost_estimate=cost(),
        name="unpack_late",
    )(place, *srcs)


YLIN = (0, 2, 1, 3)


def go_x(v, step):
    return lax.ppermute(v, "x", [(i, (i + step) % 4) for i in range(4)])


def go_y(v, step):
    return lax.ppermute(
        v, ("tensor", "yh"), [(YLIN[i], YLIN[(i + step) % 4]) for i in range(4)]
    )


def go_z(v, step):
    return lax.ppermute(v, "seq", [(i, (i + step) % 4) for i in range(4)])


def go_core(v):
    return lax.ppermute(v, "core", [(0, 1), (1, 0)])


def to_role(v):
    return lax.ppermute(v, ("tensor", "core"), [(1, 2), (2, 1)])


REL = (0, -1, 1, 2)


def near_line(shard, near):
    return (shard, near(shard, 1), near(shard, -1), near(shard, 2))


def ring_start(line, far):
    return (line, far(line, 1), far(line, -1))


def ring_halves(below, above):
    return below[:2], above[2:]


class Order:
    def __init__(self):
        self.last = ()

    def gate(self, v):
        return lax.optimization_barrier((v, self.last))[0]

    def done(self, v):
        v = self.gate(v)
        self.last = jax.tree.leaves(v)
        return v

    def run(self, step, *args):
        out = step(*self.gate(args))
        self.last = jax.tree.leaves(out)
        return out


def offsets(x, y, path):
    near = np.tile(np.array(REL, np.int32), 4)
    far = np.repeat(np.array(REL, np.int32), 4)
    if path == "yx":
        return ((x + far + 4) % 4) * 4 + (y + near + 4) % 4
    if path == "xy":
        return np.tile(np.arange(4, dtype=np.int32), 4) * 4 + (y + far + 4) % 4
    return np.repeat(np.arange(4, dtype=np.int32), 4) * 4 + (y + near + 4) % 4


def halo_back(grads):
    two, one, own = grads
    one = lax.ppermute(one, "seq", [(1, 0), (2, 1), (3, 2)])
    return (own, one, lax.ppermute(two, "seq", [(2, 0), (3, 1)]))


def shards(
    tokens,
    output_gradient,
    document_length_table,
    sequence_adapter_index,
    sequence_window_length,
    attention_norm_gain,
    feedforward_norm_gain,
    query_projection_weight,
    key_projection_weight,
    value_projection_weight,
    output_projection_weight,
    gate_projection_weight,
    up_projection_weight,
    down_projection_weight,
    query_adapter_first,
    query_adapter_second,
    key_adapter_first,
    key_adapter_second,
    value_adapter_first,
    value_adapter_second,
    output_adapter_first,
    output_adapter_second,
    gate_adapter_first,
    gate_adapter_second,
    up_adapter_first,
    up_adapter_second,
    down_adapter_first,
    down_adapter_second,
):
    z = lax.axis_index("seq")
    yl = lax.axis_index("tensor")
    x = lax.axis_index("x")
    y = lax.axis_index("yh") * 2 + yl
    core = lax.axis_index("core")
    same = core == yl

    o = Order()
    t = lambda v: v.swapaxes(1, 2)
    mine = lambda own, got: jnp.where(same, own, got)
    offs_yx, offs_xy, offs_o = (offsets(x, y, p) for p in ("yx", "xy", "o"))
    gain1 = attention_norm_gain[None, :]
    gain2 = feedforward_norm_gain[None, :]

    own_qkv = o.run(
        pack_first_call, query_projection_weight, key_projection_weight, value_projection_weight
    )
    got_qkv = to_role(own_qkv)
    own_yx, own_b = o.run(
        pack_rest_call,
        output_projection_weight,
        gate_projection_weight,
        up_projection_weight,
        down_projection_weight,
    )
    meta = jnp.concatenate(
        [document_length_table[0], sequence_adapter_index, sequence_window_length]
    )
    meta_other = go_core(meta)
    tok_other = go_core(tokens[0])
    near_qkv = near_line(o.run(mine, own_qkv, o.done(got_qkv)), go_y)
    own_halves = o.run(
        own_half_call,
        sequence_adapter_index,
        (
            query_adapter_second,
            key_adapter_second,
            value_adapter_second,
            output_adapter_first,
            gate_adapter_second,
            up_adapter_second,
            down_adapter_first,
        ),
    )
    line_qkv = o.run(lambda *v: line_call(v, 0)[0], *o.done(near_qkv))
    below_qkv, above_qkv = go_x(line_qkv, 1), go_x(line_qkv, -1)

    def tables(own, other):
        meta = mine(own, other)
        lengths, index, window = meta[:4], meta[4:5], meta[5]
        place = jnp.concatenate(
            [jnp.stack([core, z]), index, same[None]], dtype=jnp.int32
        )
        ends = jnp.cumsum(lengths, dtype=jnp.int32)
        begins = ends - lengths
        row = z * TOK + jnp.arange(TOK, dtype=jnp.int32)
        begin = jnp.max(jnp.where(row[:, None] >= begins[None, :], begins[None, :], 0), axis=1)
        low_key = (jnp.maximum(begin, row - window + 1) - (z * TOK - HALO))[None, :]
        lane = jnp.arange(128, dtype=jnp.int32) % HDIM
        frequency = ROPE_BASE ** (-((lane % 32).astype(F32) * (2.0 / HDIM)))
        angles = (row - begin).astype(F32)[:, None] * frequency[None, :]
        cos = jnp.cos(angles)
        sin = jnp.sin(angles) * jnp.where(lane < 32, -1.0, 1.0)[None, :]
        return index, place, low_key, cos, sin

    index, place, low_key, cos, sin = o.run(tables, meta, o.done(meta_other))
    got_halves, got_yx, got_b = (to_role(o.gate(v)) for v in (own_halves, own_yx, own_b))
    tok = o.run(mine, tokens[0], o.done(tok_other))
    halves = o.run(mine, own_halves, o.done(got_halves))
    a_qkv, b_qkv, a_gu, bg2, bu2, di_p, oi_p, oo2, do2 = o.run(
        factors_call,
        index,
        halves,
        (
            t(query_adapter_first),
            t(key_adapter_first),
            t(value_adapter_first),
            t(gate_adapter_first),
            t(up_adapter_first),
            output_adapter_second,
            down_adapter_second,
        ),
    )
    near_yx = near_line(o.run(mine, own_yx, o.done(got_yx)), go_y)
    own_b = o.run(mine, own_b, o.done(got_b))
    low, high = o.run(ring_halves, *o.done((below_qkv, above_qkv)))
    far_qkv = (go_x(low, 1), go_x(high, -1))
    line_b = lax.all_gather(o.gate(own_b), "x", axis=0)
    full_qkv = (line_qkv, below_qkv, above_qkv) + o.done(far_qkv)

    normed, q, kv0, mid_qkv = o.run(
        qkv_call, offs_yx, tok, gain1, a_qkv, b_qkv, cos, sin, full_qkv
    )
    kv1 = lax.ppermute(kv0, "seq", [(0, 1), (1, 2), (2, 3)])
    kv2 = lax.ppermute(kv0, "seq", [(0, 2), (1, 3)])
    line_o, line_a = o.run(lambda *v: line_call(v, HQ), *o.done(near_yx))
    full_o = lax.all_gather(line_o, "x", axis=0, tiled=True)
    line_b = o.done(line_b)
    below_b, above_b = go_y(line_b, 1), go_y(line_b, -1)
    kv1, kv2 = o.done((kv1, kv2))
    line_a = o.gate(line_a)
    below_a, above_a = go_x(line_a, 1), go_x(line_a, -1)
    og_other = go_core(o.gate(output_gradient[0]))
    att, lse = o.run(attend_call, q, low_key, kv2, kv1, kv0)
    og_other = o.done(og_other)
    low, high = o.run(ring_halves, *o.done((below_b, above_b)))
    far_b = (go_y(low, 1), go_y(high, -1))
    full_o = o.done(full_o)
    attn_part, mid_att = o.run(out_proj_call, offs_o, att, oi_p, oo2, full_o)
    attn_other = go_core(attn_part)
    low, high = o.run(ring_halves, *o.done((below_a, above_a)))
    far_a = (go_x(low, 1), go_x(high, -1))
    resid, nf, mid_gu = o.run(ffn_in_call, tok, attn_part, o.done(attn_other), gain2, a_gu)
    full_b = (line_b, below_b, above_b) + o.done(far_b)
    og, fg, mid_dg = o.run(cot_call, place, output_gradient[0], og_other, do2)
    full_a = (line_a, below_a, above_a) + o.done(far_a)
    ffn_part, nfg_part, keep_e, send_e, g_out, u_out, d_in = o.run(
        ffn_call,
        place, offs_yx, offs_xy, nf, fg, mid_gu, mid_dg, bg2, bu2, di_p, a_gu, do2, full_a, full_b,
    )

    nfg_other = go_core(nfg_part)
    got_e = go_core(send_e)
    packed = o.run(pack_early_call, keep_e, o.done(got_e), g_out, u_out, d_in)
    summed = lax.psum_scatter(packed, "seq", scatter_dimension=1, tiled=True)
    head = np.arange(16)
    head = np.where(head % 8 < 6, 6 * (head // 8) + head % 8, -1)
    hsel = jnp.asarray((np.arange(HQ) // HDIM)[None, :] == head[:, None], BF16)
    rg, do, delta, rep_o, o_in = o.run(
        out_back_call,
        offs_o, og, resid, nfg_part, o.done(nfg_other), gain2, oi_p, oo2, mid_att, att, hsel, full_o,
    )
    stats = (lse, delta, low_key, kv2, kv1, kv0)
    dqa, *da = o.run(lambda *v: attend_back_call(0, *v), q, do, *stats)
    near = near_line(o.run(quarter_call, place, o.done(summed)), go_y)
    ra = halo_back(da)
    dqb, *db = o.run(lambda *v: attend_back_call(1, *v), q, do, *stats)
    ra = o.done(ra)
    plane = lax.all_gather(o.run(lambda *v: jnp.stack(v), *o.done(near)), "x", axis=0, tiled=True)
    rb = halo_back(db)
    ffn_other = go_core(o.gate(ffn_part))
    qpart, q_in, q_out = o.run(
        q_back_call, offs_yx, dqa, dqb, cos, sin, b_qkv, a_qkv, mid_qkv, normed, full_qkv
    )
    rb = o.done(rb)
    na_part, keep_l, send_l, kv_out = o.run(
        kv_back_call,
        place, offs_yx, qpart, q_in, ra, rb, cos, sin, b_qkv, a_qkv, mid_qkv, normed, rep_o, full_qkv,
    )
    na_other = go_core(na_part)
    got_l = go_core(send_l)
    ffn_other = o.done(ffn_other)

    out = o.run(
        lambda r, a, b: (r + RS * (a.astype(F32) + b.astype(F32))).astype(BF16),
        resid, ffn_part, ffn_other,
    )
    out_other = to_role(out)
    quarters = o.run(
        lambda *v: quarters_call(LATE, place, v[0], v[1], v[2:]),
        keep_l, o.done(got_l), q_out, kv_out, o_in,
    )
    sent = [go_z(quarters[k], k) for k in (1, 2, 3)]
    dense = o.run(lambda v: by_adapter_call([v], EARLY), o.done(plane))
    early = lax.all_gather(dense, ("seq", "core"), axis=0)
    near = near_line(o.run(sum_call, place, [quarters[0]] + o.done(sent)), go_y)
    na_other = o.done(na_other)
    line = o.run(lambda *v: jnp.stack(v), *o.done(near))
    lines = [go_x(line, 1), go_x(line, -1), go_x(line, 2)]
    token_grad = o.run(token_grad_call, tok, rg, na_part, na_other, gain1)
    tg_other = to_role(token_grad)
    dense = o.run(lambda *v: by_adapter_call(v, LATE), line, *o.done(lines))
    out_other = o.done(out_other)
    zs = [go_z(dense, 1), go_z(dense, -1), go_z(dense, 2)]
    g_in, u_in, d_out, g_out, u_out, d_in = o.run(unpack_early_call, o.done(early))
    output = o.run(mine, out, out_other)
    token_grad = o.run(mine, token_grad, o.done(tg_other))
    zs = o.done(zs)
    cores = [go_core(v) for v in [dense] + zs]
    q_in, k_in, v_in, o_out, q_out, k_out, v_out, o_in = o.run(
        unpack_late_call, place, [dense] + zs + o.done(cores)
    )
    return (
        output[None],
        token_grad[None],
        t(q_in),
        q_out,
        t(k_in),
        k_out,
        t(v_in),
        v_out,
        o_in,
        o_out,
        t(g_in),
        g_out,
        t(u_in),
        u_out,
        d_in,
        d_out,
    )


def solution(mesh):
    fine = Mesh(mesh.devices.reshape(4, 2, 4, 2, 2), ("seq", "tensor", "x", "yh", "core"))
    fsdp = ("x", "yh", "core")
    weight = P(fsdp, "tensor")
    half = P(None, None, "tensor")
    return jax.shard_map(
        shards,
        mesh=fine,
        in_specs=(
            P(fsdp, "seq", None),
            P(fsdp, "seq", None),
            P(fsdp, None),
            P(fsdp),
            P(fsdp),
            P(),
            P(),
        )
        + (weight,) * 7
        + (P(), half, P(), half, P(), half, half, P(), P(), half, P(), half, half, P()),
        out_specs=(P(fsdp, "seq", None), P(fsdp, "seq", None)) + (P(),) * 14,
        check_vma=False,
    )
```

```python
import jax
import jax.numpy as jnp
import numpy as np
from jax import lax
from jax.experimental import pallas as pl
from jax.experimental.pallas import tpu as pltpu
from jax.sharding import Mesh
from jax.sharding import PartitionSpec as P

F32 = jnp.float32
BF16 = jnp.bfloat16
EPS = 1e-05
ROPE_BASE = 10000.0
RS = 1.4 / 52.0**0.5
MASKED = -1e30
TOK = 512
D = 1536
DX = D + 128
HQ = 768
HK = 256
HDIM = 64
SPAN = 1280
RT = 256
HALO = 1024
FH = 1920
FA, FB = 896, 1024
EARLY = 2048
LATE = 1280


def nn(a, b):
    return lax.dot_general(a, b, (((1,), (0,)), ((), ())), preferred_element_type=F32)


def nt(a, b):
    return lax.dot_general(a, b, (((1,), (1,)), ((), ())), preferred_element_type=F32)


VM = pl.BlockSpec(memory_space=pltpu.VMEM)
SM = pl.BlockSpec(memory_space=pltpu.SMEM)
HB = pl.BlockSpec(memory_space=pl.ANY)


def row_block(width):
    return pl.BlockSpec((128, width), lambda i: (i, 0))


def all_block(rows, width):
    return pl.BlockSpec((rows, width), lambda i: (0, 0))


def params(mib=58):
    return pltpu.CompilerParams(vmem_limit_bytes=mib * 1024 * 1024)


def cost():
    return pl.CostEstimate(flops=1, bytes_accessed=1, transcendentals=0)


def sds(shape, dtype):
    return jax.ShapeDtypeStruct(shape, dtype)


def piece_copies(offs, refs, dst, sems):
    copies = []
    for ref in refs:
        for k in range(ref.shape[0]):
            row = pl.multiple_of(offs[len(copies)] * 96, 96)
            copies.append(
                pltpu.make_async_copy(ref.at[k], dst.at[pl.ds(row, 96)], sems.at[len(copies)])
            )
    return copies


def half_swap(v):
    lane = lax.broadcasted_iota(jnp.int32, v.shape, 1)
    width = v.shape[1]
    from_low = pltpu.roll(v, 32, 1)
    from_high = pltpu.roll(v, width - 32, 1)
    return jnp.where((lane % 64) < 32, from_high, from_low)


def qkv_kernel(offs, tok, gain, a1, b2, cos, sin, *refs):
    pieces, (normed_o, q_o, kv_o, mid_o, w, sem) = refs[:5], refs[5:]
    cs = piece_copies(offs, pieces, w, sem)
    for c in cs:
        c.start()
    for r in range(4):
        rows = pl.ds(r * 128, 128)
        x = tok[rows, :].astype(F32)
        inv = lax.rsqrt(jnp.mean(x * x, axis=-1, keepdims=True) + EPS)
        normed_o[rows, :] = (x * inv * gain[...]).astype(BF16)
    normed = normed_o[...]
    mid = nt(normed, a1[...]).astype(BF16)
    mid_o[...] = mid
    for c in cs:
        c.wait()
    cw = jnp.concatenate([cos[...], cos[...]], axis=1)
    sw = jnp.concatenate([sin[...], sin[...]], axis=1)
    for n in (3, 4, 0, 1, 2):
        cols = slice(n * 256, (n + 1) * 256)
        acc = nn(normed, w[:, cols]) + nn(mid, b2[:, cols])
        if n < 4:
            acc = acc * cw + half_swap(acc) * sw
        if n < 3:
            q_o[:, cols] = (acc.astype(BF16).astype(F32) * 0.125).astype(BF16)
        else:
            kv_o[n - 3] = acc.astype(BF16)


def qkv_call(offs, tok, gain, a1, b2, cos, sin, w):
    return pl.pallas_call(
        qkv_kernel,
        out_shape=(
            sds((TOK, D), BF16),
            sds((TOK, HQ), BF16),
            sds((2, TOK, HK), BF16),
            sds((TOK, 128), BF16),
        ),
        in_specs=[SM] + [VM] * 6 + [HB] * 5,
        out_specs=(VM,) * 4,
        scratch_shapes=[pltpu.VMEM((D, 1280), BF16), pltpu.SemaphoreType.DMA((16,))],
        compiler_params=params(),
        cost_estimate=cost(),
        name="norm_qkv",
    )(offs, tok, gain, a1, b2, cos, sin, *w)


HEADS_OF_PAIR = ((0, 0, 0), (0, 1, 0), (1, 0, 0), (1, 1, 1), (2, 0, 1), (2, 1, 1))


def bias_of(lo, r):
    key = lax.broadcasted_iota(jnp.int32, (SPAN, RT), 0) + r * RT
    row = lax.broadcasted_iota(jnp.int32, (SPAN, RT), 1) + r * RT + HALO
    return jnp.where((key >= lo) & (key <= row), 0.0, MASKED)


def variants(dst, src, other=0.0):
    lane = lax.broadcasted_iota(jnp.int32, src.shape, 1)
    srcf = src.astype(F32)
    rolled = pltpu.roll(srcf, 64, 1)
    low = lane < 64
    dst[0] = jnp.where(low, srcf, other).astype(BF16)
    dst[1] = jnp.where(low, other, rolled).astype(BF16)
    dst[2] = jnp.where(low, rolled, other).astype(BF16)
    dst[3] = jnp.where(low, other, srcf).astype(BF16)


def in_half(v, half, want):
    return v if half == want else pltpu.roll(v, 64, 1)


def attend_kernel(q, lo, kv2, kv1, kv0, out, lse, kvar, vvar, bias):
    r = pl.program_id(1)
    lane = lax.broadcasted_iota(jnp.int32, (RT, 128), 1)
    low = lane < 64

    @pl.when(r == 0)
    def _():
        variants(kvar, jnp.concatenate([kv2[0], kv1[0], kv0[0]], axis=0))
        variants(vvar, jnp.concatenate([kv2[1], kv1[1], kv0[1]], axis=0), 1.0)

    key = lax.broadcasted_iota(jnp.int32, (RT, SPAN), 1) + r * RT
    row = lax.broadcasted_iota(jnp.int32, (RT, SPAN), 0) + r * RT + HALO
    bias[...] = jnp.where((key >= lo[...]) & (key <= row), 0.0, MASKED)
    keys = pl.ds(pl.multiple_of(r * RT, RT), SPAN)
    stats = jnp.zeros((RT, 128), F32)
    for tile in range(3):
        qt = q[:, tile * 128 : (tile + 1) * 128]
        pair = []
        for i in (2 * tile, 2 * tile + 1):
            _, half, kv = HEADS_OF_PAIR[i]
            s = nt(qt, kvar[2 * kv + half, keys, :]) + bias[...]
            m = jnp.max(s, axis=1, keepdims=True)
            e = jnp.exp(s - m).astype(BF16)
            o = nn(e, vvar[2 * kv + half, keys, :])
            total = o[:, 64:65] if half == 0 else o[:, 0:1]
            stats = jnp.where(lane == i, m + jnp.log(total), stats)
            pair.append(o)
        total = pltpu.roll(jnp.where(low, pair[1], pair[0]), 64, 1)
        out[:, tile * 128 : (tile + 1) * 128] = (jnp.where(low, pair[0], pair[1]) / total).astype(BF16)
    lse[...] = stats.T[0:8]


def attend_call(q, lo, kv2, kv1, kv0):
    kvspec = pl.BlockSpec((2, TOK, 128), lambda p, r: (0, 0, p))
    return pl.pallas_call(
        attend_kernel,
        grid=(2, 2),
        out_shape=(sds((TOK, HQ), BF16), sds((16, TOK), F32)),
        in_specs=[
            pl.BlockSpec((RT, 384), lambda p, r: (r, p)),
            pl.BlockSpec((RT, 1), lambda p, r: (r, 0)),
            kvspec,
            kvspec,
            kvspec,
        ],
        out_specs=(
            pl.BlockSpec((RT, 384), lambda p, r: (r, p)),
            pl.BlockSpec((8, RT), lambda p, r: (p, r)),
        ),
        scratch_shapes=[
            pltpu.VMEM((4, HALO + TOK, 128), BF16),
            pltpu.VMEM((4, HALO + TOK, 128), BF16),
            pltpu.VMEM((RT, SPAN), F32),
        ],
        compiler_params=params(),
        cost_estimate=cost(),
        name="attend",
    )(q, lo.T, kv2, kv1, kv0)


def attend_back_kernel(
    q, do, lse, delta, lo, kv2, kv1, kv0, dq, d2, d1, d0, kvar, vvar, kt, bias, dqt, dk_acc, dv_acc
):
    r = pl.program_id(1)

    @pl.when(r == 0)
    def _():
        kcat = jnp.concatenate([kv2[0], kv1[0], kv0[0]], axis=0)
        variants(kvar, kcat)
        kt[...] = kcat.astype(F32).T.astype(BF16)
        vcat = jnp.concatenate([kv2[1], kv1[1], kv0[1]], axis=0)
        variants(vvar, vcat)
        for ref in (dk_acc, dv_acc):
            ref[...] = jnp.zeros_like(ref)

    bias[...] = bias_of(lo[...], r)
    keys = pl.ds(pl.multiple_of(r * RT, RT), SPAN)
    low = lax.broadcasted_iota(jnp.int32, (RT, 128), 1) < 64
    for u in range(2):
        ps, dss, qs, dos = [], [], [], []
        for i in range(3 * u, 3 * u + 3):
            cols = slice((i // 2) * 128, (i // 2 + 1) * 128)
            half = i % 2
            qt = q[:, cols]
            dt = do[:, cols]
            keep = low if u == 0 else ~low
            qs.append(jnp.where(keep, in_half(qt.astype(F32), half, u), 0.0).astype(BF16))
            dos.append(jnp.where(keep, in_half(dt.astype(F32), half, u), 0.0).astype(BF16))
            s = nt(kvar[2 * u + half, keys, :], qt) + bias[...]
            p = jnp.exp(s - lse[i : i + 1, :])
            dp = nt(vvar[2 * u + half, keys, :], dt)
            dss.append((p * (dp - delta[i : i + 1, :])).astype(BF16))
            ps.append(p.astype(BF16))
        ds = jnp.concatenate(dss, axis=1)
        dv_acc[keys, :] += nn(jnp.concatenate(ps, axis=1), jnp.concatenate(dos, axis=0))
        dk_acc[keys, :] += nn(ds, jnp.concatenate(qs, axis=0))
        dqu = nn(kt[u * 64 : (u + 1) * 64, keys], ds)
        for g in range(3):
            i = 3 * u + g
            dqt[i * 64 : (i + 1) * 64, :] = dqu[:, g * RT : (g + 1) * RT]
    dq[...] = dqt[...].T * 0.125

    @pl.when(r == 1)
    def _():
        dk, dv = dk_acc[...], dv_acc[...]
        d2[0] = dk[0:512].astype(BF16)
        d2[1] = dv[0:512].astype(BF16)
        d1[0] = dk[512:1024].astype(BF16)
        d1[1] = dv[512:1024].astype(BF16)
        d0[0] = dk[1024:1536]
        d0[1] = dv[1024:1536]


def attend_back_call(p, q, do, lse, delta, lo, kv2, kv1, kv0):
    kvspec = pl.BlockSpec((2, TOK, 128), lambda i, r: (0, 0, p))
    rowspec = pl.BlockSpec((RT, 384), lambda i, r: (r, p))
    statspec = pl.BlockSpec((8, RT), lambda i, r: (p, r))
    kvout = pl.BlockSpec((2, TOK, 128), lambda i, r: (0, 0, 0))
    acc = pltpu.VMEM((HALO + TOK, 128), F32)
    return pl.pallas_call(
        attend_back_kernel,
        grid=(1, 2),
        out_shape=(
            sds((TOK, 384), F32),
            sds((2, TOK, 128), BF16),
            sds((2, TOK, 128), BF16),
            sds((2, TOK, 128), F32),
        ),
        in_specs=[
            rowspec,
            rowspec,
            statspec,
            statspec,
            pl.BlockSpec((1, RT), lambda i, r: (0, r)),
            kvspec,
            kvspec,
            kvspec,
        ],
        out_specs=(pl.BlockSpec((RT, 384), lambda i, r: (r, 0)), kvout, kvout, kvout),
        scratch_shapes=[
            pltpu.VMEM((4, HALO + TOK, 128), BF16),
            pltpu.VMEM((4, HALO + TOK, 128), BF16),
            pltpu.VMEM((128, HALO + TOK), BF16),
            pltpu.VMEM((SPAN, RT), F32),
            pltpu.VMEM((384, RT), F32),
            acc,
            acc,
        ],
        compiler_params=params(),
        cost_estimate=cost(),
        name="attend_back",
    )(q, do, lse, delta, lo, kv2, kv1, kv0)


def out_proj_kernel(offs, att, oi, oo2, wo, part, mid_o, w, sem):
    cs = piece_copies(offs, (wo,), w, sem)
    for c in cs:
        c.start()
    a = att[...]
    mid = nt(a, oi[...]).astype(BF16)
    mid_o[...] = mid
    for c in cs:
        c.wait()
    for n in range(3):
        cols = slice(n * 512, (n + 1) * 512)
        part[:, cols] = (nt(a, w[cols, :]) + nn(mid, oo2[:, cols])).astype(BF16)


def out_proj_call(offs, att, oi, oo2, wo):
    return pl.pallas_call(
        out_proj_kernel,
        out_shape=(sds((TOK, D), BF16), sds((TOK, 128), BF16)),
        in_specs=[SM] + [VM] * 3 + [HB],
        out_specs=(VM, VM),
        scratch_shapes=[pltpu.VMEM((D, HQ), BF16), pltpu.SemaphoreType.DMA((16,))],
        compiler_params=params(),
        cost_estimate=cost(),
        name="out_proj",
    )(offs, att, oi, oo2, wo)


def ffn_in_kernel(tok, own, other, gain, a_gu, resid_o, nf_o, mid_o):
    branch = own[...].astype(F32) + other[...].astype(F32)
    x = tok[...].astype(F32) + RS * branch
    resid_o[...] = x
    inv = lax.rsqrt(jnp.mean(x * x, axis=-1, keepdims=True) + EPS)
    nf_o[...] = (x * inv * gain[...]).astype(BF16)
    mid_o[...] = nt(nf_o[...], a_gu[...]).astype(BF16)


def ffn_in_call(tok, own, other, gain, a_gu):
    return pl.pallas_call(
        ffn_in_kernel,
        grid=(4,),
        out_shape=(sds((TOK, D), F32), sds((TOK, D), BF16), sds((TOK, 128), BF16)),
        in_specs=[row_block(D)] * 3 + [all_block(1, D), all_block(128, D)],
        out_specs=(row_block(D), row_block(D), row_block(128)),
        compiler_params=params(16),
        cost_estimate=cost(),
        name="ffn_norm",
    )(tok, own, other, gain, a_gu)


def cot_kernel(place, own, other, do2, og_o, fg_o, mid_o):
    @pl.when(place[3] == 1)
    def _():
        og_o[...] = own[...]

    @pl.when(place[3] == 0)
    def _():
        og_o[...] = other[...]

    fg_o[...] = (RS * og_o[...].astype(F32)).astype(BF16)
    mid_o[...] = nt(fg_o[...], do2[...]).astype(BF16)


def cot_call(place, own, other, do2):
    return pl.pallas_call(
        cot_kernel,
        out_shape=(sds((TOK, D), BF16), sds((TOK, D), BF16), sds((TOK, 128), BF16)),
        in_specs=[SM] + [VM] * 3,
        out_specs=(VM,) * 3,
        compiler_params=params(16),
        cost_estimate=cost(),
        name="branch_cotangent",
    )(place, own, other, do2)


SPLIT = ((0, FA, 0, 0, FA), (1, FB, FA, 0, FB))
NCUT = ((0, 512), (512, 1024), (1024, DX))


def keep_and_send(place, keep, send, rows, full):
    low, high = full[:, 0:768].astype(BF16), full[:, 768:1536].astype(BF16)

    @pl.when(place[0] == 0)
    def _():
        keep[rows, :] = low
        send[rows, :] = high

    @pl.when(place[0] == 1)
    def _():
        keep[rows, :] = high
        send[rows, :] = low


def ffn_kernel(split, place, offs_a, offs_b, nf, fg, mid_gu, mid_dg, bg, bu, di, a_gu_h, do2_h, *refs):
    pa, pb = refs[:5], refs[5:10]
    part_f, part_n, keep_o, send_o, gout, uout, din = refs[10:17]
    wa, wb, xn, xf, accf, accn, a_gu, do2, sem_a, sem_b, sem = refs[17:]

    def adapter_rows(w, start, total, at):
        blk = pl.ds(start, total)
        return [
            pltpu.make_async_copy(src.at[:, blk], w.at[pl.ds(D, 128), pl.ds(k * total, total)], sem.at[at + k])
            for k, src in enumerate((bg, bu, di))
        ]

    first = piece_copies(offs_a, pa, wa, sem_a) + adapter_rows(wa, 0, FA, 0)
    inputs = [
        pltpu.make_async_copy(nf, xn.at[:, pl.ds(0, D)], sem.at[6]),
        pltpu.make_async_copy(mid_gu, xn.at[:, pl.ds(D, 128)], sem.at[7]),
        pltpu.make_async_copy(fg, xf.at[:, pl.ds(0, D)], sem.at[8]),
        pltpu.make_async_copy(mid_dg, xf.at[:, pl.ds(D, 128)], sem.at[9]),
    ]
    for c in inputs + first:
        c.start()
    for c in inputs:
        c.wait()
    mid_t = xn[:, D:DX].astype(F32).T.astype(BF16)[0:32]
    dg_t = xf[:, D:DX].astype(F32).T.astype(BF16)[0:16]
    for c in first:
        c.wait()
    second = piece_copies(offs_b, pb, wb, sem_b) + adapter_rows(wb, FA, FB, 3)
    closing = [
        pltpu.make_async_copy(a_gu_h, a_gu, sem.at[10]),
        pltpu.make_async_copy(do2_h, do2, sem.at[11]),
    ]
    for c in second + closing:
        c.start()
    for w, total, start, at, n in split:
        if w == 0:
            w = wa
        else:
            w = wb
            if at == 0:
                for c in second:
                    c.wait()
        blk = slice(start, start + n)
        gc, uc, dc = (slice(k * total + at, k * total + at + n) for k in range(3))
        if n == total:
            gu = nn(xn[...], w[:, 0 : 2 * n])
            g, u = gu[:, 0:n], gu[:, n : 2 * n]
        else:
            g = nn(xn[...], w[:, gc])
            u = nn(xn[...], w[:, uc])
        hg = nn(xf[...], w[:, dc])
        sig = 1.0 / (1.0 + jnp.exp(-g))
        si = g * sig
        hid = (si * u).astype(BF16)
        gg = (hg * u * (sig * (1.0 + g * (1.0 - sig)))).astype(BF16)
        ug = (hg * si).astype(BF16)
        both = jnp.concatenate([gg, ug], axis=1)
        terms = 2.0 * nn(mid_t, both)
        gout[:, blk] = terms[0:16, 0:n].astype(BF16)
        uout[:, blk] = terms[16:32, n : 2 * n].astype(BF16)
        din[:, blk] = nn(dg_t, hid).astype(BF16)
        for c0, c1 in NCUT:
            cols = slice(c0, c1)
            f = nt(hid, w[cols, dc])
            if n == total:
                d = nt(both, w[cols, 0 : 2 * n])
            else:
                d = nt(gg, w[cols, gc]) + nt(ug, w[cols, uc])
            if start == 0:
                accf[:, cols] = f
                accn[:, cols] = d
            else:
                accf[:, cols] += f
                accn[:, cols] += d
    midd, midg = accf[:, D:DX], accn[:, D:DX]
    midd_b = midd.astype(BF16)
    midg_b = midg.astype(BF16)
    for c in closing:
        c.wait()
    for c0 in range(0, D, 512):
        cols = slice(c0, c0 + 512)
        part_n[:, cols] = (accn[:, cols] + nn(midg_b, a_gu[:, cols])).astype(BF16)
        part_f[:, cols] = (accf[:, cols] + nn(midd_b, do2[:, cols])).astype(BF16)
    gu_in = nn(midg.T.astype(BF16)[0:32], xn[:, 0:D])
    d_out = 2.0 * nn(midd.T.astype(BF16)[0:16], xf[:, 0:D])
    keep_and_send(place, keep_o, send_o, slice(0, 32), gu_in)
    keep_and_send(place, keep_o, send_o, slice(32, 48), d_out)


def ffn_call(place, offs_a, offs_b, nf, fg, mid_gu, mid_dg, bg, bu, di, a_gu, do2, wa, wb):
    def kernel(*refs):
        ffn_kernel(SPLIT, *refs)

    return pl.pallas_call(
        kernel,
        out_shape=(sds((TOK, D), BF16),) * 2
        + (sds((48, 768), BF16),) * 2
        + (sds((16, FH), BF16),) * 3,
        in_specs=[SM, SM, SM] + [HB] * 19,
        out_specs=(VM,) * 7,
        scratch_shapes=[
            pltpu.VMEM((DX, 3 * FA), BF16),
            pltpu.VMEM((DX, 3 * FB), BF16),
            pltpu.VMEM((TOK, DX), BF16),
            pltpu.VMEM((TOK, DX), BF16),
            pltpu.VMEM((TOK, DX), F32),
            pltpu.VMEM((TOK, DX), F32),
            pltpu.VMEM((128, D), BF16),
            pltpu.VMEM((128, D), BF16),
            pltpu.SemaphoreType.DMA((16,)),
            pltpu.SemaphoreType.DMA((16,)),
            pltpu.SemaphoreType.DMA((12,)),
        ],
        compiler_params=params(),
        cost_estimate=cost(),
        name="ffn_both",
    )(place, offs_a, offs_b, nf, fg, mid_gu, mid_dg, bg, bu, di, a_gu, do2, *wa, *wb)


def out_back_kernel(
    offs, og, resid, own, other, gain, oi, oo2, mid_att, att, hsel, wo,
    rg_o, do_o, delta_o, rep_o, oin_o, w, abg, sem,
):
    cs = piece_copies(offs, (wo,), w, sem)
    for c in cs:
        c.start()
    for r in range(4):
        rows = pl.ds(r * 128, 128)
        x = resid[rows, :]
        inv = lax.rsqrt(jnp.mean(x * x, axis=-1, keepdims=True) + EPS)
        wv = (own[rows, :].astype(F32) + other[rows, :].astype(F32)) * gain[...]
        dot = jnp.mean(wv * x, axis=-1, keepdims=True)
        rg = og[rows, :].astype(F32) + inv * wv - x * (inv * inv * inv * dot)
        rg_o[rows, :] = rg
        abg[rows, :] = (RS * rg).astype(BF16)
    g = abg[...]
    mid_g = nt(g, oo2[...]).astype(BF16)
    for c in cs:
        c.wait()
    delta = jnp.zeros((16, TOK), F32)
    for n in range(3):
        cols = slice(n * 256, (n + 1) * 256)
        dd = (nn(g, w[:, cols]) + nn(mid_g, oi[:, cols])).astype(BF16)
        do_o[:, cols] = dd
        prod = dd.astype(F32) * att[:, cols].astype(F32)
        high = prod.astype(BF16)
        low = (prod - high.astype(F32)).astype(BF16)
        delta = delta + nt(hsel[:, cols], high) + nt(hsel[:, cols], low)
    delta_o[...] = delta
    o_out = 2.0 * nn(mid_att[...].astype(F32).T.astype(BF16)[0:16], g)
    rep_o[...] = o_out.astype(BF16)
    oin_o[...] = nn(mid_g.astype(F32).T.astype(BF16)[0:16], att[...]).astype(BF16)


def out_back_call(offs, og, resid, own, other, gain, oi, oo2, mid_att, att, hsel, wo):
    return pl.pallas_call(
        out_back_kernel,
        out_shape=(
            sds((TOK, D), F32),
            sds((TOK, HQ), BF16),
            sds((16, TOK), F32),
            sds((16, D), BF16),
            sds((16, HQ), BF16),
        ),
        in_specs=[SM] + [VM] * 10 + [HB],
        out_specs=(VM,) * 5,
        scratch_shapes=[
            pltpu.VMEM((D, HQ), BF16),
            pltpu.VMEM((TOK, D), BF16),
            pltpu.SemaphoreType.DMA((16,)),
        ],
        compiler_params=params(),
        cost_estimate=cost(),
        name="out_proj_back",
    )(offs, og, resid, own, other, gain, oi, oo2, mid_att, att, hsel, wo)


def q_back_kernel(offs, dq0, dq1, cos, sin, b2, a1, mid, normed, *refs):
    pieces, (part, in_o, out_o, w, dall, sem) = refs[:5], refs[5:]
    cs = piece_copies(offs, [p.at[:, :, pl.ds(0, HQ)] for p in pieces], w, sem)
    for c in cs:
        c.start()
    cw = jnp.concatenate([cos[...], cos[...]], axis=1)
    sw = jnp.concatenate([sin[...], sin[...]], axis=1)
    dq = jnp.concatenate([dq0[...], dq1[...]], axis=1)
    for n in range(3):
        g = dq[:, n * 256 : (n + 1) * 256]
        dall[:, n * 256 : (n + 1) * 256] = (g * cw - half_swap(g) * sw).astype(BF16)
    d = dall[...]
    mid_g = nt(d, b2[:, 0:HQ]).astype(BF16)
    mid_t = mid[...].astype(F32).T.astype(BF16)
    out_o[...] = (2.0 * nn(mid_t[0:16], d)).astype(BF16)
    in_o[...] = nn(mid_g.astype(F32).T.astype(BF16)[0:16], normed[...]).astype(BF16)
    for c in cs:
        c.wait()
    for n in range(3):
        cols = slice(n * 512, (n + 1) * 512)
        part[:, cols] = nt(d, w[cols, :]) + nn(mid_g, a1[:, cols])


def q_back_call(offs, dq0, dq1, cos, sin, b2, a1, mid, normed, w):
    return pl.pallas_call(
        q_back_kernel,
        out_shape=(sds((TOK, D), F32), sds((16, D), BF16), sds((16, HQ), BF16)),
        in_specs=[SM] + [VM] * 8 + [HB] * 5,
        out_specs=(VM,) * 3,
        scratch_shapes=[
            pltpu.VMEM((D, HQ), BF16),
            pltpu.VMEM((TOK, HQ), BF16),
            pltpu.SemaphoreType.DMA((16,)),
        ],
        compiler_params=params(),
        cost_estimate=cost(),
        name="q_back",
    )(offs, dq0, dq1, cos, sin, b2, a1, mid, normed, *w)


def kv_back_kernel(place, offs, qpart, q_in, da0, da1, da2, db0, db1, db2, cos, sin, b2, a1, mid, normed, orep, *refs):
    pieces, (part, keep_o, send_o, out_o, w, dall, sem) = refs[:5], refs[5:]
    cs = piece_copies(offs, [p.at[:, :, pl.ds(HQ, 512)] for p in pieces], w, sem)
    for c in cs:
        c.start()
    cw = jnp.concatenate([cos[...], cos[...]], axis=1)
    sw = jnp.concatenate([sin[...], sin[...]], axis=1)
    both = []
    for i in range(2):
        own = jnp.concatenate([da0[i], db0[i]], axis=1)
        one = jnp.concatenate([da1[i], db1[i]], axis=1)
        two = jnp.concatenate([da2[i], db2[i]], axis=1)
        both.append(own + one.astype(F32) + two.astype(F32))
    dall[:, 0:256] = (both[0] * cw - half_swap(both[0]) * sw).astype(BF16)
    dall[:, 256:512] = both[1].astype(BF16)
    d = dall[...]
    mid_g = nt(d, b2[:, HQ:1280]).astype(BF16)
    mid_t = mid[...].astype(F32).T.astype(BF16)
    out_o[:, 0:256] = (2.0 * nn(mid_t[16:32], dall[:, 0:256])).astype(BF16)
    out_o[:, 256:512] = (2.0 * nn(mid_t[32:48], dall[:, 256:512])).astype(BF16)
    in_grads = nn(mid_g.astype(F32).T.astype(BF16)[16:48], normed[...])
    keep_and_send(place, keep_o, send_o, slice(0, 16), q_in[...])
    keep_and_send(place, keep_o, send_o, slice(16, 48), in_grads)
    keep_and_send(place, keep_o, send_o, slice(48, 64), orep[...])
    for c in cs:
        c.wait()
    for n in range(3):
        cols = slice(n * 512, (n + 1) * 512)
        part[:, cols] = (qpart[:, cols] + nt(d, w[cols, :]) + nn(mid_g, a1[:, cols])).astype(BF16)


def kv_back_call(place, offs, qpart, q_in, da, db, cos, sin, b2, a1, mid, normed, orep, w):
    return pl.pallas_call(
        kv_back_kernel,
        out_shape=(sds((TOK, D), BF16),) + (sds((64, 768), BF16),) * 2 + (sds((16, 512), BF16),),
        in_specs=[SM, SM] + [VM] * 15 + [HB] * 5,
        out_specs=(VM,) * 4,
        scratch_shapes=[
            pltpu.VMEM((D, 512), BF16),
            pltpu.VMEM((TOK, 512), BF16),
            pltpu.SemaphoreType.DMA((16,)),
        ],
        compiler_params=params(),
        cost_estimate=cost(),
        name="kv_back",
    )(place, offs, qpart, q_in, *da, *db, cos, sin, b2, a1, mid, normed, orep, *w)


def token_grad_kernel(tok, rg, own, other, gain, out):
    x = tok[...].astype(F32)
    inv = lax.rsqrt(jnp.mean(x * x, axis=-1, keepdims=True) + EPS)
    wv = (own[...].astype(F32) + other[...].astype(F32)) * gain[...]
    dot = jnp.mean(wv * x, axis=-1, keepdims=True)
    out[...] = (rg[...] + inv * wv - x * (inv * inv * inv * dot)).astype(BF16)


def token_grad_call(tok, rg, own, other, gain):
    return pl.pallas_call(
        token_grad_kernel,
        grid=(4,),
        out_shape=sds((TOK, D), BF16),
        in_specs=[row_block(D)] * 4 + [all_block(1, D)],
        out_specs=row_block(D),
        compiler_params=params(16),
        cost_estimate=cost(),
        name="token_grad",
    )(tok, rg, own, other, gain)


def pack_first_kernel(q, k, v, out):
    out[:, 0:768] = q[...]
    out[:, 768:1024] = k[...]
    out[:, 1024:1280] = v[...]


def pack_first_call(q, k, v):
    return pl.pallas_call(
        pack_first_kernel,
        out_shape=sds((96, 1280), BF16),
        in_specs=[VM] * 3,
        out_specs=VM,
        compiler_params=params(),
        cost_estimate=cost(),
        name="pack_qkv",
    )(q, k, v)


def pack_rest_kernel(o, g, u, d, yx, xy):
    yx[:, 0:HQ] = o[...]
    for i, w in enumerate((g, u, d)):
        yx[:, HQ + i * FA : HQ + (i + 1) * FA] = w[:, 0:FA]
        xy[:, i * FB : (i + 1) * FB] = w[:, FA:FH]


def pack_rest_call(o, g, u, d):
    return pl.pallas_call(
        pack_rest_kernel,
        out_shape=(
            sds((96, HQ + 3 * FA), BF16),
            sds((96, 3 * FB), BF16),
        ),
        in_specs=[VM] * 4,
        out_specs=(VM,) * 2,
        compiler_params=params(),
        cost_estimate=cost(),
        name="pack_rest",
    )(o, g, u, d)


def line_call(parts, head):
    n = parts[0].shape[1] - head

    def kernel(*refs):
        ins, outs = refs[:4], refs[4:]
        for i in range(4):
            if head:
                outs[0][i] = ins[i][:, 0:head]
            outs[-1][i] = ins[i][:, head:]

    shapes = (sds((4, 96, head), BF16),) * bool(head) + (sds((4, 96, n), BF16),)
    return pl.pallas_call(
        kernel,
        out_shape=shapes,
        in_specs=[VM] * 4,
        out_specs=(VM,) * len(shapes),
        compiler_params=params(),
        cost_estimate=cost(),
        name="line",
    )(*parts)


def own_half_kernel(idx, q, k, v, o, g, u, d, out):
    at = 0
    for ref in (q, k, v, o, g, u, d):
        n = ref.shape[2]
        out[:, at : at + n] = ref[0]
        at += n


def own_half_call(index, arrays):
    return pl.pallas_call(
        own_half_kernel,
        out_shape=sds((16, 7808), BF16),
        grid_spec=pltpu.PrefetchScalarGridSpec(
            num_scalar_prefetch=1,
            grid=(1,),
            in_specs=[
                pl.BlockSpec((1, 16, a.shape[2]), lambda i, idx: (idx[0], 0, 0)) for a in arrays
            ],
            out_specs=pl.BlockSpec((16, 7808), lambda i, idx: (0, 0)),
        ),
        compiler_params=params(),
        cost_estimate=cost(),
        name="pick_halves",
    )(index, *arrays)


def factors_kernel(
    idx, halves, aq, ak, av, ag, au, oo, do, a_qkv, b_qkv, a_gu, bg, bu, di, oi, oo2, do2
):
    for ref in (a_qkv, b_qkv, a_gu, bg, bu, di, oi, oo2, do2):
        ref[...] = jnp.zeros_like(ref)
    for i, ref in enumerate((aq, ak, av)):
        a_qkv[i * 16 : (i + 1) * 16] = ref[0]
    for i, ref in enumerate((ag, au)):
        a_gu[i * 16 : (i + 1) * 16] = ref[0]
    oo2[0:16] = 2 * oo[0]
    do2[0:16] = 2 * do[0]
    b_qkv[0:16, 0:768] = 2 * halves[:, 0:768]
    b_qkv[16:32, 768:1024] = 2 * halves[:, 768:1024]
    b_qkv[32:48, 1024:1280] = 2 * halves[:, 1024:1280]
    oi[0:16] = halves[:, 1280:2048]
    bg[0:16] = 2 * halves[:, 2048:3968]
    bu[16:32] = 2 * halves[:, 3968:5888]
    di[0:16] = halves[:, 5888:7808]


def factors_call(index, halves, arrays):
    widths = (D, 1280, D, FH, FH, FH, HQ, D, D)
    return pl.pallas_call(
        factors_kernel,
        out_shape=tuple(sds((128, w), BF16) for w in widths),
        grid_spec=pltpu.PrefetchScalarGridSpec(
            num_scalar_prefetch=1,
            grid=(1,),
            in_specs=[pl.BlockSpec((16, 7808), lambda i, idx: (0, 0))]
            + [pl.BlockSpec((1, 16, D), lambda i, idx: (idx[0], 0, 0))] * 7,
            out_specs=tuple(pl.BlockSpec((128, w), lambda i, idx: (0, 0)) for w in widths),
        ),
        compiler_params=params(),
        cost_estimate=cost(),
        name="factors",
    )(index, halves, *arrays)


def quarters_kernel(m, place, rep, got, *refs):
    parts, outs, buf = refs[:-5], refs[-5:-1], refs[-1]
    z = place[1]
    n_rep = rep.shape[0] // 16
    kept = (rep[...].astype(F32) + got[...].astype(F32)).astype(BF16)
    for i in range(n_rep):
        buf[:, i * 768 : (i + 1) * 768] = kept[i * 16 : (i + 1) * 16]
    at = n_rep * 768
    for p in parts:
        buf[:, at : at + p.shape[1]] = p[...]
        at += p.shape[1]
    if at < 4 * m:
        buf[:, at : 4 * m] = jnp.zeros((16, 4 * m - at), BF16)
    for k, out in enumerate(outs):
        quarter = lax.rem(z + k, 4)
        out[...] = buf[:, pl.ds(pl.multiple_of(quarter * m, 128), m)]


def quarters_call(m, place, rep, got, parts):
    def kernel(*refs):
        quarters_kernel(m, *refs)

    return pl.pallas_call(
        kernel,
        out_shape=(sds((16, m), BF16),) * 4,
        in_specs=[SM] + [VM] * (2 + len(parts)),
        out_specs=(VM,) * 4,
        scratch_shapes=[pltpu.VMEM((16, 4 * m), BF16)],
        compiler_params=params(6 if m == LATE else 58),
        cost_estimate=cost(),
        name="quarters",
    )(place, rep, got, *parts)


def pack_early_kernel(keep, got, g, u, d, out):
    kept = (keep[...].astype(F32) + got[...].astype(F32)).astype(BF16)
    for i in range(3):
        out[:, i * 768 : (i + 1) * 768] = kept[i * 16 : (i + 1) * 16]
    for i, ref in enumerate((g, u, d)):
        out[:, 2304 + i * FH : 2304 + (i + 1) * FH] = ref[...]
    out[:, 8064:8192] = jnp.zeros((16, 128), BF16)


def pack_early_call(keep, got, g, u, d):
    return pl.pallas_call(
        pack_early_kernel,
        out_shape=sds((16, 4 * EARLY), BF16),
        in_specs=[VM] * 5,
        out_specs=VM,
        compiler_params=params(),
        cost_estimate=cost(),
        name="pack_early",
    )(keep, got, g, u, d)


def quarter_kernel(place, total, out):
    out[:, 0:EARLY] = total[...]
    out[:, EARLY : EARLY + 128] = (
        jnp.full((16, 128), place[2], jnp.int32).astype(F32).astype(BF16)
    )


def quarter_call(place, total):
    return pl.pallas_call(
        quarter_kernel,
        out_shape=sds((16, EARLY + 128), BF16),
        in_specs=[SM, VM],
        out_specs=VM,
        compiler_params=params(),
        cost_estimate=cost(),
        name="quarter",
    )(place, total)


def sum_kernel(place, a, b, c, d, out):
    m = a.shape[1]
    total = a[...].astype(F32) + b[...].astype(F32) + c[...].astype(F32) + d[...].astype(F32)
    out[:, 0:m] = total.astype(BF16)
    out[:, m : m + 128] = jnp.full((16, 128), place[2], jnp.int32).astype(F32).astype(BF16)


def sum_call(place, parts):
    m = parts[0].shape[1]
    return pl.pallas_call(
        sum_kernel,
        out_shape=sds((16, m + 128), BF16),
        in_specs=[SM] + [VM] * 4,
        out_specs=VM,
        compiler_params=params(6),
        cost_estimate=cost(),
        name="sum_tokens",
    )(place, *parts)


def by_adapter_kernel(*refs):
    ins, out, total = refs[:-2], refs[-2], refs[-1]
    m = out.shape[2]
    total[...] = jnp.zeros_like(total)
    for r in ins:
        for k in range(r.shape[0]):
            adapter = jnp.max(r[k, :, m : m + 128].astype(F32)).astype(jnp.int32)
            total[adapter] += r[k, :, 0:m].astype(F32)
    out[...] = total[...].astype(BF16)


def by_adapter_call(parts, m):
    return pl.pallas_call(
        by_adapter_kernel,
        out_shape=sds((8, 16, m), BF16),
        in_specs=[VM] * len(parts),
        out_specs=VM,
        scratch_shapes=[pltpu.VMEM((8, 16, m), F32)],
        compiler_params=params(14),
        cost_estimate=cost(),
        name="by_adapter",
    )(*parts)


def spread(buf, outs, jobs, widths):
    at = 0
    for out, n in zip(outs, widths, strict=True):
        for c in range(2):
            out[:, :, c * n : (c + 1) * n] = buf[c, :, :, at : at + n].astype(F32)
        at += n


def unpack_early_kernel(src, *refs):
    outs, buf, sem = refs[:-2], refs[-2], refs[-1]
    copies = []
    for z in range(4):
        for c in range(2):
            copies.append(
                pltpu.make_async_copy(
                    src.at[2 * z + c], buf.at[c, :, :, pl.ds(z * EARLY, EARLY)], sem.at[2 * z + c]
                )
            )
    for c in copies:
        c.start()
    for c in copies:
        c.wait()
    spread(buf, outs, None, (768, 768, 768, FH, FH, FH))


def unpack_early_call(src):
    widths = (D, D, D, 2 * FH, 2 * FH, 2 * FH)
    return pl.pallas_call(
        unpack_early_kernel,
        out_shape=tuple(sds((8, 16, w), F32) for w in widths),
        in_specs=[HB],
        out_specs=(VM,) * 6,
        scratch_shapes=[pltpu.VMEM((2, 8, 16, 4 * EARLY), BF16), pltpu.SemaphoreType.DMA((8,))],
        compiler_params=params(),
        cost_estimate=cost(),
        name="unpack_early",
    )(src)


def unpack_late_kernel(place, *refs):
    srcs, outs, buf, sem = refs[:8], refs[8:-2], refs[-2], refs[-1]
    core, z = place[0], place[1]
    copies = []
    for i, src in enumerate(srcs):
        c = core if i < 4 else 1 - core
        at = lax.rem(z + REL[i % 4] + 4, 4) * LATE
        copies.append(
            pltpu.make_async_copy(
                src, buf.at[c, :, :, pl.ds(pl.multiple_of(at, 128), LATE)], sem.at[i]
            )
        )
    for c in copies:
        c.start()
    for c in copies:
        c.wait()
    spread(buf, outs, None, (768, 768, 768, 768, 768, 256, 256, 768))


def unpack_late_call(place, srcs):
    widths = (D, D, D, D, D, 512, 512, D)
    return pl.pallas_call(
        unpack_late_kernel,
        out_shape=tuple(sds((8, 16, w), F32) for w in widths),
        in_specs=[SM] + [HB] * 8,
        out_specs=(VM,) * 8,
        scratch_shapes=[pltpu.VMEM((2, 8, 16, 4 * LATE), BF16), pltpu.SemaphoreType.DMA((8,))],
        compiler_params=params(24),
        cost_estimate=cost(),
        name="unpack_late",
    )(place, *srcs)


YLIN = (0, 2, 1, 3)


def go_x(v, step):
    return lax.ppermute(v, "x", [(i, (i + step) % 4) for i in range(4)])


def go_y(v, step):
    return lax.ppermute(
        v, ("tensor", "yh"), [(YLIN[i], YLIN[(i + step) % 4]) for i in range(4)]
    )


def go_z(v, step):
    return lax.ppermute(v, "seq", [(i, (i + step) % 4) for i in range(4)])


def go_core(v):
    return lax.ppermute(v, "core", [(0, 1), (1, 0)])


def to_role(v):
    return lax.ppermute(v, ("tensor", "core"), [(1, 2), (2, 1)])


REL = (0, -1, 1, 2)


def near_line(shard, near):
    return (shard, near(shard, 1), near(shard, -1), near(shard, 2))


def ring_start(line, far):
    return (line, far(line, 1), far(line, -1))


def ring_halves(below, above):
    return below[:2], above[2:]


class Order:
    def __init__(self):
        self.last = ()

    def gate(self, v):
        return lax.optimization_barrier((v, self.last))[0]

    def done(self, v):
        v = self.gate(v)
        self.last = jax.tree.leaves(v)
        return v

    def run(self, step, *args):
        out = step(*self.gate(args))
        self.last = jax.tree.leaves(out)
        return out


def offsets(x, y, path):
    near = np.tile(np.array(REL, np.int32), 4)
    far = np.repeat(np.array(REL, np.int32), 4)
    if path == "yx":
        return ((x + far + 4) % 4) * 4 + (y + near + 4) % 4
    if path == "xy":
        return np.tile(np.arange(4, dtype=np.int32), 4) * 4 + (y + far + 4) % 4
    return np.repeat(np.arange(4, dtype=np.int32), 4) * 4 + (y + near + 4) % 4


def halo_back(grads):
    two, one, own = grads
    one = lax.ppermute(one, "seq", [(1, 0), (2, 1), (3, 2)])
    return (own, one, lax.ppermute(two, "seq", [(2, 0), (3, 1)]))


def shards(
    tokens,
    output_gradient,
    document_length_table,
    sequence_adapter_index,
    sequence_window_length,
    attention_norm_gain,
    feedforward_norm_gain,
    query_projection_weight,
    key_projection_weight,
    value_projection_weight,
    output_projection_weight,
    gate_projection_weight,
    up_projection_weight,
    down_projection_weight,
    query_adapter_first,
    query_adapter_second,
    key_adapter_first,
    key_adapter_second,
    value_adapter_first,
    value_adapter_second,
    output_adapter_first,
    output_adapter_second,
    gate_adapter_first,
    gate_adapter_second,
    up_adapter_first,
    up_adapter_second,
    down_adapter_first,
    down_adapter_second,
):
    z = lax.axis_index("seq")
    yl = lax.axis_index("tensor")
    x = lax.axis_index("x")
    y = lax.axis_index("yh") * 2 + yl
    core = lax.axis_index("core")
    same = core == yl

    o = Order()
    t = lambda v: v.swapaxes(1, 2)
    mine = lambda own, got: jnp.where(same, own, got)
    offs_yx, offs_xy, offs_o = (offsets(x, y, p) for p in ("yx", "xy", "o"))
    gain1 = attention_norm_gain[None, :]
    gain2 = feedforward_norm_gain[None, :]

    own_qkv = o.run(
        pack_first_call, query_projection_weight, key_projection_weight, value_projection_weight
    )
    got_qkv = to_role(own_qkv)
    own_yx, own_b = o.run(
        pack_rest_call,
        output_projection_weight,
        gate_projection_weight,
        up_projection_weight,
        down_projection_weight,
    )
    meta = jnp.concatenate(
        [document_length_table[0], sequence_adapter_index, sequence_window_length]
    )
    meta_other = go_core(meta)
    tok_other = go_core(tokens[0])
    near_qkv = near_line(o.run(mine, own_qkv, o.done(got_qkv)), go_y)
    own_halves = o.run(
        own_half_call,
        sequence_adapter_index,
        (
            query_adapter_second,
            key_adapter_second,
            value_adapter_second,
            output_adapter_first,
            gate_adapter_second,
            up_adapter_second,
            down_adapter_first,
        ),
    )
    line_qkv = o.run(lambda *v: line_call(v, 0)[0], *o.done(near_qkv))
    below_qkv, above_qkv = go_x(line_qkv, 1), go_x(line_qkv, -1)

    def tables(own, other):
        meta = mine(own, other)
        lengths, index, window = meta[:4], meta[4:5], meta[5]
        place = jnp.concatenate(
            [jnp.stack([core, z]), index, same[None]], dtype=jnp.int32
        )
        ends = jnp.cumsum(lengths, dtype=jnp.int32)
        begins = ends - lengths
        row = z * TOK + jnp.arange(TOK, dtype=jnp.int32)
        begin = jnp.max(jnp.where(row[:, None] >= begins[None, :], begins[None, :], 0), axis=1)
        low_key = (jnp.maximum(begin, row - window + 1) - (z * TOK - HALO))[None, :]
        lane = jnp.arange(128, dtype=jnp.int32) % HDIM
        frequency = ROPE_BASE ** (-((lane % 32).astype(F32) * (2.0 / HDIM)))
        angles = (row - begin).astype(F32)[:, None] * frequency[None, :]
        cos = jnp.cos(angles)
        sin = jnp.sin(angles) * jnp.where(lane < 32, -1.0, 1.0)[None, :]
        return index, place, low_key, cos, sin

    index, place, low_key, cos, sin = o.run(tables, meta, o.done(meta_other))
    got_halves, got_yx, got_b = (to_role(o.gate(v)) for v in (own_halves, own_yx, own_b))
    tok = o.run(mine, tokens[0], o.done(tok_other))
    halves = o.run(mine, own_halves, o.done(got_halves))
    a_qkv, b_qkv, a_gu, bg2, bu2, di_p, oi_p, oo2, do2 = o.run(
        factors_call,
        index,
        halves,
        (
            t(query_adapter_first),
            t(key_adapter_first),
            t(value_adapter_first),
            t(gate_adapter_first),
            t(up_adapter_first),
            output_adapter_second,
            down_adapter_second,
        ),
    )
    near_yx = near_line(o.run(mine, own_yx, o.done(got_yx)), go_y)
    own_b = o.run(mine, own_b, o.done(got_b))
    low, high = o.run(ring_halves, *o.done((below_qkv, above_qkv)))
    far_qkv = (go_x(low, 1), go_x(high, -1))
    line_b = lax.all_gather(o.gate(own_b), "x", axis=0)
    full_qkv = (line_qkv, below_qkv, above_qkv) + o.done(far_qkv)

    normed, q, kv0, mid_qkv = o.run(
        qkv_call, offs_yx, tok, gain1, a_qkv, b_qkv, cos, sin, full_qkv
    )
    kv1 = lax.ppermute(kv0, "seq", [(0, 1), (1, 2), (2, 3)])
    kv2 = lax.ppermute(kv0, "seq", [(0, 2), (1, 3)])
    line_o, line_a = o.run(lambda *v: line_call(v, HQ), *o.done(near_yx))
    full_o = lax.all_gather(line_o, "x", axis=0, tiled=True)
    line_b = o.done(line_b)
    below_b, above_b = go_y(line_b, 1), go_y(line_b, -1)
    kv1, kv2 = o.done((kv1, kv2))
    line_a = o.gate(line_a)
    below_a, above_a = go_x(line_a, 1), go_x(line_a, -1)
    og_other = go_core(o.gate(output_gradient[0]))
    att, lse = o.run(attend_call, q, low_key, kv2, kv1, kv0)
    og_other = o.done(og_other)
    low, high = o.run(ring_halves, *o.done((below_b, above_b)))
    far_b = (go_y(low, 1), go_y(high, -1))
    full_o = o.done(full_o)
    attn_part, mid_att = o.run(out_proj_call, offs_o, att, oi_p, oo2, full_o)
    attn_other = go_core(attn_part)
    low, high = o.run(ring_halves, *o.done((below_a, above_a)))
    far_a = (go_x(low, 1), go_x(high, -1))
    resid, nf, mid_gu = o.run(ffn_in_call, tok, attn_part, o.done(attn_other), gain2, a_gu)
    full_b = (line_b, below_b, above_b) + o.done(far_b)
    og, fg, mid_dg = o.run(cot_call, place, output_gradient[0], og_other, do2)
    full_a = (line_a, below_a, above_a) + o.done(far_a)
    ffn_part, nfg_part, keep_e, send_e, g_out, u_out, d_in = o.run(
        ffn_call,
        place, offs_yx, offs_xy, nf, fg, mid_gu, mid_dg, bg2, bu2, di_p, a_gu, do2, full_a, full_b,
    )

    nfg_other = go_core(nfg_part)
    got_e = go_core(send_e)
    packed = o.run(pack_early_call, keep_e, o.done(got_e), g_out, u_out, d_in)
    summed = lax.psum_scatter(packed, "seq", scatter_dimension=1, tiled=True)
    head = np.arange(16)
    head = np.where(head % 8 < 6, 6 * (head // 8) + head % 8, -1)
    hsel = jnp.asarray((np.arange(HQ) // HDIM)[None, :] == head[:, None], BF16)
    rg, do, delta, rep_o, o_in = o.run(
        out_back_call,
        offs_o, og, resid, nfg_part, o.done(nfg_other), gain2, oi_p, oo2, mid_att, att, hsel, full_o,
    )
    stats = (lse, delta, low_key, kv2, kv1, kv0)
    dqa, *da = o.run(lambda *v: attend_back_call(0, *v), q, do, *stats)
    near = near_line(o.run(quarter_call, place, o.done(summed)), go_y)
    ra = halo_back(da)
    dqb, *db = o.run(lambda *v: attend_back_call(1, *v), q, do, *stats)
    ra = o.done(ra)
    plane = lax.all_gather(o.run(lambda *v: jnp.stack(v), *o.done(near)), "x", axis=0, tiled=True)
    rb = halo_back(db)
    ffn_other = go_core(o.gate(ffn_part))
    qpart, q_in, q_out = o.run(
        q_back_call, offs_yx, dqa, dqb, cos, sin, b_qkv, a_qkv, mid_qkv, normed, full_qkv
    )
    rb = o.done(rb)
    na_part, keep_l, send_l, kv_out = o.run(
        kv_back_call,
        place, offs_yx, qpart, q_in, ra, rb, cos, sin, b_qkv, a_qkv, mid_qkv, normed, rep_o, full_qkv,
    )
    na_other = go_core(na_part)
    got_l = go_core(send_l)
    ffn_other = o.done(ffn_other)

    out = o.run(
        lambda r, a, b: (r + RS * (a.astype(F32) + b.astype(F32))).astype(BF16),
        resid, ffn_part, ffn_other,
    )
    out_other = to_role(out)
    quarters = o.run(
        lambda *v: quarters_call(LATE, place, v[0], v[1], v[2:]),
        keep_l, o.done(got_l), q_out, kv_out, o_in,
    )
    sent = [go_z(quarters[k], k) for k in (1, 2, 3)]
    dense = o.run(lambda v: by_adapter_call([v], EARLY), o.done(plane))
    early = lax.all_gather(dense, ("seq", "core"), axis=0)
    near = near_line(o.run(sum_call, place, [quarters[0]] + o.done(sent)), go_y)
    na_other = o.done(na_other)
    line = o.run(lambda *v: jnp.stack(v), *o.done(near))
    lines = [go_x(line, 1), go_x(line, -1), go_x(line, 2)]
    token_grad = o.run(token_grad_call, tok, rg, na_part, na_other, gain1)
    tg_other = to_role(token_grad)
    dense = o.run(lambda *v: by_adapter_call(v, LATE), line, *o.done(lines))
    out_other = o.done(out_other)
    zs = [go_z(dense, 1), go_z(dense, -1), go_z(dense, 2)]
    g_in, u_in, d_out, g_out, u_out, d_in = o.run(unpack_early_call, o.done(early))
    output = o.run(mine, out, out_other)
    token_grad = o.run(mine, token_grad, o.done(tg_other))
    zs = o.done(zs)
    cores = [go_core(v) for v in [dense] + zs]
    q_in, k_in, v_in, o_out, q_out, k_out, v_out, o_in = o.run(
        unpack_late_call, place, [dense] + zs + o.done(cores)
    )
    return (
        output[None],
        token_grad[None],
        t(q_in),
        q_out,
        t(k_in),
        k_out,
        t(v_in),
        v_out,
        o_in,
        o_out,
        t(g_in),
        g_out,
        t(u_in),
        u_out,
        d_in,
        d_out,
    )


def solution(mesh):
    fine = Mesh(mesh.devices.reshape(4, 2, 4, 2, 2), ("seq", "tensor", "x", "yh", "core"))
    fsdp = ("x", "yh", "core")
    weight = P(fsdp, "tensor")
    half = P(None, None, "tensor")
    return jax.shard_map(
        shards,
        mesh=fine,
        in_specs=(
            P(fsdp, "seq", None),
            P(fsdp, "seq", None),
            P(fsdp, None),
            P(fsdp),
            P(fsdp),
            P(),
            P(),
        )
        + (weight,) * 7
        + (P(), half, P(), half, P(), half, half, P(), P(), half, P(), half, half, P()),
        out_specs=(P(fsdp, "seq", None), P(fsdp, "seq", None)) + (P(),) * 14,
        check_vma=False,
    )
```
